32 devices in a mesh: dp: 8 (over y, x, core), mp: 4 (over z).
Axes of the slice: x: 2, y: 2, z: 4, core: 2. Of those that a mesh axis runs over, the one named last changes fastest.
Arguments:
- pixels: bfloat16 [32, 196, 768], P('dp'), may hold values from -6 to 6
- visible: int32 [32, 196], P('dp'), may hold values from 0 to 1, as said below
- block_master: float32 [4, 1867776], P('mp', 'dp')
- block_first: float32 [4, 1867776], P('mp', 'dp')
- block_second: float32 [4, 1867776], P('mp', 'dp')
- shared_master: float32 [4128768], P(('dp', 'mp'))
- shared_first: float32 [4128768], P(('dp', 'mp'))
- shared_second: float32 [4128768], P(('dp', 'mp'))
- gains_master: float32 [4352], P(('dp', 'mp'))
- gains_first: float32 [4352], P(('dp', 'mp'))
- gains_second: float32 [4352], P(('dp', 'mp'))
Outputs:
- grad_norm: float32 [], replicated
- loss_sum: float32 [], replicated
- masked_count: float32 [], replicated
- block_first_new: float32 [4, 1867776], P('mp', 'dp')
- block_second_new: float32 [4, 1867776], P('mp', 'dp')
- block_new: float32 [4, 1867776], P('mp', 'dp')
- block_half: bfloat16 [4, 1867776], P('mp', 'dp')
- shared_first_new: float32 [4128768], P(('dp', 'mp'))
- shared_second_new: float32 [4128768], P(('dp', 'mp'))
- shared_new: float32 [4128768], P(('dp', 'mp'))
- shared_half: bfloat16 [4128768], P(('dp', 'mp'))
- gains_first_new: float32 [4352], P(('dp', 'mp'))
- gains_second_new: float32 [4352], P(('dp', 'mp'))
- gains_new: float32 [4352], P(('dp', 'mp'))
- gains_half: bfloat16 [4352], P(('dp', 'mp'))
The draws below stay inside these ranges and needn't reach their ends.
Inputs may be any that keep to these rules, and one draw needn't show every extreme that they name: In each image the visible patches form one run in raster order that may wrap from the last patch to the first, of 40 to 60 patches; some image has exactly 60 and some exactly 40.
All inputs are finite; a program needn't handle non-finite values.
Results may differ from the reference program's by a relative error of at most 0.0035.
Values may be sent and summed in bfloat16 or wider, within the bound.
No kernel may reach another device: no remote copies, remote signals or barrier semaphores. Data moves between devices by JAX's collectives and lax.ppermute only.
A program may use at most 192 MiB of HBM per device.

```python
import math
import jax
import jax.numpy as jnp
from jax import lax

D = 768
HEADS = 12
MLP = 3072
DD = 512
DHEADS = 16
DMLP = 2048
PIX = 768
PATCHES = 196
VIS = 64
MOST_VIS = 60
LEAST_VIS = 40
STEP = 10
IMG_GRP = 4
IMAGES = 32
SPLIT = 1867776
SHARED = 4128768
SMALL = 4352
PARAMS = 11604224
N_DP = 8
N_MP = 4


def section_scales(sections):
    return jnp.concatenate([jnp.full((length,), scaling, jnp.float32) for length, scaling in sections])


def block_sections():
    model_cols = D // N_MP
    mlp_cols = MLP // N_MP
    embed_cols = DD // N_MP
    return [(D * 3 * model_cols, D ** (-0.5)), (model_cols * D, 3.0 * D ** (-0.5)), (D * mlp_cols, D ** (-0.5)), (mlp_cols * D, MLP ** (-0.5)), (D * embed_cols, D ** (-0.5))]


def shared_sections():
    return [(PIX * D, PIX ** (-0.5)), (DD * 3 * DD, DD ** (-0.5)), (DD * DD, 4.0 * DD ** (-0.5)), (DD * DMLP, DD ** (-0.5)), (DMLP * DD, DMLP ** (-0.5)), (DD * PIX, DD ** (-0.5))]


def gradient_size():
    return 0.0002 * PARAMS ** (-0.5)


def first_moment(key, shape, size_scale):
    return jax.random.normal(key, shape, jnp.float32) * (size_scale / 9.0)


def second_moment(key, shape, size_scale):
    spread = jax.random.uniform(key, shape, jnp.float32, 0.0, math.log(4.0))
    return jnp.exp(spread) * (size_scale * size_scale / 19.0)


def draw_visible(key, part):
    key = jax.random.fold_in(key, 1)
    count_key, order_key, start_key = jax.random.split(key, 3)
    counts = jax.random.randint(count_key, (IMAGES,), LEAST_VIS, MOST_VIS + 1)
    order = jax.random.permutation(order_key, IMAGES)
    counts = counts.at[order[0]].set(MOST_VIS).at[order[1]].set(LEAST_VIS)
    starts = jax.random.randint(start_key, (IMAGES,), 0, PATCHES)
    places = jnp.arange(PATCHES)[None, :]
    return ((places - starts[:, None]) % PATCHES < counts[:, None]).astype(jnp.int32)


def draw_block_master(key, part):
    key = jax.random.fold_in(key, 11)
    scales = section_scales(block_sections())
    return jax.random.normal(key, (N_MP, SPLIT), jnp.float32) * scales[None, :]


def draw_block_first(key, part):
    key = jax.random.fold_in(key, 12)
    return first_moment(key, (N_MP, SPLIT), gradient_size())


def draw_block_second(key, part):
    key = jax.random.fold_in(key, 13)
    return second_moment(key, (N_MP, SPLIT), gradient_size())


def draw_shared_master(key, part):
    key = jax.random.fold_in(key, 21)
    scales = section_scales(shared_sections())
    return jax.random.normal(key, (SHARED,), jnp.float32) * scales


def draw_shared_first(key, part):
    key = jax.random.fold_in(key, 22)
    return first_moment(key, (SHARED,), gradient_size())


def draw_shared_second(key, part):
    key = jax.random.fold_in(key, 23)
    return second_moment(key, (SHARED,), gradient_size())


def draw_gains_master(key, part):
    key = jax.random.fold_in(key, 31)
    noise = jax.random.normal(key, (SMALL,), jnp.float32)
    gain_count = 3 * D + 3 * DD
    places = jnp.arange(SMALL)
    gains = 1.0 + 0.1 * jnp.clip(noise, -5.0, 5.0)
    token = noise
    return jnp.where(places < gain_count, gains, jnp.where(places < gain_count + DD, token, 0.02 * noise))


def draw_gains_first(key, part):
    key = jax.random.fold_in(key, 32)
    return first_moment(key, (SMALL,), 5.0 * gradient_size())


def draw_gains_second(key, part):
    key = jax.random.fold_in(key, 33)
    return second_moment(key, (SMALL,), 5.0 * gradient_size())


def steps_of(own_key, dims, shards, low, high):
    def one(dim, shards_of):
        heights = jax.random.uniform(jax.random.fold_in(jax.random.fold_in(own_key, 6), dim), (shards_of,), jnp.float32, low / len(shards), high / len(shards))
        return jnp.repeat(jnp.exp(heights), dims[dim] // shards_of).reshape((-1,) + (1,) * (len(dims) - dim - 1))

    factor_of = one(*shards[0])
    for cut in shards[1:]:
        factor_of = factor_of * one(*cut)
    return factor_of


def bell_draw(own_key, shape, scale, bound, cuts=(), kind=jnp.bfloat16):
    array = jax.random.normal(own_key, shape, jnp.float32) * scale
    if len(cuts) > 0:
        array = steps_of(own_key, shape, cuts, -0.22, 0.18) * array
    return jnp.clip(array, min=-bound, max=bound).astype(kind)


def setup_inputs(seed: int = 0) -> dict:
    arg_keys = jax.random.split(jax.random.key(seed), 12)
    return {
        "pixels": bell_draw(arg_keys[0], (IMAGES, PATCHES, PIX), 1.0, 6.0, ((0, 8),)),
        "visible": draw_visible(jax.random.fold_in(arg_keys[11], 71), 0),
        "block_master": draw_block_master(jax.random.fold_in(arg_keys[11], 71), 0),
        "block_first": draw_block_first(jax.random.fold_in(arg_keys[11], 71), 0),
        "block_second": draw_block_second(jax.random.fold_in(arg_keys[11], 71), 0),
        "shared_master": draw_shared_master(jax.random.fold_in(arg_keys[11], 71), 0),
        "shared_first": draw_shared_first(jax.random.fold_in(arg_keys[11], 71), 0),
        "shared_second": draw_shared_second(jax.random.fold_in(arg_keys[11], 71), 0),
        "gains_master": draw_gains_master(jax.random.fold_in(arg_keys[11], 71), 0),
        "gains_first": draw_gains_first(jax.random.fold_in(arg_keys[11], 71), 0),
        "gains_second": draw_gains_second(jax.random.fold_in(arg_keys[11], 71), 0),
    }


@jax.custom_vjp
def low(v):
    return lax.optimization_barrier(v.astype(jnp.bfloat16)).astype(jnp.float32)

@jax.custom_vjp
def low_back(v):
    return v

def low_keep(v):
    return (low(v), None)

def low_pass(kept, grad):
    return (grad,)

def back_keep(v):
    return (v, None)

def back_low(kept, grad):
    return (low(grad),)
low.defvjp(low_keep, low_pass)
low_back.defvjp(back_keep, back_low)
highest = lax.Precision.HIGHEST
clip_norm = 0.0002
beta_one = 0.9
beta_two = 0.95
adam_eps = 1e-10
rate_matrix = 0.03
rate_gains = 0.7
weight_decay = 0.1

def both_round(values):
    return low(low_back(values))

def matmul(left_side, right_side):
    return jnp.dot(left_side, right_side, precision=highest)

def position_table(places, row_width):
    column = jnp.arange(row_width)
    step_rate = jnp.exp(-(column // 2 * 2).astype(jnp.float32) * (math.log(10000.0) / row_width))
    angle = places.astype(jnp.float32)[..., None] * step_rate
    return jnp.where(column % 2 == 0, jnp.sin(angle), jnp.cos(angle))

def layer_norm(residual, gain_vec):
    center = residual - lax.optimization_barrier(jnp.mean(residual, -1, keepdims=True))
    return center * lax.rsqrt(lax.optimization_barrier(jnp.mean(center * center, -1, keepdims=True)) + 1e-06) * gain_vec

def visible_slots(visible):
    slot_rank = jnp.cumsum(visible, 1) - 1
    select = ((visible[:, None, :] == 1) & (slot_rank[:, None, :] == jnp.arange(VIS)[None, :, None])).astype(jnp.int32)
    slot_patch = lax.optimization_barrier(jnp.sum(select * jnp.arange(visible.shape[1])[None, None, :], 2)).astype(jnp.int32)
    key_valid = jnp.arange(VIS)[None, :] < lax.optimization_barrier(jnp.sum(visible, 1))[:, None]
    return (select, slot_patch, key_valid)

def attention(packed, key_valid, head_count, scaling):
    batch_size, length, row_width = packed.shape
    unpacked = packed.reshape(batch_size, length, 3, head_count, row_width // (3 * head_count))
    scores = jnp.einsum('blhd,bmhd->bhlm', unpacked[:, :, 0], unpacked[:, :, 1], precision=highest) * scaling
    scores = low_back(scores)
    scores = jnp.where(key_valid[:, None, None, :], scores, -1e+30)
    probability = low(jax.nn.softmax(scores, -1))
    mixed_heads = jnp.einsum('bhlm,bmhd->blhd', probability, unpacked[:, :, 2], precision=highest)
    return both_round(mixed_heads.reshape(batch_size, length, -1))

def block(residual, weights, gain_pair, key_valid, head_count, scaling):
    packed_w, out_w, up_w, down_w = weights
    normed = low(layer_norm(residual, gain_pair[0]))
    packed = both_round(matmul(normed, packed_w))
    middle = residual + low_back(matmul(attention(packed, key_valid, head_count, scaling), out_w))
    inner_low = low(layer_norm(middle, gain_pair[1]))
    raised = low_back(matmul(inner_low, up_w))
    activated = low(jax.nn.gelu(raised, approximate=True))
    return middle + low_back(matmul(activated, down_w))

def cut_pieces(flat_vector, shapes):
    pieces = []
    offset = 0
    for shape in shapes:
        length = math.prod(shape)
        pieces.append(flat_vector[offset:offset + length].reshape(shape))
        offset += length
    return pieces

def unpack_block(block_w):
    model_cols = D // N_MP
    mlp_cols = MLP // N_MP
    embed_cols = DD // N_MP
    shapes = [(D, 3 * model_cols), (model_cols, D), (D, mlp_cols), (mlp_cols, D), (D, embed_cols)]
    slices = [cut_pieces(block_w[member], shapes) for member in range(N_MP)]
    packed = jnp.concatenate([piece[0][:, third * model_cols:(third + 1) * model_cols] for third in range(3) for piece in slices], 1)
    out_w = jnp.concatenate([piece[1] for piece in slices], 0)
    up_w = jnp.concatenate([piece[2] for piece in slices], 1)
    down_w = jnp.concatenate([piece[3] for piece in slices], 0)
    latent_w = jnp.concatenate([piece[4] for piece in slices], 1)
    return ((packed, out_w, up_w, down_w), latent_w)

def shared_shapes():
    return [(PIX, D), (DD, 3 * DD), (DD, DD), (DD, DMLP), (DMLP, DD), (DD, PIX)]

def group_loss(pixel_group, visible_group, params):
    enc_weights, latent_w, patch_w, dec_weights, head_w, gain_list = params
    enc_one, enc_two, enc_last, dec_one, dec_two, dec_last, mask_token = gain_list
    select, slot_patch, key_valid = visible_slots(visible_group)
    seen_patches = jnp.take_along_axis(pixel_group, slot_patch[:, :, None], 1)
    residual = low_back(matmul(seen_patches, patch_w)) + position_table(slot_patch, D)
    encoded = block(residual, enc_weights, (enc_one, enc_two), key_valid, HEADS, (D // HEADS) ** (-0.5))
    latent = both_round(matmul(low(layer_norm(encoded, enc_last)), latent_w))
    hidden_mask = (1 - visible_group).astype(jnp.float32)
    placed = jnp.einsum('gsp,gsd->gpd', select.astype(jnp.float32), latent, precision=highest)
    tokens = placed + hidden_mask[:, :, None] * mask_token + position_table(jnp.arange(PATCHES), DD)
    all_valid = jnp.ones(visible_group.shape, bool)
    decoded = block(tokens, dec_weights, (dec_one, dec_two), all_valid, DHEADS, (DD // DHEADS) ** (-0.5))
    predicted = low_back(matmul(low(layer_norm(decoded, dec_last)), head_w))
    center = pixel_group - lax.optimization_barrier(jnp.mean(pixel_group, -1, keepdims=True))
    target = center * lax.rsqrt(lax.optimization_barrier(jnp.mean(center * center, -1, keepdims=True)) + 1e-06)
    errors = predicted - target
    return jnp.sum(hidden_mask * lax.optimization_barrier(jnp.mean(errors * errors, -1)))

def adamw(gradient, first_old, second_old, master, factor, step_rate, decay_rate):
    gradient = gradient * factor
    first_new = beta_one * first_old + (1 - beta_one) * gradient
    second_new = beta_two * second_old + (1 - beta_two) * gradient * gradient
    first_hat = first_new / (1 - beta_one ** STEP)
    second_hat = second_new / (1 - beta_two ** STEP)
    master_new = master - step_rate * (first_hat / (jnp.sqrt(second_hat) + adam_eps) + decay_rate * master)
    return (first_new, second_new, master_new, master_new.astype(jnp.bfloat16))

def reference(pixels, visible, block_master, block_first, block_second, shared_master, shared_first, shared_second, gains_master, gains_first, gains_second):
    block_w = block_master.astype(jnp.bfloat16).astype(jnp.float32)
    shared_w = shared_master.astype(jnp.bfloat16).astype(jnp.float32)
    gain_w = gains_master.astype(jnp.bfloat16).astype(jnp.float32)
    count_total = jnp.sum(1 - visible).astype(jnp.float32)
    pixel_groups = pixels.astype(jnp.float32).reshape(N_DP, IMG_GRP, PATCHES, PIX)
    visible_groups = visible.reshape(N_DP, IMG_GRP, PATCHES)
    step_loss = jax.checkpoint(group_loss)

    def total_loss(block_values, shared_values, gain_values):
        enc_weights, latent_w = unpack_block(block_values)
        shared_list = cut_pieces(shared_values, shared_shapes())
        gain_list = tuple(cut_pieces(gain_values, [(D,), (D,), (D,), (DD,), (DD,), (DD,), (DD,)]))
        params = (enc_weights, latent_w, shared_list[0], tuple(shared_list[1:5]), shared_list[5], gain_list)

        def scan_step(carry, group):
            return (carry + step_loss(group[0], group[1], params), None)
        loss_total, unused = lax.scan(scan_step, jnp.zeros((), jnp.float32), (pixel_groups, visible_groups))
        return (loss_total / count_total, loss_total)
    loss_value, back_fn, loss_total = jax.vjp(total_loss, block_w, shared_w, gain_w, has_aux=True)
    block_grad, shared_grad, gain_grad = back_fn(jnp.ones((), jnp.float32))
    grad_norm = jnp.sqrt(jnp.sum(block_grad * block_grad) + jnp.sum(shared_grad * shared_grad) + jnp.sum(gain_grad * gain_grad))
    factor = jnp.minimum(1.0, clip_norm / (grad_norm + 1e-06))
    block_one, block_two, block_new, block_half = adamw(block_grad, block_first, block_second, block_master, factor, rate_matrix, weight_decay)
    shared_one, shared_two, shared_new, shared_half = adamw(shared_grad, shared_first, shared_second, shared_master, factor, rate_matrix, weight_decay)
    gains_one, gains_two, gains_new, gains_half = adamw(gain_grad, gains_first, gains_second, gains_master, factor, rate_gains, 0.0)
    return (grad_norm, loss_total, count_total, block_one, block_two, block_new, block_half, shared_one, shared_two, shared_new, shared_half, gains_one, gains_two, gains_new, gains_half)
```

```python
from functools import partial
import math

import jax
import jax.numpy as jnp
from jax import lax
from jax.experimental import pallas as pl
from jax.experimental.pallas import tpu as pltpu
from jax.sharding import PartitionSpec as P

D = 768
HEADS = 12
MLP = 3072
DD = 512
DHEADS = 16
DMLP = 2048
PIX = 768
PATCHES = 196
VIS = 64
STEP = 10


low_type = jnp.bfloat16
clip_norm = 0.0002
beta_one = 0.9
beta_two = 0.95
adam_eps = 1e-10
rate_matrix = 0.03
rate_gains = 0.7
weight_decay = 0.1


def forward_dot(left_side, right_side):
    return jnp.dot(left_side, right_side, preferred_element_type=jnp.float32)


def back_dot(left_side, right_side):
    return lax.dot_general(
        left_side,
        right_side,
        (((left_side.ndim - 1,), (1,)), ((), ())),
        preferred_element_type=jnp.float32,
    )


def outer_sum(left_side, right_side):
    left_rows = left_side.reshape(-1, left_side.shape[-1])
    right_rows = right_side.reshape(-1, right_side.shape[-1])
    return lax.dot_general(
        left_rows, right_rows, (((0,), (0,)), ((), ())), preferred_element_type=jnp.float32
    )


def swap(values, axis_name, distance):
    count = lax.axis_size(axis_name)
    return lax.ppermute(values, axis_name, [(place, place ^ distance) for place in range(count)])


def share(values):
    groups = lax.axis_size("mp")
    return jnp.stack([values] + [swap(values, "mp", step) for step in range(1, groups)])


def collect(partial_terms):
    total = partial_terms[0]
    for step in range(1, partial_terms.shape[0]):
        total = total + swap(partial_terms[step].astype(low_type), "mp", step).astype(jnp.float32)
    return total


def pick(values, index, dim):
    return lax.dynamic_index_in_dim(values, index, dim, keepdims=False)


def reorder(values, place):
    return jnp.stack([pick(values, place ^ step, 0) for step in range(values.shape[0])])


def bits_of(count):
    return count.bit_length() - 1


def after(values, token):
    first = token[(0,) * token.ndim].astype(jnp.float32)
    return values + jnp.minimum(jnp.abs(first), 0.0).astype(values.dtype)


def half_cut(values, side, dim):
    return (pick(values, side, dim), pick(values, 1 - side, dim))


def reduce_dp(values):
    width = bits_of(lax.axis_size("dp"))
    place = lax.axis_index("dp")
    rows = values.shape[1]
    shaped = values.reshape((-1, 2) + values.shape[1:])
    kept_whole, sent_whole = half_cut(shaped, place & 1, 1)
    got_whole = swap(sent_whole, "dp", 1)
    higher = tuple(range(3, width))
    halves = []
    first_marks, second_marks = [], []
    for part, order in (((0, rows // 2), (1, 2) + higher), ((rows // 2, rows), (2, 1) + higher)):
        left = list(range(width - 1, 0, -1))
        split = (2,) * (width - 1) + (part[1] - part[0],) + values.shape[2:]
        both = [
            lax.slice_in_dim(piece, part[0], part[1], axis=1).reshape(split)
            for piece in (kept_whole, got_whole)
        ]
        total = None
        for bit in order:
            dim = left.index(bit)
            side = (place >> bit) & 1
            if total is None:
                kept, sent = [
                    one.astype(jnp.float32) + two.astype(jnp.float32)
                    for one, two in zip(half_cut(both[0], side, dim), half_cut(both[1], side, dim))
                ]
            else:
                kept, sent = half_cut(total, side, dim)
            sent = sent.astype(low_type)
            (first_marks if total is None else second_marks).append(sent)
            total = kept + swap(sent, "dp", 1 << bit).astype(jnp.float32)
            left.remove(bit)
        halves.append(total)
    return jnp.concatenate(halves, 0), first_marks, second_marks


def reduce_mp(values):
    member = lax.axis_index("mp")
    total = pick(values, member, 0)
    for step in range(1, values.shape[0]):
        sent = pick(values, member ^ step, 0).astype(low_type)
        total = total + swap(sent, "mp", step).astype(jnp.float32)
    return total


def gather_small(row):
    table = reorder(share(row), lax.axis_index("mp"))[None]
    for bit in range(bits_of(lax.axis_size("dp"))):
        table = jnp.concatenate([table, swap(table, "dp", 1 << bit)], 0)
    return reorder(table, lax.axis_index("dp")).reshape(-1, row.shape[0])


def sum_small(row):
    for bit in range(bits_of(lax.axis_size("dp"))):
        row = row + swap(row, "dp", 1 << bit)
    return jnp.sum(reorder(share(row), lax.axis_index("mp")), 0)


def pair_permute(values, pairs):
    return lax.ppermute(values, ("dp", "mp"), pairs)


def spread_patch(own_rows, tail_count):
    replicas = lax.axis_size("dp")
    groups = lax.axis_size("mp")
    place = lax.axis_index("dp")
    member = lax.axis_index("mp")
    even = (place & 1) == 0
    for bit in range(1, bits_of(replicas)):
        step = 1 << bit
        pairs = [
            (dp * groups + mp, (dp ^ step) * groups + mp)
            for dp in range(step)
            for mp in range(1 if dp & 1 else groups)
        ]
        own_rows = jnp.where(place < step, own_rows, pair_permute(own_rows, pairs))
    rows = [own_rows]
    for step in range(1, groups):
        pairs = [
            (dp * groups + mp, dp * groups + (mp ^ step))
            for dp in range(replicas)
            for mp in range(1 if dp & 1 else groups)
        ]
        rows.append(pair_permute(own_rows, pairs))
    tail = rows[0][:tail_count]
    for step in range(1, groups):
        tail = jnp.where(member == step, rows[step][:tail_count], tail)
    column = jnp.stack(rows)
    column = jnp.where(even, column, lax.ppermute(column, "dp", [(dp, dp + 1) for dp in range(0, replicas, 2)]))
    tail = jnp.where(even, lax.ppermute(tail, "dp", [(dp + 1, dp) for dp in range(0, replicas, 2)]), tail)
    return jnp.concatenate([reorder(column, member).reshape(-1, D), tail], 0), own_rows


def return_patch(gradient, row_count):
    replicas = lax.axis_size("dp")
    groups = lax.axis_size("mp")
    member = lax.axis_index("mp")
    even = (lax.axis_index("dp") & 1) == 0
    rows = lax.dynamic_slice_in_dim(gradient, member * row_count, row_count, 0)
    tail = gradient[groups * row_count :]
    tail = jnp.pad(tail, ((0, row_count - tail.shape[0]), (0, 0)))
    total = jnp.where(even, rows, tail) + swap(jnp.where(even, tail, rows), "dp", 1)
    total_low = total.astype(low_type)
    for dp in range(2, replicas, 2):
        pairs = [(dp * groups + mp, mp) for mp in range(groups)] + [((dp + 1) * groups, groups)]
        total = total + pair_permute(total_low, pairs).astype(jnp.float32)
    return total


def position_table(places, row_width):
    column = jnp.arange(row_width)
    step_rate = jnp.exp(-(column // 2 * 2).astype(jnp.float32) * (math.log(10000.0) / row_width))
    angle = places.astype(jnp.float32)[..., None] * step_rate
    return jnp.where(column % 2 == 0, jnp.sin(angle), jnp.cos(angle))


def visible_slots(visible):
    slot_rank = jnp.cumsum(visible, 1) - 1
    select = (
        (visible[:, None, :] == 1) & (slot_rank[:, None, :] == jnp.arange(VIS)[None, :, None])
    ).astype(jnp.int32)
    slot_patch = jnp.sum(select * jnp.arange(visible.shape[1])[None, None, :], 2)
    key_valid = jnp.arange(VIS)[None, :] < jnp.sum(visible, 1)[:, None]
    return (select, slot_patch, key_valid)


def cut_pieces(flat_vector, shapes):
    pieces = []
    offset = 0
    for shape in shapes:
        length = math.prod(shape)
        pieces.append(flat_vector[offset : offset + length].reshape(shape))
        offset += length
    return pieces


def norm_forward(residual, gain_vec):
    center = residual - jnp.mean(residual, -1, keepdims=True)
    inverse = lax.rsqrt(jnp.mean(center * center, -1, keepdims=True) + 1e-06)
    normal_hat = center * inverse
    return (normal_hat * gain_vec, normal_hat, inverse)


def norm_backward(gradient, normal_hat, inverse, gain_vec):
    hat_grad = gradient * gain_vec
    residual_grad = inverse * (
        hat_grad
        - jnp.mean(hat_grad, -1, keepdims=True)
        - normal_hat * jnp.mean(hat_grad * normal_hat, -1, keepdims=True)
    )
    return (residual_grad, gradient * normal_hat)


def split_heads(packed, head_count):
    batch_size, length, row_width = packed.shape
    unpacked = packed.reshape(batch_size, length, 3, head_count, row_width // (3 * head_count))
    return (unpacked[:, :, 0], unpacked[:, :, 1], unpacked[:, :, 2])


def scores_of(query_part, key_part, key_valid, scaling):
    raw_scores = (
        jnp.einsum("blhd,bmhd->bhlm", query_part, key_part, preferred_element_type=jnp.float32)
        * scaling
    )
    return jnp.where(key_valid[:, None, None, :], raw_scores, -1e30)


def attend_forward(packed, key_valid, head_count, scaling):
    query_part, key_part, value_part = split_heads(packed, head_count)
    scores = scores_of(query_part, key_part, key_valid, scaling)
    row_top = jnp.max(scores, -1, keepdims=True)
    exponent = jnp.exp(scores - row_top)
    row_total = jnp.sum(exponent, -1, keepdims=True)
    probability = (exponent / row_total).astype(low_type)
    mixed_heads = jnp.einsum(
        "bhlm,bmhd->blhd", probability, value_part, preferred_element_type=jnp.float32
    )
    batch_size, length = (key_valid.shape[0], packed.shape[1])
    return (
        mixed_heads.reshape(batch_size, length, -1).astype(low_type),
        row_top + jnp.log(row_total),
    )


def attend_backward(packed, log_total, key_valid, mixed_grad, head_count, scaling):
    query_part, key_part, value_part = split_heads(packed, head_count)
    batch_size, length, row_width = mixed_grad.shape
    out_grad = mixed_grad.reshape(batch_size, length, head_count, -1)
    probability = jnp.exp(scores_of(query_part, key_part, key_valid, scaling) - log_total)
    value_grad = jnp.einsum(
        "bhlm,blhd->bmhd",
        probability.astype(low_type),
        out_grad,
        preferred_element_type=jnp.float32,
    )
    prob_grad = jnp.einsum(
        "blhd,bmhd->bhlm", out_grad, value_part, preferred_element_type=jnp.float32
    )
    score_grad = (
        probability * (prob_grad - jnp.sum(probability * prob_grad, -1, keepdims=True))
    ).astype(low_type)
    query_grad = (
        jnp.einsum("bhlm,bmhd->blhd", score_grad, key_part, preferred_element_type=jnp.float32)
        * scaling
    )
    key_grad = (
        jnp.einsum("bhlm,blhd->bmhd", score_grad, query_part, preferred_element_type=jnp.float32)
        * scaling
    )
    stacked = jnp.stack([query_grad, key_grad, value_grad], 2)
    return stacked.reshape(batch_size, length, -1).astype(low_type)


def cut_rows(rows, shapes):
    pieces = []
    offset = 0
    for shape in shapes:
        length = math.prod(shape) // 128
        pieces.append(rows[offset : offset + length].reshape(shape))
        offset += length
    return pieces


def mlp_backward(
    gradient, grad_low, activated, raised, inner_low, up_w, down_w, total_sum, norm_saved
):
    down_grad = outer_sum(activated, grad_low)
    act_grad = back_dot(grad_low, down_w)
    unused, gelu_back = jax.vjp(partial(jax.nn.gelu, approximate=True), raised)
    raised_grad = gelu_back(act_grad)[0].astype(low_type)
    up_grad = outer_sum(inner_low, raised_grad)
    inner_grad = total_sum(back_dot(raised_grad, up_w))
    normal_hat, inverse, gain_vec = norm_saved
    middle_part, second_terms = norm_backward(inner_grad, normal_hat, inverse, gain_vec)
    return (gradient + middle_part, down_grad, up_grad, second_terms)


def adamw(gradient, first_old, second_old, master, factor, step_rate, decay_rate):
    gradient = gradient * factor
    first_new = beta_one * first_old + (1 - beta_one) * gradient
    second_new = beta_two * second_old + (1 - beta_two) * gradient * gradient
    first_hat = first_new / (1 - beta_one**STEP)
    second_hat = second_new / (1 - beta_two**STEP)
    master_new = master - step_rate * (
        first_hat / (jnp.sqrt(second_hat) + adam_eps) + decay_rate * master
    )
    return (first_new, second_new, master_new, master_new.astype(jnp.bfloat16))


def low_rows(block_lanes, shared_lanes, row_width):
    pieces = row_width // 128

    def kernel(block_ref, shared_ref, block_out, shared_out, rows_out):
        for source, target in ((block_ref, block_out), (shared_ref, rows_out)):
            rows = target.shape[0]
            for piece in range(pieces):
                lanes = slice(piece * 128, (piece + 1) * 128)
                target[:, lanes] = source[pl.ds(piece, rows, stride=pieces), :].astype(low_type)
        shared_out[...] = shared_ref[...].astype(low_type)

    return pl.pallas_call(
        kernel,
        out_shape=(
            jax.ShapeDtypeStruct((block_lanes.shape[0] // pieces, row_width), low_type),
            jax.ShapeDtypeStruct(shared_lanes.shape, low_type),
            jax.ShapeDtypeStruct((shared_lanes.shape[0] // pieces, row_width), low_type),
        ),
        compiler_params=pltpu.CompilerParams(vmem_limit_bytes=32 * 2**20),
    )(block_lanes, shared_lanes)


def adamw_of(gradient, first_old, second_old, master, step_rate, decay_rate):
    first_new = beta_one * first_old + (1 - beta_one) * gradient
    second_new = beta_two * second_old + (1 - beta_two) * gradient * gradient
    first_hat = first_new / (1 - beta_one**STEP)
    second_hat = second_new / (1 - beta_two**STEP)
    master_new = master - step_rate * (
        first_hat / (jnp.sqrt(second_hat) + adam_eps) + decay_rate * master
    )
    return (first_new, second_new, master_new, master_new.astype(low_type))


def update(factor, block_rows, block_state, shared_lanes, shared_state):
    pieces = block_rows.shape[1] // 128

    def kernel(factor_ref, *refs):
        block_grad, shared_grad = refs[0], refs[4]
        scale = factor_ref[0, 0]
        rows = block_grad.shape[0]
        block_in, block_to = refs[1:4], refs[8:12]
        shared_in, shared_to = refs[5:8], refs[12:16]
        for piece in range(pieces):
            spots = pl.ds(piece, rows, stride=pieces)
            gradient = block_grad[:, piece * 128 : (piece + 1) * 128] * scale
            results = adamw_of(
                gradient, *[ref[spots, :] for ref in block_in], rate_matrix, weight_decay
            )
            for ref, result in zip(block_to[:3], results[:3]):
                ref[spots, :] = result
        block_to[3][...] = block_to[2][...].astype(low_type)
        results = adamw_of(
            shared_grad[...] * scale, *[ref[...] for ref in shared_in], rate_matrix, weight_decay
        )
        for ref, result in zip(shared_to, results):
            ref[...] = result

    kinds = (jnp.float32, jnp.float32, jnp.float32, low_type)
    shapes = [block_state[0].shape] * 4 + [shared_state[0].shape] * 4
    results = pl.pallas_call(
        kernel,
        in_specs=[pl.BlockSpec(memory_space=pltpu.SMEM)]
        + [pl.BlockSpec(memory_space=pltpu.VMEM)] * 8,
        out_shape=[jax.ShapeDtypeStruct(shape, kind) for shape, kind in zip(shapes, kinds * 2)],
        compiler_params=pltpu.CompilerParams(vmem_limit_bytes=40 * 2**20),
    )(factor.reshape(1, 1), block_rows, *block_state, shared_lanes, *shared_state)
    return (tuple(results[:4]), tuple(results[4:]))


TOKENS = 208
LANES = 128


def dot_tn(left_side, right_side):
    return lax.dot_general(
        left_side, right_side, (((0,), (0,)), ((), ())), preferred_element_type=jnp.float32
    )


def dot_nt(left_side, right_side):
    return lax.dot_general(
        left_side, right_side, (((1,), (1,)), ((), ())), preferred_element_type=jnp.float32
    )


def gelu_pair(raised):
    rate = math.sqrt(2.0 / math.pi)
    square = raised * raised
    curve = jnp.tanh(rate * (raised + 0.044715 * raised * square))
    half = 0.5 * (1.0 + curve)
    slope = half + 0.5 * raised * (1.0 - curve * curve) * rate * (1.0 + 0.134145 * square)
    return raised * half, slope


def unpack_kernel(lanes_ref, *refs):
    outs, work = refs[:-1], refs[-1]
    start = PIX * D // LANES
    for out in outs:
        depth, pieces = out.shape[0], out.shape[1] // LANES
        step = 64
        span = step * pieces

        def chunk(index, carry, out=out, start=start, pieces=pieces, span=span):
            source = pl.ds(pl.multiple_of(start + index * span, 64), span)
            work[:span, :] = lanes_ref[source, :].astype(jnp.float32)
            rows = pl.ds(pl.multiple_of(index * step, step), step)
            for piece in range(pieces):
                out[rows, piece * LANES : (piece + 1) * LANES] = work[
                    pl.ds(piece, step, stride=pieces), :
                ].astype(low_type)
            return carry

        lax.fori_loop(0, depth // step, chunk, 0)
        start += depth * pieces


def unpack_decoder(lanes):
    shapes = [(DD, 3 * DD), (DD, DD), (DD, DMLP), (DMLP, DD), (DD, PIX)]
    return pl.pallas_call(
        unpack_kernel,
        out_shape=[jax.ShapeDtypeStruct(shape, low_type) for shape in shapes],
        scratch_shapes=[pltpu.VMEM((64 * DMLP // LANES, LANES), jnp.float32)],
        compiler_params=pltpu.CompilerParams(vmem_limit_bytes=48 * 2**20),
        cost_estimate=pl.CostEstimate(
            flops=0, bytes_accessed=4 * math.prod(lanes.shape), transcendentals=0
        ),
    )(lanes)


def decoder_kernel(
    scale_ref,
    latent_ref,
    select_ref,
    mask_ref,
    table_ref,
    small_ref,
    pixels_ref,
    packed_w,
    out_w,
    up_w,
    down_w,
    head_w,
    grad_out,
    latent_out,
    small_out,
    loss_out,
    work,
    packed_ref,
    mixed_ref,
    prob_ref,
    raised_ref,
    activated_ref,
    packed_grad_ref,
):
    scaling = (DD // DHEADS) ** (-0.5)
    width = DD // DHEADS
    per_block = LANES // width
    first_gain, second_gain, last_gain, mask_token = [
        small_ref[row : row + 1, :] for row in range(4)
    ]
    mask = mask_ref[...]
    select = select_ref[...]
    key_valid = lax.broadcasted_iota(jnp.int32, (TOKENS, TOKENS), 1) < PATCHES
    lane_head = lax.broadcasted_iota(jnp.int32, (TOKENS, LANES), 1) // width
    quarter = DMLP // 4

    tokens = forward_dot(select, latent_ref[...]) + mask * mask_token + table_ref[...]
    first_norm, first_hat, first_inverse = norm_forward(tokens, first_gain)
    normed = first_norm.astype(low_type)
    for piece in range(3):
        columns = slice(piece * DD, (piece + 1) * DD)
        packed_ref[:, columns] = forward_dot(normed, packed_w[:, columns]).astype(low_type)
    mixed_ref[...] = jnp.zeros(mixed_ref.shape, jnp.float32)

    def attend(head, carry):
        block = pl.multiple_of(head // per_block * LANES, LANES)
        inside = lane_head == head % per_block
        query = jnp.where(inside, packed_ref[:, pl.ds(block, LANES)], 0)
        key = packed_ref[:, pl.ds(DD + block, LANES)]
        value = packed_ref[:, pl.ds(2 * DD + block, LANES)]
        scores = jnp.where(key_valid, dot_nt(query, key) * scaling, -1e30)
        exponent = jnp.exp(scores - jnp.max(scores, -1, keepdims=True))
        probability = exponent / jnp.sum(exponent, -1, keepdims=True)
        prob_ref[head] = probability
        mixed = forward_dot(probability.astype(low_type), value)
        mixed_ref[:, pl.ds(block, LANES)] += jnp.where(inside, mixed, 0.0)
        return carry

    lax.fori_loop(0, DHEADS, attend, 0)
    mixed_low = mixed_ref[...].astype(low_type)
    middle = tokens + forward_dot(mixed_low, out_w[...])
    second_norm, second_hat, second_inverse = norm_forward(middle, second_gain)
    inner = second_norm.astype(low_type)
    decoded = middle
    for part in range(4):
        columns = slice(part * quarter, (part + 1) * quarter)
        raised = forward_dot(inner, up_w[:, columns])
        activated, slope = gelu_pair(raised)
        raised_ref[:, columns] = slope
        activated = activated.astype(low_type)
        activated_ref[:, columns] = activated
        decoded = decoded + forward_dot(activated, down_w[columns, :])
    top_norm, top_hat, top_inverse = norm_forward(decoded, last_gain)
    top = top_norm.astype(low_type)
    predicted = forward_dot(top, head_w[...])
    target = pixels_ref[...].astype(jnp.float32)
    center = target - jnp.mean(target, -1, keepdims=True)
    target = center * lax.rsqrt(jnp.mean(center * center, -1, keepdims=True) + 1e-06)
    errors = predicted - target
    loss_out[...] = jnp.sum(
        mask * jnp.mean(errors * errors, -1, keepdims=True), axis=0, keepdims=True
    )
    pred_grad = (errors * (mask * scale_ref[0, 0])).astype(low_type)

    starts = [PIX * D // LANES]
    for size in (3 * DD * DD, DD * DD, DD * DMLP, DMLP * DD):
        starts.append(starts[-1] + size // LANES)
    grad_out[: starts[0], :] = jnp.zeros((starts[0], LANES), low_type)

    def put(left_side, right_ref_columns, pieces, base):
        depth = left_side.shape[1]
        for piece, columns in right_ref_columns:
            product = dot_tn(left_side, columns)
            for half in range(columns.shape[1] // LANES):
                work[pl.ds(base + piece + half, depth, stride=pieces), :] = product[
                    :, half * LANES : (half + 1) * LANES
                ]

    def flush(start, size):
        grad_out[start : start + size, :] = work[:size, :].astype(low_type)

    def pairs_of(values):
        return [
            (2 * pair, values[:, 2 * pair * LANES : 2 * (pair + 1) * LANES])
            for pair in range(values.shape[1] // (2 * LANES))
        ]

    put(top, pairs_of(pred_grad), PIX // LANES, 0)
    flush(starts[4], DD * PIX // LANES)
    decoded_grad, last_terms = norm_backward(
        dot_nt(pred_grad, head_w[...]), top_hat, top_inverse, last_gain
    )
    grad_low = decoded_grad.astype(low_type)
    inner_grad = jnp.zeros((TOKENS, DD), jnp.float32)
    for part in range(4):
        columns = slice(part * quarter, (part + 1) * quarter)
        put(activated_ref[:, columns], pairs_of(grad_low), DD // LANES, part * quarter * DD // LANES)
    flush(starts[3], DMLP * DD // LANES)
    for part in range(4):
        columns = slice(part * quarter, (part + 1) * quarter)
        act_grad = dot_nt(grad_low, down_w[columns, :])
        raised_grad = (act_grad * raised_ref[:, columns]).astype(low_type)
        put(inner, pairs_of(raised_grad), DMLP // LANES, part * quarter // LANES)
        inner_grad = inner_grad + dot_nt(raised_grad, up_w[:, columns])
    flush(starts[2], DD * DMLP // LANES)
    middle_part, second_terms = norm_backward(inner_grad, second_hat, second_inverse, second_gain)
    middle_grad = decoded_grad + middle_part
    middle_low = middle_grad.astype(low_type)
    put(mixed_low, pairs_of(middle_low), DD // LANES, 0)
    flush(starts[1], DD * DD // LANES)
    mixed_ref[...] = dot_nt(middle_low, out_w[...])
    packed_grad_ref[...] = jnp.zeros(packed_grad_ref.shape, jnp.float32)

    def attend_back(head, carry):
        block = pl.multiple_of(head // per_block * LANES, LANES)
        inside = lane_head == head % per_block
        out_grad = mixed_ref[:, pl.ds(block, LANES)].astype(low_type)
        query = packed_ref[:, pl.ds(block, LANES)]
        key = packed_ref[:, pl.ds(DD + block, LANES)]
        value = packed_ref[:, pl.ds(2 * DD + block, LANES)]
        probability = prob_ref[head]
        value_grad = dot_tn(probability.astype(low_type), out_grad)
        prob_grad = dot_nt(jnp.where(inside, out_grad, 0), value)
        score_grad = (
            probability * (prob_grad - jnp.sum(probability * prob_grad, -1, keepdims=True))
        ).astype(low_type)
        query_grad = forward_dot(score_grad, key) * scaling
        key_grad = dot_tn(score_grad, query) * scaling
        for piece, values in enumerate((query_grad, key_grad, value_grad)):
            packed_grad_ref[:, pl.ds(piece * DD + block, LANES)] += jnp.where(inside, values, 0.0)
        return carry

    lax.fori_loop(0, DHEADS, attend_back, 0)
    normed_grad = jnp.zeros((TOKENS, DD), jnp.float32)
    for piece in range(3):
        columns = slice(piece * DD, (piece + 1) * DD)
        packed_low = packed_grad_ref[:, columns].astype(low_type)
        put(normed, pairs_of(packed_low), 3 * DD // LANES, piece * DD // LANES)
        normed_grad = normed_grad + dot_nt(packed_low, packed_w[:, columns])
    flush(starts[0], 3 * DD * DD // LANES)
    token_part, first_terms = norm_backward(normed_grad, first_hat, first_inverse, first_gain)
    token_grad = middle_grad + token_part
    latent_out[...] = dot_tn(select, token_grad.astype(low_type)).astype(low_type)
    for row, terms in enumerate((first_terms, second_terms, last_terms, mask * token_grad)):
        small_out[row : row + 1, :] = jnp.sum(terms, axis=0, keepdims=True)


def decode(scale, latent, select, mask, table, small, pixels, weights, lane_rows):
    return pl.pallas_call(
        decoder_kernel,
        in_specs=[pl.BlockSpec(memory_space=pltpu.SMEM)]
        + [pl.BlockSpec(memory_space=pltpu.VMEM)] * 11,
        out_shape=(
            jax.ShapeDtypeStruct((lane_rows, LANES), low_type),
            jax.ShapeDtypeStruct(latent.shape, low_type),
            jax.ShapeDtypeStruct(small.shape, jnp.float32),
            jax.ShapeDtypeStruct((1, 1), jnp.float32),
        ),
        scratch_shapes=[
            pltpu.VMEM((DD * DMLP // LANES, LANES), jnp.float32),
            pltpu.VMEM((TOKENS, 3 * DD), low_type),
            pltpu.VMEM((TOKENS, DD), jnp.float32),
            pltpu.VMEM((DHEADS, TOKENS, TOKENS), jnp.float32),
            pltpu.VMEM((TOKENS, DMLP), jnp.float32),
            pltpu.VMEM((TOKENS, DMLP), low_type),
            pltpu.VMEM((TOKENS, 3 * DD), jnp.float32),
        ],
        compiler_params=pltpu.CompilerParams(vmem_limit_bytes=60 * 2**20),
        cost_estimate=pl.CostEstimate(
            flops=6 * TOKENS * lane_rows * LANES,
            bytes_accessed=4 * lane_rows * LANES,
            transcendentals=TOKENS * (DMLP + DHEADS * TOKENS),
        ),
    )(scale, latent, select, mask, table, small, pixels, *weights)


def on_device(
    pixels,
    visible,
    block_master,
    block_first,
    block_second,
    shared_master,
    shared_first,
    shared_second,
    gains_master,
    gains_first,
    gains_second,
):
    groups = lax.axis_size("mp")
    replicas = lax.axis_size("dp")
    member = lax.axis_index("mp")
    model_cols = D // groups
    mlp_cols = MLP // groups
    embed_cols = DD // groups
    block_rows = block_master.shape[1] // D
    shared_rows = shared_master.shape[0] // 128

    own_pixels = pick(pixels, member, 0)
    own_visible = pick(visible, member, 0)
    hidden_mask = (1 - own_visible).astype(jnp.float32)
    hidden_count = jnp.sum(1 - own_visible).astype(jnp.float32)

    block_lanes = block_master.reshape(-1, 128)
    shared_lanes = shared_master.reshape(-1, 128)
    block_rowed, shared_low, shared_rowed = low_rows(block_lanes, shared_lanes, D)
    block_flat = lax.all_gather(block_rowed, "dp", axis=0, tiled=True)

    patch_size = PIX * D
    head_rows = shared_master.shape[0] // D
    tail_length = patch_size - groups * head_rows * D
    early = 0 < tail_length <= shared_master.shape[0] and groups * head_rows < PIX
    small_length = gains_master.shape[0]
    small_row = jnp.concatenate([lax.reduce_precision(gains_master, 8, 7), hidden_count[None]])
    small_row = jnp.pad(small_row, (0, -small_row.shape[0] % 128))
    if early:
        patch_w, near_rows = spread_patch(shared_rowed, tail_length // D)
        small_row = after(small_row, near_rows)
        shared_low = after(shared_low, near_rows)
    small_table = gather_small(small_row)
    gain_flat = small_table[:, :small_length].reshape(-1)
    count_total = jnp.sum(small_table[:, small_length])
    shared_column = reorder(share(shared_low), member)
    shared_flat = lax.all_gather(shared_column, "dp", axis=0).reshape(-1, 128)

    bounds = [0, 3 * model_cols, model_cols, mlp_cols, mlp_cols, embed_cols]
    bounds = [sum(bounds[: place + 1]) for place in range(len(bounds))]
    enc_packed, enc_out, enc_up, enc_down, enc_latent = [
        block_flat[low:high] for low, high in zip(bounds[:-1], bounds[1:])
    ]
    enc_packed = enc_packed.reshape(D, 3 * model_cols)
    enc_up = enc_up.reshape(D, mlp_cols)
    own_latent_w = enc_latent.reshape(D, embed_cols)
    latent_w = reorder(share(own_latent_w), member)

    dec_weights = unpack_decoder(shared_flat)
    if not early:
        patch_w = shared_flat[: patch_size // 128].reshape(PIX, D)
    enc_one, enc_two, enc_last, dec_one, dec_two, dec_last, mask_token = cut_pieces(
        gain_flat, [(D,), (D,), (D,), (DD,), (DD,), (DD,), (DD,)]
    )
    enc_scaling = (D // HEADS) ** (-0.5)
    enc_heads = HEADS // groups

    near_visible = reorder(visible, member)
    near_pixels = reorder(pixels, member)
    select, slot_patch, key_valid = visible_slots(near_visible)
    chosen = (slot_patch[:, :, None] == jnp.arange(PATCHES)[None, None, :]).astype(low_type)
    seen_patches = jnp.einsum(
        "isp,ipd->isd", chosen, near_pixels, preferred_element_type=jnp.float32
    ).astype(low_type)
    residual = forward_dot(seen_patches, patch_w) + position_table(slot_patch, D)
    first_norm, first_hat, first_inverse = norm_forward(residual, enc_one)
    normed = first_norm.astype(low_type)
    packed = forward_dot(normed, enc_packed).astype(low_type)
    mixed_heads, log_total = attend_forward(packed, key_valid, enc_heads, enc_scaling)
    middle = residual[0] + collect(forward_dot(mixed_heads, enc_out))
    second_norm, second_hat, second_inverse = norm_forward(middle, enc_two)
    inner_low = share(second_norm.astype(low_type))
    raised = forward_dot(inner_low, enc_up)
    activated = jax.nn.gelu(raised, approximate=True).astype(low_type)
    encoded = middle + collect(forward_dot(activated, enc_down))
    final_norm, final_hat, final_inverse = norm_forward(encoded, enc_last)
    final_low = final_norm.astype(low_type)
    latent = jnp.einsum(
        "sd,mde->sme", final_low, latent_w, preferred_element_type=jnp.float32
    ).astype(low_type)
    latent = latent.reshape(VIS, DD)
    final_all = share(final_low)

    pad = ((0, TOKENS - PATCHES), (0, 0))
    shared_grad, latent_grad, dec_small, loss_local = decode(
        (2.0 / (PIX * count_total)).reshape(1, 1),
        latent,
        jnp.pad(select[0].T.astype(low_type), pad),
        jnp.pad(hidden_mask[:, None], pad),
        jnp.pad(position_table(jnp.arange(PATCHES), DD), pad),
        jnp.pad(jnp.stack([dec_one, dec_two, dec_last, mask_token]), ((0, 4), (0, 0))),
        jnp.pad(own_pixels, pad),
        dec_weights,
        shared_flat.shape[0],
    )
    loss_local = loss_local[0, 0]
    shared_grad = shared_grad.reshape(replicas, groups * shared_rows, 128)
    column_share, first_marks, second_marks = reduce_dp(shared_grad)
    shared_share = reduce_mp(column_share.reshape(groups, shared_rows, 128))

    final_grad = jnp.einsum(
        "sme,mde->sd",
        latent_grad.reshape(VIS, groups, embed_cols),
        latent_w,
        preferred_element_type=jnp.float32,
    )
    encoded_grad, enc_last_terms = norm_backward(final_grad, final_hat, final_inverse, enc_last)
    encoded_low = share(encoded_grad.astype(low_type))
    latent_cut = latent_grad.reshape(VIS, groups, embed_cols)
    latent_near = jnp.stack(
        [pick(latent_cut, member, 1)]
        + [swap(pick(latent_cut, member ^ step, 1), "mp", step) for step in range(1, groups)]
    )
    latent_wgrad = outer_sum(final_all, latent_near)
    middle_grad, down_grad, up_grad, enc_two_terms = mlp_backward(
        encoded_grad,
        encoded_low,
        activated,
        raised,
        inner_low,
        enc_up,
        enc_down,
        collect,
        (second_hat, second_inverse, enc_two),
    )
    middle_low = share(after(middle_grad, first_marks[0] + first_marks[1]).astype(low_type))
    out_grad = outer_sum(mixed_heads, middle_low)
    mixed_grad = back_dot(middle_low, enc_out).astype(low_type)
    pack_grad = attend_backward(packed, log_total, key_valid, mixed_grad, enc_heads, enc_scaling)
    packed_grad = outer_sum(normed, pack_grad)
    residual_part, enc_one_terms = norm_backward(
        collect(after(back_dot(pack_grad, enc_packed), second_marks[0] + second_marks[1])), first_hat[0], first_inverse[0], enc_one
    )
    residual_grad = middle_grad + residual_part
    residual_low = residual_grad.astype(low_type)

    pad_length = gain_flat.shape[0] - 3 * D - 4 * DD
    gain_grad = jnp.concatenate(
        [
            jnp.sum(enc_one_terms, 0),
            jnp.sum(enc_two_terms, 0),
            jnp.sum(enc_last_terms, 0),
            dec_small[:4].reshape(-1),
            jnp.zeros((pad_length,), jnp.float32),
        ]
    )
    block_grad = jnp.concatenate(
        [
            piece.astype(low_type).reshape(-1, D)
            for piece in (packed_grad, out_grad, up_grad, down_grad, latent_wgrad)
        ]
    ).reshape(replicas, block_rows, D)
    block_share = reduce_dp(block_grad)[0]
    place = lax.axis_index("dp")
    if early:
        rows = return_patch(outer_sum(seen_patches, share(residual_low)), head_rows)
        owner = (place == 0) | ((place == 1) & (member == 0))
        shared_share = shared_share + jnp.where(owner, rows.reshape(-1, 128), 0.0)
    else:
        patch_rows = outer_sum(seen_patches[0], residual_low).astype(low_type).reshape(-1, 128)
        patch_rows = jnp.pad(patch_rows, ((0, shared_flat.shape[0] - patch_rows.shape[0]), (0, 0)))
        column = reduce_dp(patch_rows.reshape(replicas, groups * shared_rows, 128))[0]
        shared_share = shared_share + reduce_mp(column.reshape(groups, shared_rows, 128))
    gain_total = sum_small(gain_grad.reshape(-1, 128))
    own = lax.axis_index("dp") * groups + member
    gain_share = lax.dynamic_slice_in_dim(gain_total.reshape(-1), own * small_length, small_length)
    squares = (
        jnp.sum(block_share * block_share)
        + jnp.sum(shared_share * shared_share)
        + jnp.sum(gain_share * gain_share)
    )
    sums = sum_small(jnp.stack([squares, loss_local]).reshape(1, 2))
    square_total, loss_total = sums[0, 0], sums[0, 1]
    grad_norm = jnp.sqrt(square_total)
    factor = jnp.minimum(1.0, clip_norm / (grad_norm + 1e-06))
    block_out, shared_out = update(
        factor,
        block_share,
        [block_first.reshape(-1, 128), block_second.reshape(-1, 128), block_lanes],
        shared_share,
        [shared_first.reshape(-1, 128), shared_second.reshape(-1, 128), shared_lanes],
    )
    block_out = tuple(piece.reshape(block_master.shape) for piece in block_out)
    shared_out = tuple(piece.reshape(-1) for piece in shared_out)
    gain_out = adamw(gain_share, gains_first, gains_second, gains_master, factor, rate_gains, 0.0)
    return (grad_norm, loss_total, count_total) + block_out + shared_out + gain_out


def solution(mesh):
    return jax.shard_map(
        on_device,
        mesh=mesh,
        in_specs=(
            P("dp", None, None),
            P("dp", None),
            P("mp", "dp"),
            P("mp", "dp"),
            P("mp", "dp"),
            P(("dp", "mp")),
            P(("dp", "mp")),
            P(("dp", "mp")),
            P(("dp", "mp")),
            P(("dp", "mp")),
            P(("dp", "mp")),
        ),
        out_specs=(
            P(),
            P(),
            P(),
            P("mp", "dp"),
            P("mp", "dp"),
            P("mp", "dp"),
            P("mp", "dp"),
            P(("dp", "mp")),
            P(("dp", "mp")),
            P(("dp", "mp")),
            P(("dp", "mp")),
            P(("dp", "mp")),
            P(("dp", "mp")),
            P(("dp", "mp")),
            P(("dp", "mp")),
        ),
        check_vma=False,
    )
```

```python
from functools import partial
import math

import jax
import jax.numpy as jnp
from jax import lax
from jax.experimental import pallas as pl
from jax.experimental.pallas import tpu as pltpu
from jax.sharding import PartitionSpec as P

D = 768
HEADS = 12
MLP = 3072
DD = 512
DHEADS = 16
DMLP = 2048
PIX = 768
PATCHES = 196
VIS = 64
STEP = 10


low_type = jnp.bfloat16
clip_norm = 0.0002
beta_one = 0.9
beta_two = 0.95
adam_eps = 1e-10
rate_matrix = 0.03
rate_gains = 0.7
weight_decay = 0.1


def forward_dot(left_side, right_side):
    return jnp.dot(left_side, right_side, preferred_element_type=jnp.float32)


def back_dot(left_side, right_side):
    return lax.dot_general(
        left_side,
        right_side,
        (((left_side.ndim - 1,), (1,)), ((), ())),
        preferred_element_type=jnp.float32,
    )


def outer_sum(left_side, right_side):
    left_rows = left_side.reshape(-1, left_side.shape[-1])
    right_rows = right_side.reshape(-1, right_side.shape[-1])
    return lax.dot_general(
        left_rows, right_rows, (((0,), (0,)), ((), ())), preferred_element_type=jnp.float32
    )


def swap(values, axis_name, distance):
    count = lax.axis_size(axis_name)
    return lax.ppermute(values, axis_name, [(place, place ^ distance) for place in range(count)])


def share(values):
    groups = lax.axis_size("mp")
    return jnp.stack([values] + [swap(values, "mp", step) for step in range(1, groups)])


def collect(partial_terms):
    total = partial_terms[0]
    for step in range(1, partial_terms.shape[0]):
        total = total + swap(partial_terms[step].astype(low_type), "mp", step).astype(jnp.float32)
    return total


def pick(values, index, dim):
    return lax.dynamic_index_in_dim(values, index, dim, keepdims=False)


def reorder(values, place):
    return jnp.stack([pick(values, place ^ step, 0) for step in range(values.shape[0])])


def bits_of(count):
    return count.bit_length() - 1


def after(values, token):
    first = token[(0,) * token.ndim].astype(jnp.float32)
    return values + jnp.minimum(jnp.abs(first), 0.0).astype(values.dtype)


def after_all(values, tokens):
    for token in tokens:
        values = after(values, token)
    return values


def half_cut(values, side, dim):
    return (pick(values, side, dim), pick(values, 1 - side, dim))


def reduce_chips(kept_whole, got_whole):
    width = bits_of(lax.axis_size("dp"))
    place = lax.axis_index("dp")
    rows = kept_whole.shape[1]
    higher = tuple(range(3, width))
    halves = []
    stages = [[] for level in range(width - 1)]
    for part, order in (((0, rows // 2), (1, 2) + higher), ((rows // 2, rows), (2, 1) + higher)):
        left = list(range(width - 1, 0, -1))
        split = (2,) * (width - 1) + (part[1] - part[0],) + kept_whole.shape[2:]
        both = [
            lax.slice_in_dim(piece, part[0], part[1], axis=1).reshape(split)
            for piece in (kept_whole, got_whole)
        ]
        total = None
        for level, bit in enumerate(order):
            dim = left.index(bit)
            side = (place >> bit) & 1
            if total is None:
                kept, sent = [
                    one.astype(jnp.float32) + two.astype(jnp.float32)
                    for one, two in zip(half_cut(both[0], side, dim), half_cut(both[1], side, dim))
                ]
            else:
                kept, sent = half_cut(total, side, dim)
            sent = sent.astype(low_type)
            stages[level].append(sent)
            total = kept + swap(sent, "dp", 1 << bit).astype(jnp.float32)
            left.remove(bit)
        halves.append(total)
    return jnp.concatenate(halves, 0), stages


def reduce_dp(values):
    place = lax.axis_index("dp")
    shaped = values.reshape((-1, 2) + values.shape[1:])
    kept, sent = half_cut(shaped, place & 1, 1)
    return reduce_chips(kept, swap(sent, "dp", 1))


def reduce_mp(values):
    member = lax.axis_index("mp")
    total = pick(values, member, 0)
    for step in range(1, values.shape[0]):
        sent = pick(values, member ^ step, 0).astype(low_type)
        total = total + swap(sent, "mp", step).astype(jnp.float32)
    return total, sent


def sum_small(row):
    for bit in range(bits_of(lax.axis_size("dp"))):
        row = row + swap(row, "dp", 1 << bit)
    return jnp.sum(reorder(share(row), lax.axis_index("mp")), 0)


def pair_permute(values, pairs):
    return lax.ppermute(values, ("dp", "mp"), pairs)


def gather_early(small_row, block_rows):
    replicas = lax.axis_size("dp")
    place = lax.axis_index("dp")
    member = lax.axis_index("mp")
    width = bits_of(replicas)
    higher = tuple(range(3, width))
    orders = ((1, 2) + higher, (2, 1) + higher)
    half_rows = block_rows.shape[0] // 2
    halves = [block_rows[None, :half_rows], block_rows[None, half_rows:]]
    table = reorder(share(small_row), member)[None]
    for level in range(width - 1):
        halves = [
            jnp.concatenate([half, swap(half, "dp", 1 << order[level])], 0)
            for half, order in zip(halves, orders)
        ]
    placed = []
    for half, order in zip(halves, orders):
        shaped = half.reshape((2,) * (width - 1) + half.shape[1:])
        dims = [width - 2 - order.index(bit) for bit in range(width - 1, 0, -1)]
        placed.append(shaped.transpose(dims + [width - 1, width]).reshape(half.shape))
    near = jnp.concatenate(placed, 1)
    both = jnp.stack([near, swap(near, "dp", 1)], 1).reshape((replicas,) + block_rows.shape)
    block_flat = reorder(both, place).reshape(-1, block_rows.shape[1])
    for bit in range(width):
        table = jnp.concatenate([table, swap(table, "dp", 1 << bit)], 0)
    return reorder(table, place).reshape(-1, small_row.shape[0]), block_flat


def return_patch(gradient, row_count):
    replicas = lax.axis_size("dp")
    groups = lax.axis_size("mp")
    member = lax.axis_index("mp")
    even = (lax.axis_index("dp") & 1) == 0
    rows = lax.dynamic_slice_in_dim(gradient, member * row_count, row_count, 0)
    tail = gradient[groups * row_count :]
    tail = jnp.pad(tail, ((0, row_count - tail.shape[0]), (0, 0)))
    total = jnp.where(even, rows, tail) + swap(jnp.where(even, tail, rows), "dp", 1)
    total_low = total.astype(low_type)
    for dp in range(2, replicas, 2):
        pairs = [(dp * groups + mp, mp) for mp in range(groups)] + [((dp + 1) * groups, groups)]
        total = total + pair_permute(total_low, pairs).astype(jnp.float32)
    return total


def position_table(places, row_width):
    column = jnp.arange(row_width)
    step_rate = jnp.exp(-(column // 2 * 2).astype(jnp.float32) * (math.log(10000.0) / row_width))
    angle = places.astype(jnp.float32)[..., None] * step_rate
    return jnp.where(column % 2 == 0, jnp.sin(angle), jnp.cos(angle))


def visible_slots(visible):
    slot_rank = jnp.cumsum(visible, 1) - 1
    select = (
        (visible[:, None, :] == 1) & (slot_rank[:, None, :] == jnp.arange(VIS)[None, :, None])
    ).astype(jnp.int32)
    slot_patch = jnp.sum(select * jnp.arange(visible.shape[1])[None, None, :], 2)
    key_valid = jnp.arange(VIS)[None, :] < jnp.sum(visible, 1)[:, None]
    return (select, slot_patch, key_valid)


def cut_pieces(flat_vector, shapes):
    pieces = []
    offset = 0
    for shape in shapes:
        length = math.prod(shape)
        pieces.append(flat_vector[offset : offset + length].reshape(shape))
        offset += length
    return pieces


def norm_forward(residual, gain_vec):
    center = residual - jnp.mean(residual, -1, keepdims=True)
    inverse = lax.rsqrt(jnp.mean(center * center, -1, keepdims=True) + 1e-06)
    normal_hat = center * inverse
    return (normal_hat * gain_vec, normal_hat, inverse)


def norm_backward(gradient, normal_hat, inverse, gain_vec):
    hat_grad = gradient * gain_vec
    residual_grad = inverse * (
        hat_grad
        - jnp.mean(hat_grad, -1, keepdims=True)
        - normal_hat * jnp.mean(hat_grad * normal_hat, -1, keepdims=True)
    )
    return (residual_grad, gradient * normal_hat)


def split_heads(packed, head_count):
    batch_size, length, row_width = packed.shape
    unpacked = packed.reshape(batch_size, length, 3, head_count, row_width // (3 * head_count))
    return (unpacked[:, :, 0], unpacked[:, :, 1], unpacked[:, :, 2])


def scores_of(query_part, key_part, key_valid, scaling):
    raw_scores = (
        jnp.einsum("blhd,bmhd->bhlm", query_part, key_part, preferred_element_type=jnp.float32)
        * scaling
    )
    return jnp.where(key_valid[:, None, None, :], raw_scores, -1e30)


def attend_forward(packed, key_valid, head_count, scaling):
    query_part, key_part, value_part = split_heads(packed, head_count)
    scores = scores_of(query_part, key_part, key_valid, scaling)
    row_top = jnp.max(scores, -1, keepdims=True)
    exponent = jnp.exp(scores - row_top)
    row_total = jnp.sum(exponent, -1, keepdims=True)
    probability = (exponent / row_total).astype(low_type)
    mixed_heads = jnp.einsum(
        "bhlm,bmhd->blhd", probability, value_part, preferred_element_type=jnp.float32
    )
    batch_size, length = (key_valid.shape[0], packed.shape[1])
    return (
        mixed_heads.reshape(batch_size, length, -1).astype(low_type),
        row_top + jnp.log(row_total),
    )


def attend_backward(packed, log_total, key_valid, mixed_grad, head_count, scaling):
    query_part, key_part, value_part = split_heads(packed, head_count)
    batch_size, length, row_width = mixed_grad.shape
    out_grad = mixed_grad.reshape(batch_size, length, head_count, -1)
    probability = jnp.exp(scores_of(query_part, key_part, key_valid, scaling) - log_total)
    value_grad = jnp.einsum(
        "bhlm,blhd->bmhd",
        probability.astype(low_type),
        out_grad,
        preferred_element_type=jnp.float32,
    )
    prob_grad = jnp.einsum(
        "blhd,bmhd->bhlm", out_grad, value_part, preferred_element_type=jnp.float32
    )
    score_grad = (
        probability * (prob_grad - jnp.sum(probability * prob_grad, -1, keepdims=True))
    ).astype(low_type)
    query_grad = (
        jnp.einsum("bhlm,bmhd->blhd", score_grad, key_part, preferred_element_type=jnp.float32)
        * scaling
    )
    key_grad = (
        jnp.einsum("bhlm,blhd->bmhd", score_grad, query_part, preferred_element_type=jnp.float32)
        * scaling
    )
    stacked = jnp.stack([query_grad, key_grad, value_grad], 2)
    return stacked.reshape(batch_size, length, -1).astype(low_type)


def cut_rows(rows, shapes):
    pieces = []
    offset = 0
    for shape in shapes:
        length = math.prod(shape) // 128
        pieces.append(rows[offset : offset + length].reshape(shape))
        offset += length
    return pieces


def mlp_backward(
    gradient, grad_low, activated, raised, inner_low, up_w, down_w, total_sum, norm_saved
):
    down_grad = outer_sum(activated, grad_low)
    act_grad = back_dot(grad_low, down_w)
    unused, gelu_back = jax.vjp(partial(jax.nn.gelu, approximate=True), raised)
    raised_grad = gelu_back(act_grad)[0].astype(low_type)
    up_grad = outer_sum(inner_low, raised_grad)
    inner_grad = total_sum(back_dot(raised_grad, up_w))
    normal_hat, inverse, gain_vec = norm_saved
    middle_part, second_terms = norm_backward(inner_grad, normal_hat, inverse, gain_vec)
    return (gradient + middle_part, down_grad, up_grad, second_terms)


def adamw(gradient, first_old, second_old, master, factor, step_rate, decay_rate):
    gradient = gradient * factor
    first_new = beta_one * first_old + (1 - beta_one) * gradient
    second_new = beta_two * second_old + (1 - beta_two) * gradient * gradient
    first_hat = first_new / (1 - beta_one**STEP)
    second_hat = second_new / (1 - beta_two**STEP)
    master_new = master - step_rate * (
        first_hat / (jnp.sqrt(second_hat) + adam_eps) + decay_rate * master
    )
    return (first_new, second_new, master_new, master_new.astype(jnp.bfloat16))


def low_rows(block_lanes, shared_lanes, row_width):
    pieces = row_width // 128

    def kernel(block_ref, shared_ref, block_out, shared_out, rows_out):
        for source, target in ((block_ref, block_out), (shared_ref, rows_out)):
            rows = target.shape[0]
            for piece in range(pieces):
                lanes = slice(piece * 128, (piece + 1) * 128)
                target[:, lanes] = source[pl.ds(piece, rows, stride=pieces), :].astype(low_type)
        shared_out[...] = shared_ref[...].astype(low_type)

    return pl.pallas_call(
        kernel,
        out_shape=(
            jax.ShapeDtypeStruct((block_lanes.shape[0] // pieces, row_width), low_type),
            jax.ShapeDtypeStruct(shared_lanes.shape, low_type),
            jax.ShapeDtypeStruct((shared_lanes.shape[0] // pieces, row_width), low_type),
        ),
        compiler_params=pltpu.CompilerParams(vmem_limit_bytes=32 * 2**20),
    )(block_lanes, shared_lanes)


def adamw_of(gradient, first_old, second_old, master, step_rate, decay_rate):
    first_new = beta_one * first_old + (1 - beta_one) * gradient
    second_new = beta_two * second_old + (1 - beta_two) * gradient * gradient
    first_hat = first_new / (1 - beta_one**STEP)
    second_hat = second_new / (1 - beta_two**STEP)
    master_new = master - step_rate * (
        first_hat / (jnp.sqrt(second_hat) + adam_eps) + decay_rate * master
    )
    return (first_new, second_new, master_new, master_new.astype(low_type))


def update(factor, block_rows, block_state, shared_lanes, shared_state):
    pieces = block_rows.shape[1] // 128

    def kernel(factor_ref, *refs):
        block_grad, shared_grad = refs[0], refs[4]
        scale = factor_ref[0, 0]
        rows = block_grad.shape[0]
        block_in, block_to = refs[1:4], refs[8:12]
        shared_in, shared_to = refs[5:8], refs[12:16]
        for piece in range(pieces):
            spots = pl.ds(piece, rows, stride=pieces)
            gradient = block_grad[:, piece * 128 : (piece + 1) * 128] * scale
            results = adamw_of(
                gradient, *[ref[spots, :] for ref in block_in], rate_matrix, weight_decay
            )
            for ref, result in zip(block_to[:3], results[:3]):
                ref[spots, :] = result
        block_to[3][...] = block_to[2][...].astype(low_type).reshape(block_to[3].shape)
        results = adamw_of(
            shared_grad[...] * scale, *[ref[...] for ref in shared_in], rate_matrix, weight_decay
        )
        for ref, result in zip(shared_to, results):
            ref[...] = result

    kinds = (jnp.float32, jnp.float32, jnp.float32, low_type)
    shapes = [block_state[0].shape] * 4 + [shared_state[0].shape] * 4
    shapes[3] = (1, math.prod(shapes[3]))
    results = pl.pallas_call(
        kernel,
        in_specs=[pl.BlockSpec(memory_space=pltpu.SMEM)]
        + [pl.BlockSpec(memory_space=pltpu.VMEM)] * 8,
        out_shape=[jax.ShapeDtypeStruct(shape, kind) for shape, kind in zip(shapes, kinds * 2)],
        compiler_params=pltpu.CompilerParams(vmem_limit_bytes=40 * 2**20),
    )(factor.reshape(1, 1), block_rows, *block_state, shared_lanes, *shared_state)
    return (tuple(results[:4]), tuple(results[4:]))


TOKENS = 208
LANES = 128


def dot_tn(left_side, right_side):
    return lax.dot_general(
        left_side, right_side, (((0,), (0,)), ((), ())), preferred_element_type=jnp.float32
    )


def dot_nt(left_side, right_side):
    return lax.dot_general(
        left_side, right_side, (((1,), (1,)), ((), ())), preferred_element_type=jnp.float32
    )


def gelu_pair(raised):
    rate = math.sqrt(2.0 / math.pi)
    square = raised * raised
    curve = jnp.tanh(rate * (raised + 0.044715 * raised * square))
    half = 0.5 * (1.0 + curve)
    slope = half + 0.5 * raised * (1.0 - curve * curve) * rate * (1.0 + 0.134145 * square)
    return raised * half, slope


def unpack(lanes, first_entry, shapes):
    step = 64

    def kernel(lanes_ref, *refs):
        work = refs[-1]
        start = first_entry // LANES
        for out in refs[:-1]:
            depth, pieces = out.shape[0], out.shape[1] // LANES
            span = step * pieces

            def chunk(index, carry, out=out, start=start, pieces=pieces, span=span):
                source = pl.ds(pl.multiple_of(start + index * span, 64), span)
                work[:span, :] = lanes_ref[source, :].astype(jnp.float32)
                rows = pl.ds(pl.multiple_of(index * step, step), step)
                for piece in range(pieces):
                    out[rows, piece * LANES : (piece + 1) * LANES] = work[
                        pl.ds(piece, step, stride=pieces), :
                    ].astype(low_type)
                return carry

            lax.fori_loop(0, depth // step, chunk, 0)
            start += depth * pieces

    entries = sum(math.prod(shape) for shape in shapes)
    widest = max(shape[1] for shape in shapes)
    block = first_entry // LANES + entries // LANES
    return pl.pallas_call(
        kernel,
        grid=(1,),
        in_specs=[pl.BlockSpec((block, LANES), lambda index: (0, 0))],
        out_specs=[pl.BlockSpec(shape, lambda index: (0, 0)) for shape in shapes],
        out_shape=[jax.ShapeDtypeStruct(shape, low_type) for shape in shapes],
        scratch_shapes=[pltpu.VMEM((step * widest // LANES, LANES), jnp.float32)],
        compiler_params=pltpu.CompilerParams(vmem_limit_bytes=56 * 2**20),
        cost_estimate=pl.CostEstimate(flops=0, bytes_accessed=4 * entries, transcendentals=0),
    )(lanes)


def decoder_kernel(
    core_ref,
    scale_ref,
    latent_ref,
    select_ref,
    mask_ref,
    table_ref,
    small_ref,
    pixels_ref,
    packed_w,
    out_w,
    up_w,
    down_w,
    head_w,
    sent_out,
    kept_out,
    latent_out,
    small_out,
    loss_out,
    grad_ref,
    copy_sems,
    work,
    packed_ref,
    mixed_ref,
    prob_ref,
    raised_ref,
    activated_ref,
    packed_grad_ref,
):
    scaling = (DD // DHEADS) ** (-0.5)
    width = DD // DHEADS
    per_block = LANES // width
    first_gain, second_gain, last_gain, mask_token = [
        small_ref[row : row + 1, :] for row in range(4)
    ]
    mask = mask_ref[...]
    select = select_ref[...]
    key_valid = lax.broadcasted_iota(jnp.int32, (TOKENS, TOKENS), 1) < PATCHES
    lane_head = lax.broadcasted_iota(jnp.int32, (TOKENS, LANES), 1) // width
    quarter = DMLP // 4

    tokens = forward_dot(select, latent_ref[...]) + mask * mask_token + table_ref[...]
    first_norm, first_hat, first_inverse = norm_forward(tokens, first_gain)
    normed = first_norm.astype(low_type)
    for piece in range(3):
        columns = slice(piece * DD, (piece + 1) * DD)
        packed_ref[:, columns] = forward_dot(normed, packed_w[:, columns]).astype(low_type)
    mixed_ref[...] = jnp.zeros(mixed_ref.shape, jnp.float32)

    def attend(head, carry):
        block = pl.multiple_of(head // per_block * LANES, LANES)
        inside = lane_head == head % per_block
        query = jnp.where(inside, packed_ref[:, pl.ds(block, LANES)], 0)
        key = packed_ref[:, pl.ds(DD + block, LANES)]
        value = packed_ref[:, pl.ds(2 * DD + block, LANES)]
        scores = jnp.where(key_valid, dot_nt(query, key) * scaling, -1e30)
        exponent = jnp.exp(scores - jnp.max(scores, -1, keepdims=True))
        probability = exponent / jnp.sum(exponent, -1, keepdims=True)
        prob_ref[head] = probability
        mixed = forward_dot(probability.astype(low_type), value)
        mixed_ref[:, pl.ds(block, LANES)] += jnp.where(inside, mixed, 0.0)
        return carry

    lax.fori_loop(0, DHEADS, attend, 0)
    mixed_low = mixed_ref[...].astype(low_type)
    middle = tokens + forward_dot(mixed_low, out_w[...])
    second_norm, second_hat, second_inverse = norm_forward(middle, second_gain)
    inner = second_norm.astype(low_type)
    decoded = middle
    for part in range(4):
        columns = slice(part * quarter, (part + 1) * quarter)
        raised = forward_dot(inner, up_w[:, columns])
        activated, slope = gelu_pair(raised)
        raised_ref[:, columns] = slope
        activated = activated.astype(low_type)
        activated_ref[:, columns] = activated
        decoded = decoded + forward_dot(activated, down_w[columns, :])
    top_norm, top_hat, top_inverse = norm_forward(decoded, last_gain)
    top = top_norm.astype(low_type)
    predicted = forward_dot(top, head_w[...])
    target = pixels_ref[...].astype(jnp.float32)
    center = target - jnp.mean(target, -1, keepdims=True)
    target = center * lax.rsqrt(jnp.mean(center * center, -1, keepdims=True) + 1e-06)
    errors = predicted - target
    loss_out[...] = jnp.sum(
        mask * jnp.mean(errors * errors, -1, keepdims=True), axis=0, keepdims=True
    )
    pred_grad = (errors * (mask * scale_ref[0, 0])).astype(low_type)

    starts = [PIX * D // LANES]
    for size in (3 * DD * DD, DD * DD, DD * DMLP, DMLP * DD):
        starts.append(starts[-1] + size // LANES)
    grad_ref[: starts[0], :] = jnp.zeros((starts[0], LANES), low_type)
    slot_rows = sent_out.shape[1]
    slots = 2 * sent_out.shape[0]
    core = core_ref[0, 0]
    copies = []

    def send_from(first_row, last_row):
        for slot in range(slots):
            if first_row <= slot * slot_rows < last_row:
                rows = grad_ref.at[pl.ds(slot * slot_rows, slot_rows), :]
                side = slot % 2
                pair = slot // 2

                def start(target, rows=rows, pair=pair, slot=slot):
                    pltpu.make_async_copy(rows, target.at[pair], copy_sems.at[slot]).start()

                pl.when(core == side)(partial(start, kept_out))
                pl.when(core != side)(partial(start, sent_out))
                copies.append(
                    pltpu.make_async_copy(rows, kept_out.at[pair], copy_sems.at[slot])
                )

    def put(left_side, right_ref_columns, pieces, base):
        depth = left_side.shape[1]
        for piece, columns in right_ref_columns:
            product = dot_tn(left_side, columns)
            for half in range(columns.shape[1] // LANES):
                work[pl.ds(base + piece + half, depth, stride=pieces), :] = product[
                    :, half * LANES : (half + 1) * LANES
                ]

    def flush(start, size):
        grad_ref[start : start + size, :] = work[:size, :].astype(low_type)
        send_from(start, start + size)

    def pairs_of(values):
        return [
            (2 * pair, values[:, 2 * pair * LANES : 2 * (pair + 1) * LANES])
            for pair in range(values.shape[1] // (2 * LANES))
        ]

    put(top, pairs_of(pred_grad), PIX // LANES, 0)
    flush(starts[4], DD * PIX // LANES)
    decoded_grad, last_terms = norm_backward(
        dot_nt(pred_grad, head_w[...]), top_hat, top_inverse, last_gain
    )
    grad_low = decoded_grad.astype(low_type)
    inner_grad = jnp.zeros((TOKENS, DD), jnp.float32)
    for part in range(4):
        columns = slice(part * quarter, (part + 1) * quarter)
        put(activated_ref[:, columns], pairs_of(grad_low), DD // LANES, part * quarter * DD // LANES)
    flush(starts[3], DMLP * DD // LANES)
    for part in range(4):
        columns = slice(part * quarter, (part + 1) * quarter)
        act_grad = dot_nt(grad_low, down_w[columns, :])
        raised_grad = (act_grad * raised_ref[:, columns]).astype(low_type)
        put(inner, pairs_of(raised_grad), DMLP // LANES, part * quarter // LANES)
        inner_grad = inner_grad + dot_nt(raised_grad, up_w[:, columns])
    flush(starts[2], DD * DMLP // LANES)
    middle_part, second_terms = norm_backward(inner_grad, second_hat, second_inverse, second_gain)
    middle_grad = decoded_grad + middle_part
    middle_low = middle_grad.astype(low_type)
    put(mixed_low, pairs_of(middle_low), DD // LANES, 0)
    flush(starts[1], DD * DD // LANES)
    mixed_ref[...] = dot_nt(middle_low, out_w[...])
    packed_grad_ref[...] = jnp.zeros(packed_grad_ref.shape, jnp.float32)

    def attend_back(head, carry):
        block = pl.multiple_of(head // per_block * LANES, LANES)
        inside = lane_head == head % per_block
        out_grad = mixed_ref[:, pl.ds(block, LANES)].astype(low_type)
        query = packed_ref[:, pl.ds(block, LANES)]
        key = packed_ref[:, pl.ds(DD + block, LANES)]
        value = packed_ref[:, pl.ds(2 * DD + block, LANES)]
        probability = prob_ref[head]
        value_grad = dot_tn(probability.astype(low_type), out_grad)
        prob_grad = dot_nt(jnp.where(inside, out_grad, 0), value)
        score_grad = (
            probability * (prob_grad - jnp.sum(probability * prob_grad, -1, keepdims=True))
        ).astype(low_type)
        query_grad = forward_dot(score_grad, key) * scaling
        key_grad = dot_tn(score_grad, query) * scaling
        for piece, values in enumerate((query_grad, key_grad, value_grad)):
            packed_grad_ref[:, pl.ds(piece * DD + block, LANES)] += jnp.where(inside, values, 0.0)
        return carry

    lax.fori_loop(0, DHEADS, attend_back, 0)
    normed_grad = jnp.zeros((TOKENS, DD), jnp.float32)
    for piece in range(3):
        columns = slice(piece * DD, (piece + 1) * DD)
        packed_low = packed_grad_ref[:, columns].astype(low_type)
        put(normed, pairs_of(packed_low), 3 * DD // LANES, piece * DD // LANES)
        normed_grad = normed_grad + dot_nt(packed_low, packed_w[:, columns])
    flush(starts[0], 3 * DD * DD // LANES)
    token_part, first_terms = norm_backward(normed_grad, first_hat, first_inverse, first_gain)
    token_grad = middle_grad + token_part
    latent_out[...] = dot_tn(select, token_grad.astype(low_type)).astype(low_type)
    for row, terms in enumerate((first_terms, second_terms, last_terms, mask * token_grad)):
        small_out[row : row + 1, :] = jnp.sum(terms, axis=0, keepdims=True)
    send_from(0, starts[0])
    for copy in copies:
        copy.wait()


def decode(core, scale, latent, select, mask, table, small, pixels, weights, slots, slot_rows):
    half = jax.ShapeDtypeStruct((slots // 2, slot_rows, LANES), low_type)
    return pl.pallas_call(
        decoder_kernel,
        in_specs=[pl.BlockSpec(memory_space=pltpu.SMEM)] * 2
        + [pl.BlockSpec(memory_space=pltpu.VMEM)] * 11,
        out_specs=[pl.BlockSpec(memory_space=pl.ANY)] * 2
        + [pl.BlockSpec(memory_space=pltpu.VMEM)] * 3,
        out_shape=(
            half,
            half,
            jax.ShapeDtypeStruct(latent.shape, low_type),
            jax.ShapeDtypeStruct(small.shape, jnp.float32),
            jax.ShapeDtypeStruct((1, 1), jnp.float32),
        ),
        scratch_shapes=[
            pltpu.VMEM((slots * slot_rows, LANES), low_type),
            pltpu.SemaphoreType.DMA((slots,)),
            pltpu.VMEM((DD * DMLP // LANES, LANES), jnp.float32),
            pltpu.VMEM((TOKENS, 3 * DD), low_type),
            pltpu.VMEM((TOKENS, DD), jnp.float32),
            pltpu.VMEM((DHEADS, TOKENS, TOKENS), jnp.float32),
            pltpu.VMEM((TOKENS, DMLP), jnp.float32),
            pltpu.VMEM((TOKENS, DMLP), low_type),
            pltpu.VMEM((TOKENS, 3 * DD), jnp.float32),
        ],
        compiler_params=pltpu.CompilerParams(vmem_limit_bytes=60 * 2**20),
        cost_estimate=pl.CostEstimate(
            flops=6 * TOKENS * slots * slot_rows * LANES,
            bytes_accessed=4 * slots * slot_rows * LANES,
            transcendentals=TOKENS * (DMLP + DHEADS * TOKENS),
        ),
    )(core, scale, latent, select, mask, table, small, pixels, *weights)


def run_kernel(kernel, tokens, arguments, outputs, scratch=(), flops=0):
    count = len(tokens)

    def body(*refs):
        kernel(*refs[count:])

    return pl.pallas_call(
        body,
        in_specs=[pl.BlockSpec(memory_space=pl.ANY)] * count
        + [pl.BlockSpec(memory_space=pltpu.VMEM)] * len(arguments),
        out_specs=[pl.BlockSpec(memory_space=pltpu.VMEM)] * len(outputs),
        out_shape=[jax.ShapeDtypeStruct(shape, kind) for shape, kind in outputs],
        scratch_shapes=list(scratch),
        compiler_params=pltpu.CompilerParams(vmem_limit_bytes=48 * 2**20),
        cost_estimate=pl.CostEstimate(flops=flops, bytes_accessed=2**20, transcendentals=0),
    )(*tokens, *arguments)


def put_terms(terms, outs):
    for place, out in enumerate(outs):
        out[...] = terms[place * VIS : (place + 1) * VIS].astype(out.dtype)


def term_outputs(groups):
    return [((VIS, D), jnp.float32)] + [((VIS, D), low_type)] * (groups - 1)


def sum_terms(refs):
    total = refs[0][...]
    for ref in refs[1:]:
        total = total + ref[...].astype(jnp.float32)
    return total


def join(refs):
    return jnp.concatenate([ref[...] for ref in refs], 0)


def exchange(terms):
    return [terms[0]] + [swap(terms[step], "mp", step) for step in range(1, len(terms))]


def spread(values):
    groups = lax.axis_size("mp")
    return [values] + [swap(values, "mp", step) for step in range(1, groups)]


def head_lanes(rows, columns):
    return lax.broadcasted_iota(jnp.int32, (rows, columns), 1) // (D // HEADS)


def enter_encoder(seen, patch_w, table, gain, packed_w, out_w, valid):
    groups = lax.axis_size("mp")
    rows, columns = groups * VIS, D // groups
    heads = HEADS // groups
    scaling = (D // HEADS) ** (-0.5)

    def kernel(seen, patch_w, table, gain, packed_w, out_w, valid, *outs):
        residual_out, hat_out, inverse_out, normed_out, packed_out, prob_out, mixed_out = outs[:7]
        residual = forward_dot(seen[...], patch_w[...]) + table[...]
        norm, hat, inverse = norm_forward(residual, gain[...])
        residual_out[...] = residual[:VIS]
        hat_out[...] = hat[:VIS]
        inverse_out[...] = jnp.broadcast_to(inverse[:VIS], (VIS, LANES))
        normed = norm.astype(low_type)
        normed_out[...] = normed
        packed = forward_dot(normed, packed_w[...]).astype(low_type)
        packed_out[...] = packed
        query, key, value = [packed[:, third * columns : (third + 1) * columns] for third in range(3)]
        one = lax.broadcasted_iota(jnp.int32, (rows, rows), 0) // VIS
        other = lax.broadcasted_iota(jnp.int32, (rows, rows), 1) // VIS
        allowed = (one == other) & (valid[...] > 0.5)
        lanes = head_lanes(rows, columns)
        mixed = jnp.zeros((rows, columns), jnp.float32)
        for head in range(heads):
            inside = lanes == head
            scores = dot_nt(jnp.where(inside, query, 0), key) * scaling
            scores = jnp.where(allowed, scores, -1e30)
            exponent = jnp.exp(scores - jnp.max(scores, -1, keepdims=True))
            probability = exponent / jnp.sum(exponent, -1, keepdims=True)
            prob_out[head] = probability
            mixed = mixed + jnp.where(inside, forward_dot(probability.astype(low_type), value), 0.0)
        mixed_low = mixed.astype(low_type)
        mixed_out[...] = mixed_low
        put_terms(forward_dot(mixed_low, out_w[...]), outs[7:])

    outputs = [
        ((VIS, D), jnp.float32),
        ((VIS, D), jnp.float32),
        ((VIS, LANES), jnp.float32),
        ((rows, D), low_type),
        ((rows, 3 * columns), low_type),
        ((heads, rows, rows), jnp.float32),
        ((rows, columns), low_type),
    ] + term_outputs(groups)
    results = run_kernel(
        kernel, [], [seen, patch_w, table, gain, packed_w, out_w, valid], outputs, flops=10**9
    )
    return results[:7], results[7:]


def norm_of_sum(terms, residual, gain):
    count = len(terms)

    def kernel(*refs):
        residual, gain = refs[count : count + 2]
        sum_out, low_out, hat_out, inverse_out = refs[count + 2 :]
        total = residual[...] + sum_terms(refs[:count])
        norm, hat, inverse = norm_forward(total, gain[...])
        sum_out[...] = total
        low_out[...] = norm.astype(low_type)
        hat_out[...] = hat
        inverse_out[...] = jnp.broadcast_to(inverse, (VIS, LANES))

    outputs = [
        ((VIS, D), jnp.float32),
        ((VIS, D), low_type),
        ((VIS, D), jnp.float32),
        ((VIS, LANES), jnp.float32),
    ]
    return run_kernel(kernel, [], [*terms, residual, gain], outputs)


def raise_and_lower(inner, up_w, down_w):
    groups = len(inner)
    rows, columns = groups * VIS, MLP // groups

    def kernel(*refs):
        up_w, down_w, activated_out, slope_out = refs[groups : groups + 4]
        activated, slope = gelu_pair(forward_dot(join(refs[:groups]), up_w[...]))
        slope_out[...] = slope
        activated = activated.astype(low_type)
        activated_out[...] = activated
        put_terms(forward_dot(activated, down_w[...]), refs[groups + 4 :])

    outputs = [((rows, columns), low_type), ((rows, columns), jnp.float32)] + term_outputs(groups)
    results = run_kernel(kernel, [], [*inner, up_w, down_w], outputs, flops=6 * 10**8)
    return results[:2], results[2:]


def latent_of_sum(tokens, terms, residual, gain, latent_w):
    count = len(terms)

    def kernel(*refs):
        residual, gain, latent_w, low_out, hat_out, inverse_out, latent_out = refs[count:]
        norm, hat, inverse = norm_forward(residual[...] + sum_terms(refs[:count]), gain[...])
        final_low = norm.astype(low_type)
        low_out[...] = final_low
        hat_out[...] = hat
        inverse_out[...] = jnp.broadcast_to(inverse, (VIS, LANES))
        columns = latent_w.shape[2]
        for place in range(count):
            latent_out[:, place * columns : (place + 1) * columns] = forward_dot(
                final_low, latent_w[place]
            ).astype(low_type)

    outputs = [
        ((VIS, D), low_type),
        ((VIS, D), jnp.float32),
        ((VIS, LANES), jnp.float32),
        ((VIS, DD), low_type),
    ]
    return run_kernel(kernel, tokens, [*terms, residual, gain, latent_w], outputs)


def latent_back(latent_grad, latent_w, hat, inverse, gain):
    def kernel(latent_grad, latent_w, hat, inverse, gain, grad_out, low_out, gain_out):
        columns = latent_w.shape[2]
        total = jnp.zeros((VIS, D), jnp.float32)
        for place in range(latent_w.shape[0]):
            total = total + dot_nt(
                latent_grad[:, place * columns : (place + 1) * columns], latent_w[place]
            )
        gradient, terms = norm_backward(total, hat[...], inverse[:, :1], gain[...])
        grad_out[...] = gradient
        low_out[...] = gradient.astype(low_type)
        gain_out[...] = jnp.sum(terms, axis=0, keepdims=True)

    outputs = [((VIS, D), jnp.float32), ((VIS, D), low_type), ((1, D), jnp.float32)]
    return run_kernel(kernel, [], [latent_grad, latent_w, hat, inverse, gain], outputs)


def norm_back_of_sum(tokens, terms, upstream, hat, inverse, gain):
    count = len(terms)

    def kernel(*refs):
        upstream, hat, inverse, gain, grad_out, low_out, gain_out = refs[count:]
        part, gain_terms = norm_backward(
            sum_terms(refs[:count]), hat[...], inverse[:, :1], gain[...]
        )
        gradient = upstream[...] + part
        grad_out[...] = gradient
        low_out[...] = gradient.astype(low_type)
        gain_out[...] = jnp.sum(gain_terms, axis=0, keepdims=True)

    outputs = [((VIS, D), jnp.float32), ((VIS, D), low_type), ((1, D), jnp.float32)]
    return run_kernel(kernel, tokens, [*terms, upstream, hat, inverse, gain], outputs)


def mlp_back(tokens, grad_low, inner, activated, slope, up_w, down_w):
    groups = len(grad_low)

    def kernel(*refs):
        activated, slope, up_w, down_w, up_out, down_out = refs[2 * groups : 2 * groups + 6]
        grad_low = join(refs[:groups])
        raised_grad = (dot_nt(grad_low, down_w[...]) * slope[...]).astype(low_type)
        put_terms(dot_nt(raised_grad, up_w[...]), refs[2 * groups + 6 :])
        down_out[...] = dot_tn(activated[...], grad_low).astype(low_type)
        up_out[...] = dot_tn(join(refs[groups : 2 * groups]), raised_grad).astype(low_type)

    outputs = [(up_w.shape, low_type), (down_w.shape, low_type)] + term_outputs(groups)
    results = run_kernel(
        kernel,
        tokens,
        [*grad_low, *inner, activated, slope, up_w, down_w],
        outputs,
        flops=12 * 10**8,
    )
    return results[:2], results[2:]


def attend_back(tokens, grad_low, normed, packed, prob, mixed, packed_w, out_w):
    groups = len(grad_low)
    rows, columns = groups * VIS, D // groups
    heads = HEADS // groups
    scaling = (D // HEADS) ** (-0.5)

    def kernel(*refs):
        normed, packed, prob, mixed, packed_w, out_w, packed_out, out_out = refs[
            groups : groups + 8
        ]
        grad_low = join(refs[:groups])
        mixed_grad = dot_nt(grad_low, out_w[...]).astype(low_type)
        query, key, value = [packed[:, third * columns : (third + 1) * columns] for third in range(3)]
        lanes = head_lanes(rows, columns)
        totals = [jnp.zeros((rows, columns), jnp.float32)] * 3
        for head in range(heads):
            inside = lanes == head
            probability = prob[head]
            value_grad = dot_tn(probability.astype(low_type), mixed_grad)
            prob_grad = dot_nt(jnp.where(inside, mixed_grad, 0), value)
            score_grad = (
                probability * (prob_grad - jnp.sum(probability * prob_grad, -1, keepdims=True))
            ).astype(low_type)
            query_grad = forward_dot(score_grad, key) * scaling
            key_grad = dot_tn(score_grad, query) * scaling
            totals = [
                total + jnp.where(inside, values, 0.0)
                for total, values in zip(totals, (query_grad, key_grad, value_grad))
            ]
        packed_grad = jnp.concatenate(totals, 1).astype(low_type)
        put_terms(dot_nt(packed_grad, packed_w[...]), refs[groups + 8 :])
        out_out[...] = dot_tn(mixed[...], grad_low).astype(low_type)
        packed_out[...] = dot_tn(normed[...], packed_grad).astype(low_type)

    outputs = [(packed_w.shape, low_type), (out_w.shape, low_type)] + term_outputs(groups)
    results = run_kernel(
        kernel,
        tokens,
        [*grad_low, normed, packed, prob, mixed, packed_w, out_w],
        outputs,
        flops=10**9,
    )
    return results[:2], results[2:]


def on_device(
    pixels,
    visible,
    block_master,
    block_first,
    block_second,
    shared_master,
    shared_first,
    shared_second,
    gains_master,
    gains_first,
    gains_second,
):
    groups = lax.axis_size("mp")
    replicas = lax.axis_size("dp")
    member = lax.axis_index("mp")
    model_cols = D // groups
    mlp_cols = MLP // groups
    embed_cols = DD // groups
    block_rows = block_master.shape[1] // D
    shared_rows = shared_master.shape[0] // 128

    own_pixels = pick(pixels, member, 0)
    own_visible = pick(visible, member, 0)
    hidden_mask = (1 - own_visible).astype(jnp.float32)
    hidden_count = jnp.sum(1 - own_visible).astype(jnp.float32)

    block_lanes = block_master.reshape(-1, 128)
    shared_lanes = shared_master.reshape(-1, 128)
    block_rowed, shared_low, shared_rowed = low_rows(block_lanes, shared_lanes, D)
    shared_flat = lax.all_gather(shared_low, ("dp", "mp"), axis=0).reshape(-1, 128)

    patch_size = PIX * D
    head_rows = shared_master.shape[0] // D
    tail_length = patch_size - groups * head_rows * D
    early = 0 < tail_length <= shared_master.shape[0] and groups * head_rows < PIX
    small_length = gains_master.shape[0]
    small_row = jnp.concatenate([lax.reduce_precision(gains_master, 8, 7), hidden_count[None]])
    small_row = jnp.pad(small_row, (0, -small_row.shape[0] % 128))
    near_visible = reorder(visible, member)
    near_pixels = reorder(pixels, member)
    select, slot_patch, key_valid = visible_slots(near_visible)
    chosen = (slot_patch[:, :, None] == jnp.arange(PATCHES)[None, None, :]).astype(low_type)
    seen_patches = jnp.einsum(
        "isp,ipd->isd", chosen, near_pixels, preferred_element_type=jnp.float32
    ).astype(low_type)
    small_table, block_flat = gather_early(small_row, block_rowed)
    gain_flat = small_table[:, :small_length].reshape(-1)
    count_total = jnp.sum(small_table[:, small_length])

    bounds = [0, 3 * model_cols, model_cols, mlp_cols, mlp_cols, embed_cols]
    bounds = [sum(bounds[: place + 1]) for place in range(len(bounds))]
    enc_packed, enc_out, enc_up, enc_down, enc_latent = [
        block_flat[low:high] for low, high in zip(bounds[:-1], bounds[1:])
    ]
    enc_packed = enc_packed.reshape(D, 3 * model_cols)
    enc_up = enc_up.reshape(D, mlp_cols)
    own_latent_w = enc_latent.reshape(D, embed_cols)

    (patch_w,) = unpack(shared_flat, 0, [(PIX, D)])
    dec_weights = unpack(
        shared_flat, PIX * D, [(DD, 3 * DD), (DD, DD), (DD, DMLP), (DMLP, DD), (DD, PIX)]
    )
    enc_one, enc_two, enc_last, dec_one, dec_two, dec_last, mask_token = cut_pieces(
        gain_flat, [(D,), (D,), (D,), (DD,), (DD,), (DD,), (DD,)]
    )

    latent_w = reorder(share(own_latent_w), member)
    saved, terms = enter_encoder(
        seen_patches.reshape(-1, PIX),
        patch_w,
        position_table(slot_patch, D).reshape(-1, D),
        enc_one[None],
        enc_packed,
        enc_out,
        key_valid.astype(jnp.float32).reshape(1, -1),
    )
    residual, first_hat, first_inverse, normed, packed, prob, mixed_heads = saved
    middle, inner_low, second_hat, second_inverse = norm_of_sum(
        exchange(terms), residual, enc_two[None]
    )
    inner_low = spread(inner_low)
    (activated, slope), terms = raise_and_lower(inner_low, enc_up, enc_down)
    final_low, final_hat, final_inverse, latent = latent_of_sum(
        [], exchange(terms), middle, enc_last[None], latent_w
    )
    final_all = share(final_low)

    pad = ((0, TOKENS - PATCHES), (0, 0))
    place = lax.axis_index("dp")
    sent_grad, kept_grad, latent_grad, dec_small, loss_local = decode(
        (place & 1).reshape(1, 1),
        (2.0 / (PIX * count_total)).reshape(1, 1),
        latent,
        jnp.pad(select[0].T.astype(low_type), pad),
        jnp.pad(hidden_mask[:, None], pad),
        jnp.pad(position_table(jnp.arange(PATCHES), DD), pad),
        jnp.pad(jnp.stack([dec_one, dec_two, dec_last, mask_token]), ((0, 4), (0, 0))),
        jnp.pad(own_pixels, pad),
        dec_weights,
        replicas,
        groups * shared_rows,
    )
    loss_local = loss_local[0, 0]
    column_share, stages = reduce_chips(kept_grad, swap(sent_grad, "dp", 1))
    shared_share, column_sent = reduce_mp(column_share.reshape(groups, shared_rows, 128))

    encoded_grad, encoded_low, enc_last_grad = latent_back(
        latent_grad, latent_w, final_hat, final_inverse, enc_last[None]
    )
    encoded_low = spread(encoded_low)
    latent_cut = latent_grad.reshape(VIS, groups, embed_cols)
    latent_near = jnp.stack(
        [pick(latent_cut, member, 1)]
        + [swap(pick(latent_cut, member ^ step, 1), "mp", step) for step in range(1, groups)]
    )
    latent_wgrad = outer_sum(final_all, latent_near)
    (up_grad, down_grad), terms = mlp_back(
        [], encoded_low, inner_low, activated, slope, enc_up, enc_down
    )
    middle_grad, middle_low, enc_two_grad = norm_back_of_sum(
        stages[0], exchange(terms), encoded_grad, second_hat, second_inverse, enc_two[None]
    )
    (packed_grad, out_grad), terms = attend_back(
        stages[-1], spread(middle_low), normed, packed, prob, mixed_heads, enc_packed, enc_out
    )
    block_grad = jnp.concatenate(
        [
            piece.astype(low_type).reshape(-1, D)
            for piece in (packed_grad, out_grad, up_grad, down_grad, latent_wgrad)
        ]
    ).reshape(replicas, block_rows, D)
    block_share, block_stages = reduce_dp(block_grad)
    residual_grad, residual_low, enc_one_grad = norm_back_of_sum(
        block_stages[0], exchange(terms), middle_grad, first_hat, first_inverse, enc_one[None]
    )

    if early:
        residual_all = after_all(share(residual_low), block_stages[-1])
        enc_one_grad = after(enc_one_grad, residual_all)
        rows = return_patch(outer_sum(seen_patches, residual_all), head_rows)
        owner = (place == 0) | ((place == 1) & (member == 0))
        shared_share = shared_share + jnp.where(owner, rows.reshape(-1, 128), 0.0)
    else:
        patch_rows = outer_sum(seen_patches[0], residual_low).astype(low_type).reshape(-1, 128)
        patch_rows = jnp.pad(patch_rows, ((0, shared_flat.shape[0] - patch_rows.shape[0]), (0, 0)))
        column = reduce_dp(patch_rows.reshape(replicas, groups * shared_rows, 128))[0]
        shared_share = shared_share + reduce_mp(column.reshape(groups, shared_rows, 128))[0]
    pad_length = gain_flat.shape[0] - 3 * D - 4 * DD
    gain_grad = jnp.concatenate(
        [
            enc_one_grad[0],
            enc_two_grad[0],
            enc_last_grad[0],
            dec_small[:4].reshape(-1),
            jnp.zeros((pad_length,), jnp.float32),
        ]
    )
    gain_total = sum_small(gain_grad.reshape(-1, 128))
    own = lax.axis_index("dp") * groups + member
    gain_share = lax.dynamic_slice_in_dim(gain_total.reshape(-1), own * small_length, small_length)
    squares = (
        jnp.sum(block_share * block_share)
        + jnp.sum(shared_share * shared_share)
        + jnp.sum(gain_share * gain_share)
    )
    sums = sum_small(jnp.stack([squares, loss_local]).reshape(1, 2))
    square_total, loss_total = sums[0, 0], sums[0, 1]
    grad_norm = jnp.sqrt(square_total)
    factor = jnp.minimum(1.0, clip_norm / (grad_norm + 1e-06))
    block_out, shared_out = update(
        factor,
        block_share,
        [block_first.reshape(-1, 128), block_second.reshape(-1, 128), block_lanes],
        shared_share,
        [shared_first.reshape(-1, 128), shared_second.reshape(-1, 128), shared_lanes],
    )
    block_out = tuple(piece.reshape(block_master.shape) for piece in block_out)
    shared_out = tuple(piece.reshape(-1) for piece in shared_out)
    gain_out = adamw(gain_share, gains_first, gains_second, gains_master, factor, rate_gains, 0.0)
    return (grad_norm, loss_total, count_total) + block_out + shared_out + gain_out


def solution(mesh):
    return jax.shard_map(
        on_device,
        mesh=mesh,
        in_specs=(
            P("dp", None, None),
            P("dp", None),
            P("mp", "dp"),
            P("mp", "dp"),
            P("mp", "dp"),
            P(("dp", "mp")),
            P(("dp", "mp")),
            P(("dp", "mp")),
            P(("dp", "mp")),
            P(("dp", "mp")),
            P(("dp", "mp")),
        ),
        out_specs=(
            P(),
            P(),
            P(),
            P("mp", "dp"),
            P("mp", "dp"),
            P("mp", "dp"),
            P("mp", "dp"),
            P(("dp", "mp")),
            P(("dp", "mp")),
            P(("dp", "mp")),
            P(("dp", "mp")),
            P(("dp", "mp")),
            P(("dp", "mp")),
            P(("dp", "mp")),
            P(("dp", "mp")),
        ),
        check_vma=False,
    )
```

```python
from functools import partial
import math

import jax
import jax.numpy as jnp
from jax import lax
from jax.experimental import pallas as pl
from jax.experimental.pallas import tpu as pltpu
from jax.sharding import PartitionSpec as P

D = 768
HEADS = 12
MLP = 3072
DD = 512
DHEADS = 16
DMLP = 2048
PIX = 768
PATCHES = 196
VIS = 64
STEP = 10


low_type = jnp.bfloat16
clip_norm = 0.0002
beta_one = 0.9
beta_two = 0.95
adam_eps = 1e-10
rate_matrix = 0.03
rate_gains = 0.7
weight_decay = 0.1


def forward_dot(left_side, right_side):
    return jnp.dot(left_side, right_side, preferred_element_type=jnp.float32)


def back_dot(left_side, right_side):
    return lax.dot_general(
        left_side,
        right_side,
        (((left_side.ndim - 1,), (1,)), ((), ())),
        preferred_element_type=jnp.float32,
    )


def outer_sum(left_side, right_side):
    left_rows = left_side.reshape(-1, left_side.shape[-1])
    right_rows = right_side.reshape(-1, right_side.shape[-1])
    return lax.dot_general(
        left_rows, right_rows, (((0,), (0,)), ((), ())), preferred_element_type=jnp.float32
    )


def swap(values, axis_name, distance):
    count = lax.axis_size(axis_name)
    return lax.ppermute(values, axis_name, [(place, place ^ distance) for place in range(count)])


def share(values):
    groups = lax.axis_size("mp")
    return jnp.stack([values] + [swap(values, "mp", step) for step in range(1, groups)])


def pick(values, index, dim):
    return lax.dynamic_index_in_dim(values, index, dim, keepdims=False)


def reorder(values, place):
    return jnp.stack([pick(values, place ^ step, 0) for step in range(values.shape[0])])


def bits_of(count):
    return count.bit_length() - 1


def after(values, token):
    first = token[(0,) * token.ndim].astype(jnp.float32)
    return values + jnp.minimum(jnp.abs(first), 0.0).astype(values.dtype)


def after_all(values, tokens):
    for token in tokens:
        values = after(values, token)
    return values


def half_cut(values, side, dim):
    return (pick(values, side, dim), pick(values, 1 - side, dim))


def bit_orders():
    higher = tuple(range(3, bits_of(lax.axis_size("dp"))))
    return ((1, 2) + higher, (2, 1) + higher)


def first_stage(kept_whole, got_whole):
    width = bits_of(lax.axis_size("dp"))
    place = lax.axis_index("dp")
    rows = kept_whole.shape[1]
    split = (2,) * (width - 1) + kept_whole.shape[1:]
    both = [piece.reshape(split) for piece in (kept_whole, got_whole)]
    totals, sents = [], []
    for (first, last), order in zip(((0, rows // 2), (rows // 2, rows)), bit_orders()):
        dim = width - 1 - order[0]
        side = (place >> order[0]) & 1

        def part_of(values, where, dim=dim, first=first, last=last):
            starts = [0] * values.ndim
            sizes = list(values.shape)
            starts[dim], sizes[dim] = where, 1
            starts[width - 1], sizes[width - 1] = first, last - first
            cut = lax.dynamic_slice(values, starts, sizes)
            return cut.reshape(sizes[:dim] + sizes[dim + 1 :]).astype(jnp.float32)

        kept, sent = [sum(part_of(piece, where) for piece in both) for where in (side, 1 - side)]
        sent = sent.astype(low_type)
        sents.append(sent)
        totals.append(kept + swap(sent, "dp", 1 << order[0]).astype(jnp.float32))
    return totals, sents


def later_stages(totals, tokens=()):
    width = bits_of(lax.axis_size("dp"))
    place = lax.axis_index("dp")
    halves, sents = [], []
    for total, order in zip(totals, bit_orders()):
        total = after_all(total, tokens)
        left = [bit for bit in range(width - 1, 0, -1) if bit != order[0]]
        for bit in order[1:]:
            kept, sent = half_cut(total, (place >> bit) & 1, left.index(bit))
            sent = sent.astype(low_type)
            total = kept + swap(sent, "dp", 1 << bit).astype(jnp.float32)
            left.remove(bit)
        sents.append(sent)
        halves.append(total)
    return halves, sents


def reduce_dp(values):
    place = lax.axis_index("dp")
    shaped = values.reshape((-1, 2) + values.shape[1:])
    kept, sent = half_cut(shaped, place & 1, 1)
    totals, sents = first_stage(kept, swap(sent, "dp", 1))
    return jnp.concatenate(later_stages(totals)[0], 0)


def to_members(values):
    return lax.all_to_all(values, "mp", 0, 0, tiled=True)


def sum_chips(row):
    width = bits_of(lax.axis_size("dp"))
    if width == 3:
        place = lax.axis_index("dp") >> 1
        rows = jnp.stack([row] + [swap(row, "dp", 2 * step) for step in range(1, 4)])
        return jnp.sum(reorder(rows, place), 0)
    for bit in range(1, width):
        row = row + swap(row, "dp", 1 << bit)
    return row


def sum_small(row):
    row = sum_chips(row + swap(row, "dp", 1))
    return jnp.sum(reorder(share(row), lax.axis_index("mp")), 0)


def pair_permute(values, pairs):
    return lax.ppermute(values, ("dp", "mp"), pairs)


def gather_early(small_row, block_rows):
    replicas = lax.axis_size("dp")
    place = lax.axis_index("dp")
    member = lax.axis_index("mp")
    width = bits_of(replicas)
    higher = tuple(range(3, width))
    orders = ((1, 2) + higher, (2, 1) + higher)
    half_rows = block_rows.shape[0] // 2
    halves = [block_rows[None, :half_rows], block_rows[None, half_rows:]]
    table = reorder(share(small_row), member)[None]
    for level in range(width - 1):
        halves = [
            jnp.concatenate([half, swap(half, "dp", 1 << order[level])], 0)
            for half, order in zip(halves, orders)
        ]
    placed = []
    for half, order in zip(halves, orders):
        shaped = half.reshape((2,) * (width - 1) + half.shape[1:])
        dims = [width - 2 - order.index(bit) for bit in range(width - 1, 0, -1)]
        placed.append(shaped.transpose(dims + [width - 1, width]).reshape(half.shape))
    near = jnp.concatenate(placed, 1)
    both = jnp.stack([near, swap(near, "dp", 1)], 1).reshape((replicas,) + block_rows.shape)
    block_flat = reorder(both, place).reshape(-1, block_rows.shape[1])
    for bit in range(width):
        table = jnp.concatenate([table, swap(table, "dp", 1 << bit)], 0)
    return reorder(table, place).reshape(-1, small_row.shape[0]), block_flat


def position_table(places, row_width):
    column = jnp.arange(row_width)
    step_rate = jnp.exp(-(column // 2 * 2).astype(jnp.float32) * (math.log(10000.0) / row_width))
    angle = places.astype(jnp.float32)[..., None] * step_rate
    return jnp.where(column % 2 == 0, jnp.sin(angle), jnp.cos(angle))


def visible_slots(visible):
    slot_rank = jnp.cumsum(visible, 1) - 1
    select = (
        (visible[:, None, :] == 1) & (slot_rank[:, None, :] == jnp.arange(VIS)[None, :, None])
    ).astype(jnp.int32)
    slot_patch = jnp.sum(select * jnp.arange(visible.shape[1])[None, None, :], 2)
    key_valid = jnp.arange(VIS)[None, :] < jnp.sum(visible, 1)[:, None]
    return (select, slot_patch, key_valid)


def cut_pieces(flat_vector, shapes):
    pieces = []
    offset = 0
    for shape in shapes:
        length = math.prod(shape)
        pieces.append(flat_vector[offset : offset + length].reshape(shape))
        offset += length
    return pieces


def norm_forward(residual, gain_vec):
    center = residual - jnp.mean(residual, -1, keepdims=True)
    inverse = lax.rsqrt(jnp.mean(center * center, -1, keepdims=True) + 1e-06)
    normal_hat = center * inverse
    return (normal_hat * gain_vec, normal_hat, inverse)


def norm_backward(gradient, normal_hat, inverse, gain_vec):
    hat_grad = gradient * gain_vec
    residual_grad = inverse * (
        hat_grad
        - jnp.mean(hat_grad, -1, keepdims=True)
        - normal_hat * jnp.mean(hat_grad * normal_hat, -1, keepdims=True)
    )
    return (residual_grad, gradient * normal_hat)


def split_heads(packed, head_count):
    batch_size, length, row_width = packed.shape
    unpacked = packed.reshape(batch_size, length, 3, head_count, row_width // (3 * head_count))
    return (unpacked[:, :, 0], unpacked[:, :, 1], unpacked[:, :, 2])


def scores_of(query_part, key_part, key_valid, scaling):
    raw_scores = (
        jnp.einsum("blhd,bmhd->bhlm", query_part, key_part, preferred_element_type=jnp.float32)
        * scaling
    )
    return jnp.where(key_valid[:, None, None, :], raw_scores, -1e30)


def attend_forward(packed, key_valid, head_count, scaling):
    query_part, key_part, value_part = split_heads(packed, head_count)
    scores = scores_of(query_part, key_part, key_valid, scaling)
    row_top = jnp.max(scores, -1, keepdims=True)
    exponent = jnp.exp(scores - row_top)
    row_total = jnp.sum(exponent, -1, keepdims=True)
    probability = (exponent / row_total).astype(low_type)
    mixed_heads = jnp.einsum(
        "bhlm,bmhd->blhd", probability, value_part, preferred_element_type=jnp.float32
    )
    batch_size, length = (key_valid.shape[0], packed.shape[1])
    return (
        mixed_heads.reshape(batch_size, length, -1).astype(low_type),
        row_top + jnp.log(row_total),
    )


def attend_backward(packed, log_total, key_valid, mixed_grad, head_count, scaling):
    query_part, key_part, value_part = split_heads(packed, head_count)
    batch_size, length, row_width = mixed_grad.shape
    out_grad = mixed_grad.reshape(batch_size, length, head_count, -1)
    probability = jnp.exp(scores_of(query_part, key_part, key_valid, scaling) - log_total)
    value_grad = jnp.einsum(
        "bhlm,blhd->bmhd",
        probability.astype(low_type),
        out_grad,
        preferred_element_type=jnp.float32,
    )
    prob_grad = jnp.einsum(
        "blhd,bmhd->bhlm", out_grad, value_part, preferred_element_type=jnp.float32
    )
    score_grad = (
        probability * (prob_grad - jnp.sum(probability * prob_grad, -1, keepdims=True))
    ).astype(low_type)
    query_grad = (
        jnp.einsum("bhlm,bmhd->blhd", score_grad, key_part, preferred_element_type=jnp.float32)
        * scaling
    )
    key_grad = (
        jnp.einsum("bhlm,blhd->bmhd", score_grad, query_part, preferred_element_type=jnp.float32)
        * scaling
    )
    stacked = jnp.stack([query_grad, key_grad, value_grad], 2)
    return stacked.reshape(batch_size, length, -1).astype(low_type)


def cut_rows(rows, shapes):
    pieces = []
    offset = 0
    for shape in shapes:
        length = math.prod(shape) // 128
        pieces.append(rows[offset : offset + length].reshape(shape))
        offset += length
    return pieces


def mlp_backward(
    gradient, grad_low, activated, raised, inner_low, up_w, down_w, total_sum, norm_saved
):
    down_grad = outer_sum(activated, grad_low)
    act_grad = back_dot(grad_low, down_w)
    unused, gelu_back = jax.vjp(partial(jax.nn.gelu, approximate=True), raised)
    raised_grad = gelu_back(act_grad)[0].astype(low_type)
    up_grad = outer_sum(inner_low, raised_grad)
    inner_grad = total_sum(back_dot(raised_grad, up_w))
    normal_hat, inverse, gain_vec = norm_saved
    middle_part, second_terms = norm_backward(inner_grad, normal_hat, inverse, gain_vec)
    return (gradient + middle_part, down_grad, up_grad, second_terms)


def adamw(gradient, first_old, second_old, master, factor, step_rate, decay_rate):
    gradient = gradient * factor
    first_new = beta_one * first_old + (1 - beta_one) * gradient
    second_new = beta_two * second_old + (1 - beta_two) * gradient * gradient
    first_hat = first_new / (1 - beta_one**STEP)
    second_hat = second_new / (1 - beta_two**STEP)
    master_new = master - step_rate * (
        first_hat / (jnp.sqrt(second_hat) + adam_eps) + decay_rate * master
    )
    return (first_new, second_new, master_new, master_new.astype(jnp.bfloat16))


def low_rows(block_lanes, shared_lanes, row_width):
    pieces = row_width // 128

    def kernel(block_ref, shared_ref, block_out, shared_out, rows_out):
        for source, target in ((block_ref, block_out), (shared_ref, rows_out)):
            rows = target.shape[0]
            for piece in range(pieces):
                lanes = slice(piece * 128, (piece + 1) * 128)
                target[:, lanes] = source[pl.ds(piece, rows, stride=pieces), :].astype(low_type)
        shared_out[...] = shared_ref[...].astype(low_type)

    return pl.pallas_call(
        kernel,
        out_shape=(
            jax.ShapeDtypeStruct((block_lanes.shape[0] // pieces, row_width), low_type),
            jax.ShapeDtypeStruct(shared_lanes.shape, low_type),
            jax.ShapeDtypeStruct((shared_lanes.shape[0] // pieces, row_width), low_type),
        ),
        compiler_params=pltpu.CompilerParams(vmem_limit_bytes=8 * 2**20),
    )(block_lanes, shared_lanes)


def adamw_of(gradient, first_old, second_old, master, step_rate, decay_rate):
    first_new = beta_one * first_old + (1 - beta_one) * gradient
    second_new = beta_two * second_old + (1 - beta_two) * gradient * gradient
    first_hat = first_new / (1 - beta_one**STEP)
    second_hat = second_new / (1 - beta_two**STEP)
    master_new = master - step_rate * (
        first_hat / (jnp.sqrt(second_hat) + adam_eps) + decay_rate * master
    )
    return (first_new, second_new, master_new, master_new.astype(low_type))


def update(factor, block_rows, block_state, shared_lanes, shared_state):
    pieces = block_rows.shape[1] // 128

    def kernel(factor_ref, *refs):
        block_grad, shared_grad = refs[0], refs[4]
        scale = factor_ref[0, 0]
        rows = block_grad.shape[0]
        block_in, block_to = refs[1:4], refs[8:12]
        shared_in, shared_to = refs[5:8], refs[12:16]
        for piece in range(pieces):
            spots = pl.ds(piece, rows, stride=pieces)
            gradient = block_grad[:, piece * 128 : (piece + 1) * 128] * scale
            results = adamw_of(
                gradient, *[ref[spots, :] for ref in block_in], rate_matrix, weight_decay
            )
            for ref, result in zip(block_to[:3], results[:3]):
                ref[spots, :] = result
        block_to[3][...] = block_to[2][...].astype(low_type).reshape(block_to[3].shape)
        results = adamw_of(
            shared_grad[...] * scale, *[ref[...] for ref in shared_in], rate_matrix, weight_decay
        )
        for ref, result in zip(shared_to, results):
            ref[...] = result

    kinds = (jnp.float32, jnp.float32, jnp.float32, low_type)
    shapes = [block_state[0].shape] * 4 + [shared_state[0].shape] * 4
    shapes[3] = (1, math.prod(shapes[3]))
    results = pl.pallas_call(
        kernel,
        in_specs=[pl.BlockSpec(memory_space=pltpu.SMEM)]
        + [pl.BlockSpec(memory_space=pltpu.VMEM)] * 8,
        out_shape=[jax.ShapeDtypeStruct(shape, kind) for shape, kind in zip(shapes, kinds * 2)],
        compiler_params=pltpu.CompilerParams(vmem_limit_bytes=20 * 2**20),
    )(factor.reshape(1, 1), block_rows, *block_state, shared_lanes, *shared_state)
    return (tuple(results[:4]), tuple(results[4:]))


TOKENS = 208
LANES = 128


def dot_tn(left_side, right_side):
    return lax.dot_general(
        left_side, right_side, (((0,), (0,)), ((), ())), preferred_element_type=jnp.float32
    )


def dot_nt(left_side, right_side):
    return lax.dot_general(
        left_side, right_side, (((1,), (1,)), ((), ())), preferred_element_type=jnp.float32
    )


def gelu_pair(raised):
    rate = math.sqrt(2.0 / math.pi)
    square = raised * raised
    curve = jnp.tanh(rate * (raised + 0.044715 * raised * square))
    half = 0.5 * (1.0 + curve)
    slope = half + 0.5 * raised * (1.0 - curve * curve) * rate * (1.0 + 0.134145 * square)
    return raised * half, slope


def unpack(lanes, first_entry, shapes):
    step = 64

    def kernel(lanes_ref, *refs):
        work = refs[-1]
        start = first_entry // LANES
        for out in refs[:-1]:
            depth, pieces = out.shape[0], out.shape[1] // LANES
            span = step * pieces

            def chunk(index, carry, out=out, start=start, pieces=pieces, span=span):
                source = pl.ds(pl.multiple_of(start + index * span, 64), span)
                work[:span, :] = lanes_ref[source, :].astype(jnp.float32)
                rows = pl.ds(pl.multiple_of(index * step, step), step)
                for piece in range(pieces):
                    out[rows, piece * LANES : (piece + 1) * LANES] = work[
                        pl.ds(piece, step, stride=pieces), :
                    ].astype(low_type)
                return carry

            lax.fori_loop(0, depth // step, chunk, 0)
            start += depth * pieces

    entries = sum(math.prod(shape) for shape in shapes)
    widest = max(shape[1] for shape in shapes)
    block = first_entry // LANES + entries // LANES
    return pl.pallas_call(
        kernel,
        grid=(1,),
        in_specs=[pl.BlockSpec((block, LANES), lambda index: (0, 0))],
        out_specs=[pl.BlockSpec(shape, lambda index: (0, 0)) for shape in shapes],
        out_shape=[jax.ShapeDtypeStruct(shape, low_type) for shape in shapes],
        scratch_shapes=[pltpu.VMEM((step * widest // LANES, LANES), jnp.float32)],
        compiler_params=pltpu.CompilerParams(vmem_limit_bytes=36 * 2**20),
        cost_estimate=pl.CostEstimate(flops=0, bytes_accessed=4 * entries, transcendentals=0),
    )(lanes)


def decoder_kernel(
    latent_rows,
    core_ref,
    scale_ref,
    final_ref,
    latent_ref,
    select_ref,
    mask_ref,
    table_ref,
    small_ref,
    pixels_ref,
    packed_w,
    out_w,
    up_w,
    down_w,
    head_w,
    sent_out,
    kept_out,
    latent_out,
    small_out,
    loss_out,
    grad_ref,
    copy_sems,
    work,
    packed_ref,
    mixed_ref,
    prob_ref,
    raised_ref,
    activated_ref,
    packed_grad_ref,
):
    scaling = (DD // DHEADS) ** (-0.5)
    width = DD // DHEADS
    per_block = LANES // width
    first_gain, second_gain, last_gain, mask_token = [
        small_ref[row : row + 1, :] for row in range(4)
    ]
    mask = mask_ref[...]
    select = select_ref[...]
    key_valid = lax.broadcasted_iota(jnp.int32, (TOKENS, TOKENS), 1) < PATCHES
    lane_head = lax.broadcasted_iota(jnp.int32, (TOKENS, LANES), 1) // width
    quarter = DMLP // 4

    tokens = forward_dot(select, latent_ref[...]) + mask * mask_token + table_ref[...]
    first_norm, first_hat, first_inverse = norm_forward(tokens, first_gain)
    normed = first_norm.astype(low_type)
    for piece in range(3):
        columns = slice(piece * DD, (piece + 1) * DD)
        packed_ref[:, columns] = forward_dot(normed, packed_w[:, columns]).astype(low_type)
    mixed_ref[...] = jnp.zeros(mixed_ref.shape, jnp.float32)

    def attend(head, carry):
        block = pl.multiple_of(head // per_block * LANES, LANES)
        inside = lane_head == head % per_block
        query = jnp.where(inside, packed_ref[:, pl.ds(block, LANES)], 0)
        key = packed_ref[:, pl.ds(DD + block, LANES)]
        value = packed_ref[:, pl.ds(2 * DD + block, LANES)]
        scores = jnp.where(key_valid, dot_nt(query, key) * scaling, -1e30)
        exponent = jnp.exp(scores - jnp.max(scores, -1, keepdims=True))
        probability = exponent / jnp.sum(exponent, -1, keepdims=True)
        prob_ref[head] = probability
        mixed = forward_dot(probability.astype(low_type), value)
        mixed_ref[:, pl.ds(block, LANES)] += jnp.where(inside, mixed, 0.0)
        return carry

    lax.fori_loop(0, DHEADS, attend, 0)
    mixed_low = mixed_ref[...].astype(low_type)
    middle = tokens + forward_dot(mixed_low, out_w[...])
    second_norm, second_hat, second_inverse = norm_forward(middle, second_gain)
    inner = second_norm.astype(low_type)
    decoded = middle
    for part in range(4):
        columns = slice(part * quarter, (part + 1) * quarter)
        raised = forward_dot(inner, up_w[:, columns])
        activated, slope = gelu_pair(raised)
        raised_ref[:, columns] = slope
        activated = activated.astype(low_type)
        activated_ref[:, columns] = activated
        decoded = decoded + forward_dot(activated, down_w[columns, :])
    top_norm, top_hat, top_inverse = norm_forward(decoded, last_gain)
    top = top_norm.astype(low_type)
    predicted = forward_dot(top, head_w[...])
    target = pixels_ref[...].astype(jnp.float32)
    center = target - jnp.mean(target, -1, keepdims=True)
    target = center * lax.rsqrt(jnp.mean(center * center, -1, keepdims=True) + 1e-06)
    errors = predicted - target
    loss_out[...] = jnp.sum(
        mask * jnp.mean(errors * errors, -1, keepdims=True), axis=0, keepdims=True
    )
    pred_grad = (errors * (mask * scale_ref[0, 0])).astype(low_type)

    starts = [PIX * D // LANES]
    for size in (3 * DD * DD, DD * DD, DD * DMLP, DMLP * DD):
        starts.append(starts[-1] + size // LANES)
    grad_ref[: starts[0], :] = jnp.zeros((starts[0], LANES), low_type)
    slot_rows = sent_out.shape[1]
    slots = 2 * sent_out.shape[0]
    core = core_ref[0, 0]
    copies = []

    def send_from(first_row, last_row):
        for slot in range(slots):
            if first_row <= slot * slot_rows < last_row:
                rows = grad_ref.at[pl.ds(slot * slot_rows, slot_rows), :]
                side = slot % 2
                pair = slot // 2

                def start(target, rows=rows, pair=pair, slot=slot):
                    pltpu.make_async_copy(rows, target.at[pair], copy_sems.at[slot]).start()

                pl.when(core == side)(partial(start, kept_out))
                pl.when(core != side)(partial(start, sent_out))
                copies.append(
                    pltpu.make_async_copy(rows, kept_out.at[pair], copy_sems.at[slot])
                )

    def put(left_side, right_ref_columns, pieces, base):
        depth = left_side.shape[1]
        for piece, columns in right_ref_columns:
            product = dot_tn(left_side, columns)
            for half in range(columns.shape[1] // LANES):
                work[pl.ds(base + piece + half, depth, stride=pieces), :] = product[
                    :, half * LANES : (half + 1) * LANES
                ]

    def flush(start, size):
        grad_ref[start : start + size, :] = work[:size, :].astype(low_type)
        send_from(start, start + size)

    def pairs_of(values):
        return [
            (2 * pair, values[:, 2 * pair * LANES : 2 * (pair + 1) * LANES])
            for pair in range(values.shape[1] // (2 * LANES))
        ]

    put(top, pairs_of(pred_grad), PIX // LANES, 0)
    flush(starts[4], DD * PIX // LANES)
    decoded_grad, last_terms = norm_backward(
        dot_nt(pred_grad, head_w[...]), top_hat, top_inverse, last_gain
    )
    grad_low = decoded_grad.astype(low_type)
    inner_grad = jnp.zeros((TOKENS, DD), jnp.float32)
    for part in range(4):
        columns = slice(part * quarter, (part + 1) * quarter)
        put(activated_ref[:, columns], pairs_of(grad_low), DD // LANES, part * quarter * DD // LANES)
    flush(starts[3], DMLP * DD // LANES)
    for part in range(4):
        columns = slice(part * quarter, (part + 1) * quarter)
        act_grad = dot_nt(grad_low, down_w[columns, :])
        raised_grad = (act_grad * raised_ref[:, columns]).astype(low_type)
        put(inner, pairs_of(raised_grad), DMLP // LANES, part * quarter // LANES)
        inner_grad = inner_grad + dot_nt(raised_grad, up_w[:, columns])
    flush(starts[2], DD * DMLP // LANES)
    middle_part, second_terms = norm_backward(inner_grad, second_hat, second_inverse, second_gain)
    middle_grad = decoded_grad + middle_part
    middle_low = middle_grad.astype(low_type)
    put(mixed_low, pairs_of(middle_low), DD // LANES, 0)
    flush(starts[1], DD * DD // LANES)
    mixed_ref[...] = dot_nt(middle_low, out_w[...])
    packed_grad_ref[...] = jnp.zeros(packed_grad_ref.shape, jnp.float32)

    def attend_back(head, carry):
        block = pl.multiple_of(head // per_block * LANES, LANES)
        inside = lane_head == head % per_block
        out_grad = mixed_ref[:, pl.ds(block, LANES)].astype(low_type)
        query = packed_ref[:, pl.ds(block, LANES)]
        key = packed_ref[:, pl.ds(DD + block, LANES)]
        value = packed_ref[:, pl.ds(2 * DD + block, LANES)]
        probability = prob_ref[head]
        value_grad = dot_tn(probability.astype(low_type), out_grad)
        prob_grad = dot_nt(jnp.where(inside, out_grad, 0), value)
        score_grad = (
            probability * (prob_grad - jnp.sum(probability * prob_grad, -1, keepdims=True))
        ).astype(low_type)
        query_grad = forward_dot(score_grad, key) * scaling
        key_grad = dot_tn(score_grad, query) * scaling
        for piece, values in enumerate((query_grad, key_grad, value_grad)):
            packed_grad_ref[:, pl.ds(piece * DD + block, LANES)] += jnp.where(inside, values, 0.0)
        return carry

    lax.fori_loop(0, DHEADS, attend_back, 0)
    normed_grad = jnp.zeros((TOKENS, DD), jnp.float32)
    for piece in range(3):
        columns = slice(piece * DD, (piece + 1) * DD)
        packed_low = packed_grad_ref[:, columns].astype(low_type)
        put(normed, pairs_of(packed_low), 3 * DD // LANES, piece * DD // LANES)
        normed_grad = normed_grad + dot_nt(packed_low, packed_w[:, columns])
    flush(starts[0], 3 * DD * DD // LANES)
    token_part, first_terms = norm_backward(normed_grad, first_hat, first_inverse, first_gain)
    token_grad = middle_grad + token_part
    latent_grad = dot_tn(select, token_grad.astype(low_type)).astype(low_type)
    latent_out[...] = latent_grad
    if latent_rows > 0:
        for part in range(slot_rows // latent_rows):
            columns = DD // (slot_rows // latent_rows)
            product = dot_tn(final_ref[...], latent_grad[:, part * columns : (part + 1) * columns])
            grad_ref[part * latent_rows : part * latent_rows + D, :] = product.astype(low_type)
    for row, terms in enumerate((first_terms, second_terms, last_terms, mask * token_grad)):
        small_out[row : row + 1, :] = jnp.sum(terms, axis=0, keepdims=True)
    send_from(0, starts[0])
    for copy in copies:
        copy.wait()


def decode(
    latent_rows, core, scale, final_low, latent, select, mask, table, small, pixels, weights, slots, slot_rows
):
    half = jax.ShapeDtypeStruct((slots // 2, slot_rows, LANES), low_type)
    return pl.pallas_call(
        partial(decoder_kernel, latent_rows),
        in_specs=[pl.BlockSpec(memory_space=pltpu.SMEM)] * 2
        + [pl.BlockSpec(memory_space=pltpu.VMEM)] * 12,
        out_specs=[pl.BlockSpec(memory_space=pltpu.HBM)] * 2
        + [pl.BlockSpec(memory_space=pltpu.VMEM)] * 3,
        out_shape=(
            half,
            half,
            jax.ShapeDtypeStruct(latent.shape, low_type),
            jax.ShapeDtypeStruct(small.shape, jnp.float32),
            jax.ShapeDtypeStruct((1, 1), jnp.float32),
        ),
        scratch_shapes=[
            pltpu.VMEM((slots * slot_rows, LANES), low_type),
            pltpu.SemaphoreType.DMA((slots,)),
            pltpu.VMEM((DD * DMLP // LANES, LANES), jnp.float32),
            pltpu.VMEM((TOKENS, 3 * DD), low_type),
            pltpu.VMEM((TOKENS, DD), jnp.float32),
            pltpu.VMEM((DHEADS, TOKENS, TOKENS), jnp.float32),
            pltpu.VMEM((TOKENS, DMLP), jnp.float32),
            pltpu.VMEM((TOKENS, DMLP), low_type),
            pltpu.VMEM((TOKENS, 3 * DD), jnp.float32),
        ],
        compiler_params=pltpu.CompilerParams(vmem_limit_bytes=36 * 2**20),
        cost_estimate=pl.CostEstimate(
            flops=6 * TOKENS * slots * slot_rows * LANES,
            bytes_accessed=4 * slots * slot_rows * LANES,
            transcendentals=TOKENS * (DMLP + DHEADS * TOKENS),
        ),
    )(core, scale, final_low, latent, select, mask, table, small, pixels, *weights)


def cut_spans(rows_of, slots, slot_rows):
    spans = []
    start = 0
    for source, rows in enumerate(rows_of):
        for slot in range(slots):
            first = max(start, slot * slot_rows)
            last = min(start + rows, (slot + 1) * slot_rows)
            if first < last:
                spans.append((source, first - start, slot, first - slot * slot_rows, last - first))
        start += rows
    return spans


def move_spans(core, spans, sources, sent, kept, sems):
    def move(number, target):
        source, first, slot, place, size = spans[number]
        return pltpu.make_async_copy(
            sources[source].at[pl.ds(first, size), :],
            target.at[slot // 2, pl.ds(place, size), :],
            sems.at[number],
        )

    for number, span in enumerate(spans):
        side = span[2] % 2
        pl.when(core == side)(lambda number=number: move(number, kept).start())
        pl.when(core != side)(lambda number=number: move(number, sent).start())
    for number in range(len(spans)):
        move(number, kept).wait()


def smem(value):
    return value.reshape(1, 1)


def run_kernel(kernel, tokens, arguments, outputs, scratch=(), flops=0, scalars=0, saved=0):
    count = len(tokens)
    held = arguments[len(arguments) - saved :]

    def body(*refs):
        refs = refs[count:]
        sources = refs[len(arguments) - saved : len(arguments)]
        given, rest = refs[: len(arguments) - saved], refs[len(arguments) :]
        results, rest = rest[: len(outputs)], rest[len(outputs) :]
        own, local = rest[: len(scratch)], rest[len(scratch) :][:saved]
        if saved:
            sems = rest[-1]
            copies = [
                pltpu.make_async_copy(source, target, sems.at[number])
                for number, (source, target) in enumerate(zip(sources, local))
            ]
            for copy in copies:
                copy.start()
            for copy in copies:
                copy.wait()
        kernel(*given, *local, *results, *own)

    return pl.pallas_call(
        body,
        in_specs=[pl.BlockSpec(memory_space=pl.ANY)] * count
        + [pl.BlockSpec(memory_space=pltpu.SMEM)] * scalars
        + [pl.BlockSpec(memory_space=pltpu.VMEM)] * (len(arguments) - scalars - saved)
        + [pl.BlockSpec(memory_space=pltpu.HBM)] * saved,
        out_specs=[pl.BlockSpec(memory_space=pltpu.VMEM)] * len(outputs),
        out_shape=[jax.ShapeDtypeStruct(shape, kind) for shape, kind in outputs],
        scratch_shapes=list(scratch)
        + [pltpu.VMEM(array.shape, array.dtype) for array in held]
        + [pltpu.SemaphoreType.DMA((saved,))] * (saved > 0),
        compiler_params=pltpu.CompilerParams(vmem_limit_bytes=16 * 2**20),
        cost_estimate=pl.CostEstimate(flops=flops, bytes_accessed=2**20, transcendentals=0),
    )(*tokens, *arguments)


def put_terms(terms, outs):
    for place, out in enumerate(outs):
        out[...] = terms[place * VIS : (place + 1) * VIS].astype(out.dtype)


def term_outputs(groups):
    return [((VIS, D), jnp.float32)] + [((VIS, D), low_type)] * (groups - 1)


def sum_terms(refs):
    total = refs[0][...]
    for ref in refs[1:]:
        total = total + ref[...].astype(jnp.float32)
    return total


def join(refs):
    return jnp.concatenate([ref[...] for ref in refs], 0)


def exchange(terms):
    return [terms[0]] + [swap(terms[step], "mp", step) for step in range(1, len(terms))]


def spread(values):
    groups = lax.axis_size("mp")
    return [values] + [swap(values, "mp", step) for step in range(1, groups)]


def head_lanes(rows, columns):
    return lax.broadcasted_iota(jnp.int32, (rows, columns), 1) // (D // HEADS)


def enter_encoder(seen, patch_w, table, gain, packed_w, out_w, valid):
    groups = lax.axis_size("mp")
    rows, columns = groups * VIS, D // groups
    heads = HEADS // groups
    scaling = (D // HEADS) ** (-0.5)

    def kernel(seen, patch_w, table, gain, packed_w, out_w, valid, *outs):
        residual_out, hat_out, inverse_out, normed_out, packed_out, prob_out, mixed_out = outs[:7]
        residual = forward_dot(seen[...], patch_w[...]) + table[...]
        norm, hat, inverse = norm_forward(residual, gain[...])
        residual_out[...] = residual[:VIS]
        hat_out[...] = hat[:VIS]
        inverse_out[...] = jnp.broadcast_to(inverse[:VIS], (VIS, LANES))
        normed = norm.astype(low_type)
        normed_out[...] = normed
        packed = forward_dot(normed, packed_w[...]).astype(low_type)
        packed_out[...] = packed
        query, key, value = [packed[:, third * columns : (third + 1) * columns] for third in range(3)]
        one = lax.broadcasted_iota(jnp.int32, (rows, rows), 0) // VIS
        other = lax.broadcasted_iota(jnp.int32, (rows, rows), 1) // VIS
        allowed = (one == other) & (valid[...] > 0.5)
        lanes = head_lanes(rows, columns)
        mixed = jnp.zeros((rows, columns), jnp.float32)
        for head in range(heads):
            inside = lanes == head
            scores = dot_nt(jnp.where(inside, query, 0), key) * scaling
            scores = jnp.where(allowed, scores, -1e30)
            exponent = jnp.exp(scores - jnp.max(scores, -1, keepdims=True))
            probability = exponent / jnp.sum(exponent, -1, keepdims=True)
            prob_out[head] = probability
            mixed = mixed + jnp.where(inside, forward_dot(probability.astype(low_type), value), 0.0)
        mixed_low = mixed.astype(low_type)
        mixed_out[...] = mixed_low
        put_terms(forward_dot(mixed_low, out_w[...]), outs[7:])

    outputs = [
        ((VIS, D), jnp.float32),
        ((VIS, D), jnp.float32),
        ((VIS, LANES), jnp.float32),
        ((rows, D), low_type),
        ((rows, 3 * columns), low_type),
        ((heads, rows, rows), jnp.float32),
        ((rows, columns), low_type),
    ] + term_outputs(groups)
    results = run_kernel(
        kernel, [], [seen, patch_w, table, gain, packed_w, out_w, valid], outputs, flops=10**9
    )
    return results[:7], results[7:]


def norm_of_sum(terms, residual, gain):
    count = len(terms)

    def kernel(*refs):
        residual, gain = refs[count : count + 2]
        sum_out, low_out, hat_out, inverse_out = refs[count + 2 :]
        total = residual[...] + sum_terms(refs[:count])
        norm, hat, inverse = norm_forward(total, gain[...])
        sum_out[...] = total
        low_out[...] = norm.astype(low_type)
        hat_out[...] = hat
        inverse_out[...] = jnp.broadcast_to(inverse, (VIS, LANES))

    outputs = [
        ((VIS, D), jnp.float32),
        ((VIS, D), low_type),
        ((VIS, D), jnp.float32),
        ((VIS, LANES), jnp.float32),
    ]
    return run_kernel(kernel, [], [*terms, residual, gain], outputs)


def raise_and_lower(inner, up_w, down_w):
    groups = len(inner)

    def kernel(*refs):
        up_w, down_w, inner_out = refs[groups : groups + 3]
        inner = join(refs[:groups])
        inner_out[...] = inner
        activated, slope = gelu_pair(forward_dot(inner, up_w[...]))
        put_terms(forward_dot(activated.astype(low_type), down_w[...]), refs[groups + 3 :])

    outputs = [((groups * VIS, D), low_type)] + term_outputs(groups)
    results = run_kernel(kernel, [], [*inner, up_w, down_w], outputs, flops=6 * 10**8)
    return results[0], results[1:]


def latent_of_sum(tokens, terms, residual, gain, latent_w):
    count = len(terms)

    def kernel(*refs):
        residual, gain, latent_w, low_out, hat_out, inverse_out, latent_out = refs[count:]
        norm, hat, inverse = norm_forward(residual[...] + sum_terms(refs[:count]), gain[...])
        final_low = norm.astype(low_type)
        low_out[...] = final_low
        hat_out[...] = hat
        inverse_out[...] = jnp.broadcast_to(inverse, (VIS, LANES))
        columns = latent_w.shape[2]
        for place in range(count):
            latent_out[:, place * columns : (place + 1) * columns] = forward_dot(
                final_low, latent_w[place]
            ).astype(low_type)

    outputs = [
        ((VIS, D), low_type),
        ((VIS, D), jnp.float32),
        ((VIS, LANES), jnp.float32),
        ((VIS, DD), low_type),
    ]
    return run_kernel(kernel, tokens, [*terms, residual, gain, latent_w], outputs)


def latent_back(tokens, member, along, latent_grad, latent_w, hat, inverse, gain):
    groups, rows, columns = latent_w.shape

    def kernel(member, latent_grad, latent_w, hat, inverse, gain, grad_out, gain_out, work, *outs):
        total = jnp.zeros((VIS, D), jnp.float32)
        for place in range(groups):
            cut = latent_grad[:, place * columns : (place + 1) * columns]
            work[place] = cut
            total = total + dot_nt(cut, latent_w[place])
        gradient, terms = norm_backward(total, hat[...], inverse[:, :1], gain[...])
        grad_out[...] = gradient
        for step, out in enumerate(outs):
            out[:, :D] = gradient.astype(low_type)
            if not along:
                out[:, D:] = work[member[0, 0] ^ step]
        gain_out[...] = jnp.sum(terms, axis=0, keepdims=True)

    outputs = [((VIS, D), jnp.float32), ((1, D), jnp.float32), ((groups, VIS, columns), low_type)]
    outputs += [((VIS, D + (0 if along else columns)), low_type)] * groups
    results = run_kernel(
        kernel,
        tokens,
        [smem(member), latent_grad, latent_w, hat, inverse, gain],
        outputs,
        scalars=1,
    )
    return results[0], results[1], results[3:]


def norm_back_of_sum(tokens, terms, upstream, hat, inverse, gain):
    count = len(terms)

    def kernel(*refs):
        upstream, hat, inverse, gain, grad_out, low_out, gain_out = refs[count:]
        part, gain_terms = norm_backward(
            sum_terms(refs[:count]), hat[...], inverse[:, :1], gain[...]
        )
        gradient = upstream[...] + part
        grad_out[...] = gradient
        low_out[...] = gradient.astype(low_type)
        gain_out[...] = jnp.sum(gain_terms, axis=0, keepdims=True)

    outputs = [((VIS, D), jnp.float32), ((VIS, D), low_type), ((1, D), jnp.float32)]
    return run_kernel(kernel, tokens, [*terms, upstream, hat, inverse, gain], outputs)


def mlp_back(tokens, core, grads, finals, inner, up_w, down_w, slots, slot_rows, first_row):
    groups = len(grads)
    embed_cols = grads[0].shape[1] - D
    count = len(tokens)
    given = groups + len(finals)
    spans = cut_spans([first_row, up_w.shape[0], down_w.shape[0]], slots, slot_rows)
    spans = [span for span in spans if span[0] > 0]

    def kernel(*refs):
        core, refs = refs[count], refs[count + 1 :]
        sources = refs[given : given + 3]
        outs = refs[given + 3 :]
        *outs, inner, up_w, down_w, load_sems = outs
        copies = [
            pltpu.make_async_copy(source, target, load_sems.at[number])
            for number, (source, target) in enumerate(zip(sources, (inner, up_w, down_w)))
        ]
        for copy in copies:
            copy.start()
        for copy in copies:
            copy.wait()
        both = join(refs[:groups])
        grad_low = both[:, :D]
        inner_low = inner[...]
        activated, slope = gelu_pair(forward_dot(inner_low, up_w[...]))
        raised_grad = (dot_nt(grad_low, down_w[...]) * slope).astype(low_type)
        put_terms(dot_nt(raised_grad, up_w[...]), outs[2 : 2 + groups])
        down_grad = dot_tn(activated.astype(low_type), grad_low).astype(low_type)
        up_grad = dot_tn(inner_low, raised_grad).astype(low_type)
        if slots > 0:
            up_work, down_work, sems = outs[2 + groups :][-3:]
            up_work[...] = up_grad
            down_work[...] = down_grad
            move_spans(core[0, 0], spans, [None, up_work, down_work], outs[0], outs[1], sems)
        else:
            outs[0][...] = up_grad
            outs[1][...] = down_grad
        if embed_cols > 0:
            final_low = join(refs[groups:given])
            outs[2 + groups][...] = dot_tn(final_low, both[:, D:]).astype(low_type)

    space = pltpu.VMEM
    shapes = [up_w.shape, down_w.shape]
    scratch = []
    if slots > 0:
        space = pltpu.HBM
        shapes = [(slots // 2, slot_rows, D)] * 2
        scratch = [
            pltpu.VMEM(up_w.shape, low_type),
            pltpu.VMEM(down_w.shape, low_type),
            pltpu.SemaphoreType.DMA((len(spans),)),
        ]
    outputs = [(shape, low_type) for shape in shapes] + term_outputs(groups)
    if embed_cols > 0:
        outputs.append(((D, embed_cols), low_type))
    results = pl.pallas_call(
        kernel,
        in_specs=[pl.BlockSpec(memory_space=pl.ANY)] * count
        + [pl.BlockSpec(memory_space=pltpu.SMEM)]
        + [pl.BlockSpec(memory_space=pltpu.VMEM)] * given
        + [pl.BlockSpec(memory_space=pltpu.HBM)] * 3,
        out_specs=[pl.BlockSpec(memory_space=space)] * 2
        + [pl.BlockSpec(memory_space=pltpu.VMEM)] * (len(outputs) - 2),
        out_shape=[jax.ShapeDtypeStruct(shape, kind) for shape, kind in outputs],
        scratch_shapes=scratch
        + [pltpu.VMEM(array.shape, low_type) for array in (inner, up_w, down_w)]
        + [pltpu.SemaphoreType.DMA((3,))],
        compiler_params=pltpu.CompilerParams(vmem_limit_bytes=16 * 2**20),
        cost_estimate=pl.CostEstimate(flops=15 * 10**8, bytes_accessed=2**20, transcendentals=0),
    )(*tokens, smem(core), *grads, *finals, inner, up_w, down_w)
    return results[:2], results[2 : 2 + groups], results[2 + groups :]


def attend_back(tokens, grad_low, normed, packed, prob, mixed, packed_w, out_w):
    groups = len(grad_low)
    rows, columns = groups * VIS, D // groups
    heads = HEADS // groups
    scaling = (D // HEADS) ** (-0.5)

    def kernel(*refs):
        normed, packed, prob, mixed, packed_w, out_w, packed_out, out_out = refs[
            groups : groups + 8
        ]
        grad_low = join(refs[:groups])
        mixed_grad = dot_nt(grad_low, out_w[...]).astype(low_type)
        query, key, value = [packed[:, third * columns : (third + 1) * columns] for third in range(3)]
        lanes = head_lanes(rows, columns)
        totals = [jnp.zeros((rows, columns), jnp.float32)] * 3
        for head in range(heads):
            inside = lanes == head
            probability = prob[head]
            value_grad = dot_tn(probability.astype(low_type), mixed_grad)
            prob_grad = dot_nt(jnp.where(inside, mixed_grad, 0), value)
            score_grad = (
                probability * (prob_grad - jnp.sum(probability * prob_grad, -1, keepdims=True))
            ).astype(low_type)
            query_grad = forward_dot(score_grad, key) * scaling
            key_grad = dot_tn(score_grad, query) * scaling
            totals = [
                total + jnp.where(inside, values, 0.0)
                for total, values in zip(totals, (query_grad, key_grad, value_grad))
            ]
        packed_grad = jnp.concatenate(totals, 1).astype(low_type)
        put_terms(dot_nt(packed_grad, packed_w[...]), refs[groups + 8 :])
        out_out[...] = dot_tn(mixed[...], grad_low).astype(low_type)
        packed_out[...] = dot_tn(normed[...], packed_grad).astype(low_type)

    outputs = [(packed_w.shape, low_type), (out_w.shape, low_type)] + term_outputs(groups)
    results = run_kernel(
        kernel,
        tokens,
        [*grad_low, normed, packed, prob, mixed, packed_w, out_w],
        outputs,
        flops=10**9,
        saved=6,
    )
    return results[:2], results[2:]


def last_norm_back(tokens, terms, upstream, hat, inverse, gain, second_gain, last_gain, dec_small):
    count = len(terms)

    def kernel(*refs):
        upstream, hat, inverse, gain, second_gain, last_gain, dec_small, low_out, work = refs[count:]
        part, gain_terms = norm_backward(
            sum_terms(refs[:count]), hat[...], inverse[:, :1], gain[...]
        )
        low_out[:VIS, :] = (upstream[...] + part).astype(low_type)
        work[...] = jnp.zeros(work.shape, jnp.float32)
        work[0:1, :] = jnp.sum(gain_terms, axis=0, keepdims=True)
        work[1:2, :] = second_gain[...]
        work[2:3, :] = last_gain[...]
        work[3:7, :DD] = dec_small[:4, :]
        values = work[...]
        high = values.astype(low_type)
        rest = (values - high.astype(jnp.float32)).astype(low_type)
        low_out[VIS:, :] = jnp.concatenate([high, rest], 0)

    return run_kernel(
        kernel,
        tokens,
        [*terms, upstream, hat, inverse, gain, second_gain, last_gain, dec_small],
        [((VIS + 16, D), low_type)],
        [pltpu.VMEM((8, D), jnp.float32)],
    )[0]


def patch_back(tokens, member, core, seen, grads, row_count):
    groups = len(grads)
    tail = PIX - groups * row_count
    early = 0 < tail <= row_count

    def kernel(member, core, seen, *refs):
        kept_out, sent_out, work = refs[groups:]
        rows_low = jnp.concatenate([ref[:VIS, :] for ref in refs[:groups]], 0)
        gains = jnp.zeros((8, D), jnp.float32)
        for ref in refs[:groups]:
            parts = ref[VIS:, :].astype(jnp.float32)
            gains = gains + (parts[:8] + parts[8:])
        if early:
            work[:PIX, :] = dot_tn(seen[...], rows_low)
            work[PIX:, :] = jnp.zeros((work.shape[0] - PIX, D), jnp.float32)
            rows = work[pl.ds(pl.multiple_of(member[0, 0] * row_count, 8), row_count), :]
            last = work[PIX - tail : PIX - tail + row_count, :]
            even = core[0, 0] == 0
            kept_out[:row_count, :] = jnp.where(even, rows, last)
            sent_out[:row_count, :] = jnp.where(even, last, rows)
        kept_out[kept_out.shape[0] - 8 :, :] = gains
        sent_out[sent_out.shape[0] - 8 :, :] = gains

    rows = row_count if early else 0
    return run_kernel(
        kernel,
        tokens,
        [smem(member), smem(core), seen, *grads],
        [((rows + 8, D), jnp.float32)] * 2,
        [pltpu.VMEM((PIX + row_count, D), jnp.float32)],
        4 * 10**8,
        2,
    )


def pack_block(tokens, core, packed_grad, out_grad, sent, kept):
    depth, columns = packed_grad.shape
    pair = depth // 2
    nine = 2 * columns // LANES
    six = D // LANES
    count = len(tokens)
    tiles = (columns + LANES - 1) // LANES
    slots, slot_rows = 2 * sent.shape[0], sent.shape[1]
    hidden_rows = 2 * D
    rows_of = [depth * columns // D, out_grad.shape[0], hidden_rows]
    rows_of.append(slots * slot_rows - sum(rows_of))
    spans = [span for span in cut_spans(rows_of, slots, slot_rows) if span[0] != 2]
    late = [span for span in spans if span[0] == 0]
    soon = [span for span in spans if span[0] != 0]

    def kernel(*refs):
        core, packed, out_grad, sent_in, kept_in, sent_out, kept_out = refs[count : count + 7]
        wide, flat, rows, zeros, out_work, late_sems, soon_sems = refs[count + 7 :]
        zeros[...] = jnp.zeros(zeros.shape, low_type)
        out_work[...] = out_grad[...]
        halves = []
        for tile in range(tiles):
            lanes = min(LANES, columns - tile * LANES)
            wide[tile * depth : (tile + 1) * depth, :lanes] = packed[
                :, tile * LANES : tile * LANES + lanes
            ].astype(jnp.float32)
        for side in range(2):
            pieces = [wide[pl.ds(tile * depth + side, pair, stride=2), :] for tile in range(tiles)]
            halves.append(jnp.concatenate(pieces, 1)[:, :columns])
        both = jnp.concatenate(halves, 1)
        for tile in range(nine):
            flat[pl.ds(tile, pair, stride=nine), :] = both[:, tile * LANES : (tile + 1) * LANES]
        for piece in range(six):
            rows[:, piece * LANES : (piece + 1) * LANES] = flat[
                pl.ds(piece, rows.shape[0], stride=six), :
            ].astype(low_type)
        sources = [rows, out_work, None, zeros]
        move_spans(core[0, 0], late + soon, sources, sent_out, kept_out, late_sems)

    return pl.pallas_call(
        kernel,
        in_specs=[pl.BlockSpec(memory_space=pl.ANY)] * count
        + [pl.BlockSpec(memory_space=pltpu.SMEM)]
        + [pl.BlockSpec(memory_space=pltpu.VMEM)] * 2
        + [pl.BlockSpec(memory_space=pltpu.HBM)] * 2,
        out_specs=[pl.BlockSpec(memory_space=pltpu.HBM)] * 2,
        out_shape=[jax.ShapeDtypeStruct(sent.shape, low_type)] * 2,
        input_output_aliases={count + 3: 0, count + 4: 1},
        scratch_shapes=[
            pltpu.VMEM((tiles * depth, LANES), jnp.float32),
            pltpu.VMEM((pair * nine, LANES), jnp.float32),
            pltpu.VMEM((rows_of[0], D), low_type),
            pltpu.VMEM((rows_of[-1], D), low_type),
            pltpu.VMEM(out_grad.shape, low_type),
            pltpu.SemaphoreType.DMA((len(spans),)),
            pltpu.SemaphoreType.DMA((len(spans),)),
        ],
        compiler_params=pltpu.CompilerParams(vmem_limit_bytes=16 * 2**20),
        cost_estimate=pl.CostEstimate(flops=0, bytes_accessed=8 * 2**20, transcendentals=0),
    )(*tokens, smem(core), packed_grad, out_grad, sent, kept)


def close_shared(tokens, place, owner, arrived, patch_rows):
    groups, lane_rows, lanes = arrived.shape
    pieces = patch_rows.shape[1] // LANES

    def kernel(place, owner, arrived, patch_rows, shared_out, latent_out, square_out, work):
        total = arrived[0].astype(jnp.float32)
        for member in range(1, groups):
            total = total + arrived[member].astype(jnp.float32)
        latent_out[...] = total[:D]
        for piece in range(pieces):
            work[pl.ds(piece, patch_rows.shape[0], stride=pieces), :] = patch_rows[
                :, piece * LANES : (piece + 1) * LANES
            ]
        patch = jnp.where(owner[0, 0] == 1, work[...], 0.0)
        total = jnp.where(place[0, 0] == 0, 0.0, total) + patch
        shared_out[...] = total
        squares = jnp.sum(total * total, axis=0, keepdims=True)
        square_out[...] = jnp.sum(squares, axis=1, keepdims=True)

    return run_kernel(
        kernel,
        tokens,
        [smem(place), smem(owner), arrived, patch_rows],
        [((lane_rows, lanes), jnp.float32), ((D, lanes), jnp.float32), ((1, 1), jnp.float32)],
        [pltpu.VMEM((lane_rows, lanes), jnp.float32)],
        scalars=2,
    )


def close_block(halves, latent):
    rows = [half.shape[0] for half in halves]
    pieces = D // LANES
    latent_rows = latent.shape[0] // pieces

    def kernel(one, two, latent, block_out, square_out):
        block_out[: rows[0], :] = one[...]
        block_out[rows[0] :, :] = two[...]
        last = slice(sum(rows) - latent_rows, sum(rows))
        for piece in range(pieces):
            block_out[last, piece * LANES : (piece + 1) * LANES] += latent[
                pl.ds(piece, latent_rows, stride=pieces), :
            ]
        total = block_out[...]
        squares = jnp.sum(total * total, axis=0, keepdims=True)
        square_out[...] = jnp.sum(squares, axis=1, keepdims=True)

    return run_kernel(
        kernel,
        [],
        [*halves, latent],
        [((sum(rows), D), jnp.float32), ((1, 1), jnp.float32)],
    )


def on_device(
    pixels,
    visible,
    block_master,
    block_first,
    block_second,
    shared_master,
    shared_first,
    shared_second,
    gains_master,
    gains_first,
    gains_second,
):
    groups = lax.axis_size("mp")
    replicas = lax.axis_size("dp")
    member = lax.axis_index("mp")
    model_cols = D // groups
    mlp_cols = MLP // groups
    embed_cols = DD // groups
    block_rows = block_master.shape[1] // D
    shared_rows = shared_master.shape[0] // 128

    own_pixels = pick(pixels, member, 0)
    own_visible = pick(visible, member, 0)
    hidden_mask = (1 - own_visible).astype(jnp.float32)
    hidden_count = jnp.sum(1 - own_visible).astype(jnp.float32)

    block_lanes = block_master.reshape(-1, 128)
    shared_lanes = shared_master.reshape(-1, 128)
    block_rowed, shared_low, shared_rowed = low_rows(block_lanes, shared_lanes, D)
    shared_flat = lax.all_gather(shared_low, ("dp", "mp"), axis=0).reshape(-1, 128)

    patch_size = PIX * D
    head_rows = shared_master.shape[0] // D
    tail_length = patch_size - groups * head_rows * D
    early = 0 < tail_length <= shared_master.shape[0] and groups * head_rows < PIX
    small_length = gains_master.shape[0]
    small_row = jnp.concatenate([lax.reduce_precision(gains_master, 8, 7), hidden_count[None]])
    small_row = jnp.pad(small_row, (0, -small_row.shape[0] % 128))
    near_visible = reorder(visible, member)
    near_pixels = reorder(pixels, member)
    select, slot_patch, key_valid = visible_slots(near_visible)
    chosen = (slot_patch[:, :, None] == jnp.arange(PATCHES)[None, None, :]).astype(low_type)
    seen_patches = jnp.einsum(
        "isp,ipd->isd", chosen, near_pixels, preferred_element_type=jnp.float32
    ).astype(low_type)
    small_table, block_flat = gather_early(small_row, block_rowed)
    gain_flat = small_table[:, :small_length].reshape(-1)
    count_total = jnp.sum(small_table[:, small_length])

    bounds = [0, 3 * model_cols, model_cols, mlp_cols, mlp_cols, embed_cols]
    bounds = [sum(bounds[: place + 1]) for place in range(len(bounds))]
    enc_packed, enc_out, enc_up, enc_down, enc_latent = [
        block_flat[low:high] for low, high in zip(bounds[:-1], bounds[1:])
    ]
    enc_packed = enc_packed.reshape(D, 3 * model_cols)
    enc_up = enc_up.reshape(D, mlp_cols)
    own_latent_w = enc_latent.reshape(D, embed_cols)

    (patch_w,) = unpack(shared_flat, 0, [(PIX, D)])
    dec_weights = unpack(
        shared_flat, PIX * D, [(DD, 3 * DD), (DD, DD), (DD, DMLP), (DMLP, DD), (DD, PIX)]
    )
    enc_one, enc_two, enc_last, dec_one, dec_two, dec_last, mask_token = cut_pieces(
        gain_flat, [(D,), (D,), (D,), (DD,), (DD,), (DD,), (DD,)]
    )

    latent_w = reorder(share(own_latent_w), member)
    saved, terms = enter_encoder(
        seen_patches.reshape(-1, PIX),
        patch_w,
        position_table(slot_patch, D).reshape(-1, D),
        enc_one[None],
        enc_packed,
        enc_out,
        key_valid.astype(jnp.float32).reshape(1, -1),
    )
    residual, first_hat, first_inverse, normed, packed, prob, mixed_heads = saved
    middle, inner_low, second_hat, second_inverse = norm_of_sum(
        exchange(terms), residual, enc_two[None]
    )
    inner_low = spread(inner_low)
    inner_low, terms = raise_and_lower(inner_low, enc_up, enc_down)
    final_low, final_hat, final_inverse, latent = latent_of_sum(
        [], exchange(terms), middle, enc_last[None], latent_w
    )

    pad = ((0, TOKENS - PATCHES), (0, 0))
    place = lax.axis_index("dp")
    along = early and shared_rows >= D and bounds[4] >= (replicas - 1) * block_rows
    along = along and block_rows % 16 == 0
    sent_grad, kept_grad, latent_grad, dec_small, loss_local = decode(
        shared_rows if along else 0,
        (place & 1).reshape(1, 1),
        (2.0 / (PIX * count_total)).reshape(1, 1),
        final_low,
        latent,
        jnp.pad(select[0].T.astype(low_type), pad),
        jnp.pad(hidden_mask[:, None], pad),
        jnp.pad(position_table(jnp.arange(PATCHES), DD), pad),
        jnp.pad(jnp.stack([dec_one, dec_two, dec_last, mask_token]), ((0, 4), (0, 0))),
        jnp.pad(own_pixels, pad),
        dec_weights,
        replicas,
        groups * shared_rows,
    )
    loss_local = loss_local[0, 0]
    got_grad = swap(sent_grad, "dp", 1)

    encoded_grad, enc_last_grad, encoded_low = latent_back(
        [], member, along, latent_grad, latent_w, final_hat, final_inverse, enc_last[None]
    )
    (up_grad, down_grad), terms, latent_wgrad = mlp_back(
        [],
        place & 1,
        exchange(encoded_low),
        [] if along else spread(final_low),
        inner_low,
        enc_up,
        enc_down,
        replicas if along else 0,
        block_rows,
        bounds[2],
    )
    terms = exchange(terms)
    column_totals, column_first = first_stage(kept_grad, after_all(got_grad, terms[1:]))
    middle_grad, middle_low, enc_two_grad = norm_back_of_sum(
        [], terms, encoded_grad, second_hat, second_inverse, enc_two[None]
    )
    (packed_grad, out_grad), terms = attend_back(
        column_first, spread(middle_low), normed, packed, prob, mixed_heads, enc_packed, enc_out
    )
    terms = exchange(terms)
    if along:
        sent_block, kept_block = pack_block(
            terms[1:], place & 1, packed_grad, out_grad, up_grad, down_grad
        )
        block_totals, block_sent = first_stage(kept_block, swap(sent_block, "dp", 1))
    else:
        block_grad = jnp.concatenate(
            [
                piece.reshape(-1, D)
                for piece in (packed_grad, out_grad, up_grad, down_grad, latent_wgrad[0])
            ]
        )
        block_share = reduce_dp(block_grad.reshape(replicas, block_rows, D))
        block_sent = []
    column_halves, column_last = later_stages(column_totals, terms[1:])
    column_share = jnp.concatenate(column_halves, 0)
    residual_low = last_norm_back(
        [],
        terms,
        middle_grad,
        first_hat,
        first_inverse,
        enc_one[None],
        enc_two_grad,
        enc_last_grad,
        dec_small,
    )

    residual_all = spread(residual_low)
    kept, sent = patch_back(
        block_sent,
        member,
        place & 1,
        seen_patches.reshape(-1, PIX),
        residual_all,
        head_rows,
    )
    column_share = column_share.reshape(groups, shared_rows, 128).astype(low_type)
    arrived = to_members(column_share)
    total = kept + swap(sent, "dp", 1)
    gain_rows = total[-8:]
    if early:
        total = total[:-8]
        total_low = total.astype(low_type)
        for dp in range(2, replicas, 2):
            pairs = [(dp * groups + mp, mp) for mp in range(groups)] + [((dp + 1) * groups, groups)]
            total = total + pair_permute(total_low, pairs).astype(jnp.float32)
        owner = (place == 0) | ((place == 1) & (member == 0))
        gain_rows = sum_chips(gain_rows)
        if along:
            block_halves, block_last = later_stages(block_totals)
            shared_share, latent_share, shared_square = close_shared(
                [], place, owner.astype(jnp.int32), arrived, total
            )
            latent_share = lax.ppermute(latent_share, "dp", [(0, replicas - 1)])
            block_share, block_square = close_block(block_halves, latent_share)
            squares = block_square[0, 0] + shared_square[0, 0]
        else:
            shared_share = jnp.sum(arrived.astype(jnp.float32), 0)
            shared_share = shared_share + jnp.where(owner, total.reshape(-1, 128), 0.0)
    else:
        patch_rows = outer_sum(seen_patches[0], residual_low[:VIS])
        patch_rows = patch_rows.astype(low_type).reshape(-1, 128)
        patch_rows = jnp.pad(patch_rows, ((0, shared_flat.shape[0] - patch_rows.shape[0]), (0, 0)))
        column = reduce_dp(patch_rows.reshape(replicas, groups * shared_rows, 128))
        column = column.reshape(groups, shared_rows, 128).astype(low_type)
        shared_share = jnp.sum(arrived.astype(jnp.float32), 0)
        shared_share = shared_share + jnp.sum(to_members(column).astype(jnp.float32), 0)
        gain_rows = sum_chips(gain_rows)
    pad_length = gain_flat.shape[0] - 3 * D - 4 * DD
    gain_grad = jnp.concatenate(
        [
            gain_rows[:3].reshape(-1),
            gain_rows[3:7, :DD].reshape(-1),
            jnp.zeros((pad_length,), jnp.float32),
        ]
    )
    own = lax.axis_index("dp") * groups + member
    gain_share = lax.dynamic_slice_in_dim(gain_grad, own * small_length, small_length)
    if not along:
        squares = jnp.sum(block_share * block_share) + jnp.sum(shared_share * shared_share)
    squares = squares + jnp.sum(gain_share * gain_share)
    sums = sum_small(jnp.stack([squares, loss_local]).reshape(1, 2))
    square_total, loss_total = sums[0, 0], sums[0, 1]
    grad_norm = jnp.sqrt(square_total)
    factor = jnp.minimum(1.0, clip_norm / (grad_norm + 1e-06))
    block_out, shared_out = update(
        factor,
        block_share,
        [block_first.reshape(-1, 128), block_second.reshape(-1, 128), block_lanes],
        shared_share,
        [shared_first.reshape(-1, 128), shared_second.reshape(-1, 128), shared_lanes],
    )
    block_out = tuple(piece.reshape(block_master.shape) for piece in block_out)
    shared_out = tuple(piece.reshape(-1) for piece in shared_out)
    gain_out = adamw(gain_share, gains_first, gains_second, gains_master, factor, rate_gains, 0.0)
    return (grad_norm, loss_total, count_total) + block_out + shared_out + gain_out


def solution(mesh):
    return jax.shard_map(
        on_device,
        mesh=mesh,
        in_specs=(
            P("dp", None, None),
            P("dp", None),
            P("mp", "dp"),
            P("mp", "dp"),
            P("mp", "dp"),
            P(("dp", "mp")),
            P(("dp", "mp")),
            P(("dp", "mp")),
            P(("dp", "mp")),
            P(("dp", "mp")),
            P(("dp", "mp")),
        ),
        out_specs=(
            P(),
            P(),
            P(),
            P("mp", "dp"),
            P("mp", "dp"),
            P("mp", "dp"),
            P("mp", "dp"),
            P(("dp", "mp")),
            P(("dp", "mp")),
            P(("dp", "mp")),
            P(("dp", "mp")),
            P(("dp", "mp")),
            P(("dp", "mp")),
            P(("dp", "mp")),
            P(("dp", "mp")),
        ),
        check_vma=False,
    )
```

```python
from functools import partial
import math

import jax
import jax.numpy as jnp
from jax import lax
from jax.experimental import pallas as pl
from jax.experimental.pallas import tpu as pltpu
from jax.sharding import PartitionSpec as P

D = 768
HEADS = 12
MLP = 3072
DD = 512
DHEADS = 16
DMLP = 2048
PIX = 768
PATCHES = 196
VIS = 64
STEP = 10


low_type = jnp.bfloat16
clip_norm = 0.0002
beta_one = 0.9
beta_two = 0.95
adam_eps = 1e-10
rate_matrix = 0.03
rate_gains = 0.7
weight_decay = 0.1


def forward_dot(left_side, right_side):
    return jnp.dot(left_side, right_side, preferred_element_type=jnp.float32)


def back_dot(left_side, right_side):
    return lax.dot_general(
        left_side,
        right_side,
        (((left_side.ndim - 1,), (1,)), ((), ())),
        preferred_element_type=jnp.float32,
    )


def outer_sum(left_side, right_side):
    left_rows = left_side.reshape(-1, left_side.shape[-1])
    right_rows = right_side.reshape(-1, right_side.shape[-1])
    return lax.dot_general(
        left_rows, right_rows, (((0,), (0,)), ((), ())), preferred_element_type=jnp.float32
    )


def swap(values, axis_name, distance):
    count = lax.axis_size(axis_name)
    return lax.ppermute(values, axis_name, [(place, place ^ distance) for place in range(count)])


def share(values):
    groups = lax.axis_size("mp")
    return jnp.stack([values] + [swap(values, "mp", step) for step in range(1, groups)])


def share_by_core(values):
    core = lax.axis_index("dp") & 1
    rows = values.shape[0] // 2
    near = share(lax.dynamic_slice_in_dim(values, core * rows, rows, 0))
    other = swap(near, "dp", 1)
    first = jnp.where(core == 0, near, other)
    return jnp.concatenate([first, jnp.where(core == 0, other, near)], 1)


def pick(values, index, dim):
    return lax.dynamic_index_in_dim(values, index, dim, keepdims=False)


def reorder(values, place):
    return jnp.stack([pick(values, place ^ step, 0) for step in range(values.shape[0])])


def bits_of(count):
    return count.bit_length() - 1


def after(values, token):
    first = token[(0,) * token.ndim].astype(jnp.float32)
    return values + jnp.minimum(jnp.abs(first), 0.0).astype(values.dtype)


def after_all(values, tokens):
    for token in tokens:
        values = after(values, token)
    return values


def half_cut(values, side, dim):
    return (pick(values, side, dim), pick(values, 1 - side, dim))


def bit_orders():
    higher = tuple(range(3, bits_of(lax.axis_size("dp"))))
    return ((1, 2) + higher, (2, 1) + higher)


def first_stage(kept_whole, got_whole):
    width = bits_of(lax.axis_size("dp"))
    place = lax.axis_index("dp")
    rows = kept_whole.shape[1]
    split = (2,) * (width - 1) + kept_whole.shape[1:]
    both = [piece.reshape(split) for piece in (kept_whole, got_whole)]
    totals, sents = [], []
    for (first, last), order in zip(((0, rows // 2), (rows // 2, rows)), bit_orders()):
        dim = width - 1 - order[0]
        side = (place >> order[0]) & 1

        def part_of(values, where, dim=dim, first=first, last=last):
            starts = [0] * values.ndim
            sizes = list(values.shape)
            starts[dim], sizes[dim] = where, 1
            starts[width - 1], sizes[width - 1] = first, last - first
            cut = lax.dynamic_slice(values, starts, sizes)
            return cut.reshape(sizes[:dim] + sizes[dim + 1 :]).astype(jnp.float32)

        kept, sent = [sum(part_of(piece, where) for piece in both) for where in (side, 1 - side)]
        sent = sent.astype(low_type)
        sents.append(sent)
        totals.append(kept + swap(sent, "dp", 1 << order[0]).astype(jnp.float32))
    return totals, sents


def later_stages(totals, tokens=()):
    width = bits_of(lax.axis_size("dp"))
    place = lax.axis_index("dp")
    halves, sents = [], []
    for total, order in zip(totals, bit_orders()):
        total = after_all(total, tokens)
        left = [bit for bit in range(width - 1, 0, -1) if bit != order[0]]
        for bit in order[1:]:
            kept, sent = half_cut(total, (place >> bit) & 1, left.index(bit))
            sent = sent.astype(low_type)
            total = kept + swap(sent, "dp", 1 << bit).astype(jnp.float32)
            left.remove(bit)
        sents.append(sent)
        halves.append(total)
    return halves, sents


def reduce_dp(values):
    place = lax.axis_index("dp")
    shaped = values.reshape((-1, 2) + values.shape[1:])
    kept, sent = half_cut(shaped, place & 1, 1)
    totals, sents = first_stage(kept, swap(sent, "dp", 1))
    return jnp.concatenate(later_stages(totals)[0], 0)


def to_members(values):
    return lax.all_to_all(values, "mp", 0, 0, tiled=True)


def sum_chips(row):
    width = bits_of(lax.axis_size("dp"))
    if width == 3:
        place = lax.axis_index("dp") >> 1
        rows = jnp.stack([row] + [swap(row, "dp", 2 * step) for step in range(1, 4)])
        return jnp.sum(reorder(rows, place), 0)
    for bit in range(1, width):
        row = row + swap(row, "dp", 1 << bit)
    return row


def sum_small(row):
    row = sum_chips(row + swap(row, "dp", 1))
    return jnp.sum(reorder(share(row), lax.axis_index("mp")), 0)


def pair_permute(values, pairs):
    return lax.ppermute(values, ("dp", "mp"), pairs)


def gather_early(small_row, block_rows):
    replicas = lax.axis_size("dp")
    place = lax.axis_index("dp")
    member = lax.axis_index("mp")
    width = bits_of(replicas)
    higher = tuple(range(3, width))
    orders = ((1, 2) + higher, (2, 1) + higher)
    half_rows = block_rows.shape[0] // 2
    halves = [block_rows[None, :half_rows], block_rows[None, half_rows:]]
    table = reorder(share(small_row), member)[None]
    for level in range(width - 1):
        halves = [
            jnp.concatenate([half, swap(half, "dp", 1 << order[level])], 0)
            for half, order in zip(halves, orders)
        ]
    placed = []
    for half, order in zip(halves, orders):
        shaped = half.reshape((2,) * (width - 1) + half.shape[1:])
        dims = [width - 2 - order.index(bit) for bit in range(width - 1, 0, -1)]
        placed.append(shaped.transpose(dims + [width - 1, width]).reshape(half.shape))
    near = jnp.concatenate(placed, 1)
    both = jnp.stack([near, swap(near, "dp", 1)], 1).reshape((replicas,) + block_rows.shape)
    block_flat = reorder(both, place).reshape(-1, block_rows.shape[1])
    for bit in range(width):
        table = jnp.concatenate([table, swap(table, "dp", 1 << bit)], 0)
    return reorder(table, place).reshape(-1, small_row.shape[0]), block_flat


def position_table(places, row_width):
    column = jnp.arange(row_width)
    step_rate = jnp.exp(-(column // 2 * 2).astype(jnp.float32) * (math.log(10000.0) / row_width))
    angle = places.astype(jnp.float32)[..., None] * step_rate
    return jnp.where(column % 2 == 0, jnp.sin(angle), jnp.cos(angle))


def visible_slots(visible):
    slot_rank = jnp.cumsum(visible, 1) - 1
    select = (
        (visible[:, None, :] == 1) & (slot_rank[:, None, :] == jnp.arange(VIS)[None, :, None])
    ).astype(jnp.int32)
    slot_patch = jnp.sum(select * jnp.arange(visible.shape[1])[None, None, :], 2)
    key_valid = jnp.arange(VIS)[None, :] < jnp.sum(visible, 1)[:, None]
    return (select, slot_patch, key_valid)


def cut_pieces(flat_vector, shapes):
    pieces = []
    offset = 0
    for shape in shapes:
        length = math.prod(shape)
        pieces.append(flat_vector[offset : offset + length].reshape(shape))
        offset += length
    return pieces


def norm_forward(residual, gain_vec):
    center = residual - jnp.mean(residual, -1, keepdims=True)
    inverse = lax.rsqrt(jnp.mean(center * center, -1, keepdims=True) + 1e-06)
    normal_hat = center * inverse
    return (normal_hat * gain_vec, normal_hat, inverse)


def norm_backward(gradient, normal_hat, inverse, gain_vec):
    hat_grad = gradient * gain_vec
    residual_grad = inverse * (
        hat_grad
        - jnp.mean(hat_grad, -1, keepdims=True)
        - normal_hat * jnp.mean(hat_grad * normal_hat, -1, keepdims=True)
    )
    return (residual_grad, gradient * normal_hat)


def split_heads(packed, head_count):
    batch_size, length, row_width = packed.shape
    unpacked = packed.reshape(batch_size, length, 3, head_count, row_width // (3 * head_count))
    return (unpacked[:, :, 0], unpacked[:, :, 1], unpacked[:, :, 2])


def scores_of(query_part, key_part, key_valid, scaling):
    raw_scores = (
        jnp.einsum("blhd,bmhd->bhlm", query_part, key_part, preferred_element_type=jnp.float32)
        * scaling
    )
    return jnp.where(key_valid[:, None, None, :], raw_scores, -1e30)


def attend_forward(packed, key_valid, head_count, scaling):
    query_part, key_part, value_part = split_heads(packed, head_count)
    scores = scores_of(query_part, key_part, key_valid, scaling)
    row_top = jnp.max(scores, -1, keepdims=True)
    exponent = jnp.exp(scores - row_top)
    row_total = jnp.sum(exponent, -1, keepdims=True)
    probability = (exponent / row_total).astype(low_type)
    mixed_heads = jnp.einsum(
        "bhlm,bmhd->blhd", probability, value_part, preferred_element_type=jnp.float32
    )
    batch_size, length = (key_valid.shape[0], packed.shape[1])
    return (
        mixed_heads.reshape(batch_size, length, -1).astype(low_type),
        row_top + jnp.log(row_total),
    )


def attend_backward(packed, log_total, key_valid, mixed_grad, head_count, scaling):
    query_part, key_part, value_part = split_heads(packed, head_count)
    batch_size, length, row_width = mixed_grad.shape
    out_grad = mixed_grad.reshape(batch_size, length, head_count, -1)
    probability = jnp.exp(scores_of(query_part, key_part, key_valid, scaling) - log_total)
    value_grad = jnp.einsum(
        "bhlm,blhd->bmhd",
        probability.astype(low_type),
        out_grad,
        preferred_element_type=jnp.float32,
    )
    prob_grad = jnp.einsum(
        "blhd,bmhd->bhlm", out_grad, value_part, preferred_element_type=jnp.float32
    )
    score_grad = (
        probability * (prob_grad - jnp.sum(probability * prob_grad, -1, keepdims=True))
    ).astype(low_type)
    query_grad = (
        jnp.einsum("bhlm,bmhd->blhd", score_grad, key_part, preferred_element_type=jnp.float32)
        * scaling
    )
    key_grad = (
        jnp.einsum("bhlm,blhd->bmhd", score_grad, query_part, preferred_element_type=jnp.float32)
        * scaling
    )
    stacked = jnp.stack([query_grad, key_grad, value_grad], 2)
    return stacked.reshape(batch_size, length, -1).astype(low_type)


def cut_rows(rows, shapes):
    pieces = []
    offset = 0
    for shape in shapes:
        length = math.prod(shape) // 128
        pieces.append(rows[offset : offset + length].reshape(shape))
        offset += length
    return pieces


def mlp_backward(
    gradient, grad_low, activated, raised, inner_low, up_w, down_w, total_sum, norm_saved
):
    down_grad = outer_sum(activated, grad_low)
    act_grad = back_dot(grad_low, down_w)
    unused, gelu_back = jax.vjp(partial(jax.nn.gelu, approximate=True), raised)
    raised_grad = gelu_back(act_grad)[0].astype(low_type)
    up_grad = outer_sum(inner_low, raised_grad)
    inner_grad = total_sum(back_dot(raised_grad, up_w))
    normal_hat, inverse, gain_vec = norm_saved
    middle_part, second_terms = norm_backward(inner_grad, normal_hat, inverse, gain_vec)
    return (gradient + middle_part, down_grad, up_grad, second_terms)


def adamw(gradient, first_old, second_old, master, factor, step_rate, decay_rate):
    gradient = gradient * factor
    first_new = beta_one * first_old + (1 - beta_one) * gradient
    second_new = beta_two * second_old + (1 - beta_two) * gradient * gradient
    first_hat = first_new / (1 - beta_one**STEP)
    second_hat = second_new / (1 - beta_two**STEP)
    master_new = master - step_rate * (
        first_hat / (jnp.sqrt(second_hat) + adam_eps) + decay_rate * master
    )
    return (first_new, second_new, master_new, master_new.astype(jnp.bfloat16))


def low_rows(block_lanes, row_width):
    pieces = row_width // 128

    def kernel(block_ref, block_out):
        for piece in range(pieces):
            lanes = slice(piece * 128, (piece + 1) * 128)
            spots = pl.ds(piece, block_out.shape[0], stride=pieces)
            block_out[:, lanes] = block_ref[spots, :].astype(low_type)

    return pl.pallas_call(
        kernel,
        out_shape=jax.ShapeDtypeStruct((block_lanes.shape[0] // pieces, row_width), low_type),
        compiler_params=pltpu.CompilerParams(vmem_limit_bytes=8 * 2**20),
    )(block_lanes)


def adamw_of(gradient, first_old, second_old, master, step_rate, decay_rate):
    first_new = beta_one * first_old + (1 - beta_one) * gradient
    second_new = beta_two * second_old + (1 - beta_two) * gradient * gradient
    first_hat = first_new / (1 - beta_one**STEP)
    second_hat = second_new / (1 - beta_two**STEP)
    master_new = master - step_rate * (
        first_hat / (jnp.sqrt(second_hat) + adam_eps) + decay_rate * master
    )
    return (first_new, second_new, master_new, master_new.astype(low_type))


def update(factor, block_rows, block_state, shared_lanes, shared_state):
    pieces = block_rows.shape[1] // 128

    def kernel(factor_ref, *refs):
        block_grad, shared_grad = refs[0], refs[4]
        scale = factor_ref[0, 0]
        rows = block_grad.shape[0]
        block_in, block_to = refs[1:4], refs[8:12]
        shared_in, shared_to = refs[5:8], refs[12:16]
        for piece in range(pieces):
            spots = pl.ds(piece, rows, stride=pieces)
            gradient = block_grad[:, piece * 128 : (piece + 1) * 128] * scale
            results = adamw_of(
                gradient, *[ref[spots, :] for ref in block_in], rate_matrix, weight_decay
            )
            for ref, result in zip(block_to[:3], results[:3]):
                ref[spots, :] = result
        block_to[3][...] = block_to[2][...].astype(low_type).reshape(block_to[3].shape)
        results = adamw_of(
            shared_grad[...] * scale, *[ref[...] for ref in shared_in], rate_matrix, weight_decay
        )
        for ref, result in zip(shared_to, results):
            ref[...] = result

    kinds = (jnp.float32, jnp.float32, jnp.float32, low_type)
    shapes = [block_state[0].shape] * 4 + [shared_state[0].shape] * 4
    shapes[3] = (1, math.prod(shapes[3]))
    results = pl.pallas_call(
        kernel,
        in_specs=[pl.BlockSpec(memory_space=pltpu.SMEM)]
        + [pl.BlockSpec(memory_space=pltpu.VMEM)] * 8,
        out_shape=[jax.ShapeDtypeStruct(shape, kind) for shape, kind in zip(shapes, kinds * 2)],
        compiler_params=pltpu.CompilerParams(vmem_limit_bytes=20 * 2**20),
    )(factor.reshape(1, 1), block_rows, *block_state, shared_lanes, *shared_state)
    return (tuple(results[:4]), tuple(results[4:]))


TOKENS = 208
LANES = 128


def dot_tn(left_side, right_side):
    return lax.dot_general(
        left_side, right_side, (((0,), (0,)), ((), ())), preferred_element_type=jnp.float32
    )


def dot_nt(left_side, right_side):
    return lax.dot_general(
        left_side, right_side, (((1,), (1,)), ((), ())), preferred_element_type=jnp.float32
    )


def gelu_pair(raised):
    rate = math.sqrt(2.0 / math.pi)
    square = raised * raised
    curve = jnp.tanh(rate * (raised + 0.044715 * raised * square))
    half = 0.5 * (1.0 + curve)
    slope = half + 0.5 * raised * (1.0 - curve * curve) * rate * (1.0 + 0.134145 * square)
    return raised * half, slope


def unpack(lanes, first_entry, shapes):
    step = 64

    def kernel(lanes_ref, *refs):
        work = refs[-1]
        start = first_entry // LANES
        for out in refs[:-1]:
            depth, pieces = out.shape[0], out.shape[1] // LANES
            span = step * pieces

            def chunk(index, carry, out=out, start=start, pieces=pieces, span=span):
                source = pl.ds(pl.multiple_of(start + index * span, 64), span)
                work[:span, :] = lanes_ref[source, :].astype(jnp.float32)
                rows = pl.ds(pl.multiple_of(index * step, step), step)
                for piece in range(pieces):
                    out[rows, piece * LANES : (piece + 1) * LANES] = work[
                        pl.ds(piece, step, stride=pieces), :
                    ].astype(low_type)
                return carry

            lax.fori_loop(0, depth // step, chunk, 0)
            start += depth * pieces

    entries = sum(math.prod(shape) for shape in shapes)
    widest = max(shape[1] for shape in shapes)
    block = first_entry // LANES + entries // LANES
    return pl.pallas_call(
        kernel,
        grid=(1,),
        in_specs=[pl.BlockSpec((block, LANES), lambda index: (0, 0))],
        out_specs=[pl.BlockSpec(shape, lambda index: (0, 0)) for shape in shapes],
        out_shape=[jax.ShapeDtypeStruct(shape, low_type) for shape in shapes],
        scratch_shapes=[pltpu.VMEM((step * widest // LANES, LANES), jnp.float32)],
        compiler_params=pltpu.CompilerParams(vmem_limit_bytes=36 * 2**20),
        cost_estimate=pl.CostEstimate(flops=0, bytes_accessed=4 * entries, transcendentals=0),
    )(lanes)


def decoder_kernel(
    latent_rows,
    core_ref,
    scale_ref,
    final_ref,
    latent_ref,
    select_ref,
    mask_ref,
    table_ref,
    small_ref,
    pixels_ref,
    packed_w,
    out_w,
    up_w,
    down_w,
    head_w,
    sent_out,
    kept_out,
    latent_out,
    small_out,
    loss_out,
    grad_ref,
    copy_sems,
    work,
    packed_ref,
    mixed_ref,
    prob_ref,
    raised_ref,
    activated_ref,
    packed_grad_ref,
):
    scaling = (DD // DHEADS) ** (-0.5)
    width = DD // DHEADS
    per_block = LANES // width
    first_gain, second_gain, last_gain, mask_token = [
        small_ref[row : row + 1, :] for row in range(4)
    ]
    mask = mask_ref[...]
    select = select_ref[...]
    key_valid = lax.broadcasted_iota(jnp.int32, (TOKENS, TOKENS), 1) < PATCHES
    lane_head = lax.broadcasted_iota(jnp.int32, (TOKENS, LANES), 1) // width
    quarter = DMLP // 4

    tokens = forward_dot(select, latent_ref[...]) + mask * mask_token + table_ref[...]
    first_norm, first_hat, first_inverse = norm_forward(tokens, first_gain)
    normed = first_norm.astype(low_type)
    for piece in range(3):
        columns = slice(piece * DD, (piece + 1) * DD)
        packed_ref[:, columns] = forward_dot(normed, packed_w[:, columns]).astype(low_type)
    mixed_ref[...] = jnp.zeros(mixed_ref.shape, jnp.float32)

    def attend(head, carry):
        block = pl.multiple_of(head // per_block * LANES, LANES)
        inside = lane_head == head % per_block
        query = jnp.where(inside, packed_ref[:, pl.ds(block, LANES)], 0)
        key = packed_ref[:, pl.ds(DD + block, LANES)]
        value = packed_ref[:, pl.ds(2 * DD + block, LANES)]
        scores = jnp.where(key_valid, dot_nt(query, key) * scaling, -1e30)
        exponent = jnp.exp(scores - jnp.max(scores, -1, keepdims=True))
        probability = exponent / jnp.sum(exponent, -1, keepdims=True)
        prob_ref[head] = probability
        mixed = forward_dot(probability.astype(low_type), value)
        mixed_ref[:, pl.ds(block, LANES)] += jnp.where(inside, mixed, 0.0)
        return carry

    lax.fori_loop(0, DHEADS, attend, 0, unroll=8)
    mixed_low = mixed_ref[...].astype(low_type)
    middle = tokens + forward_dot(mixed_low, out_w[...])
    second_norm, second_hat, second_inverse = norm_forward(middle, second_gain)
    inner = second_norm.astype(low_type)
    decoded = middle
    for part in range(4):
        columns = slice(part * quarter, (part + 1) * quarter)
        raised = forward_dot(inner, up_w[:, columns])
        activated, slope = gelu_pair(raised)
        raised_ref[:, columns] = slope
        activated = activated.astype(low_type)
        activated_ref[:, columns] = activated
        decoded = decoded + forward_dot(activated, down_w[columns, :])
    top_norm, top_hat, top_inverse = norm_forward(decoded, last_gain)
    top = top_norm.astype(low_type)
    predicted = forward_dot(top, head_w[...])
    target = pixels_ref[...].astype(jnp.float32)
    center = target - jnp.mean(target, -1, keepdims=True)
    target = center * lax.rsqrt(jnp.mean(center * center, -1, keepdims=True) + 1e-06)
    errors = predicted - target
    loss_out[...] = jnp.sum(
        mask * jnp.mean(errors * errors, -1, keepdims=True), axis=0, keepdims=True
    )
    pred_grad = (errors * (mask * scale_ref[0, 0])).astype(low_type)

    starts = [PIX * D // LANES]
    for size in (3 * DD * DD, DD * DD, DD * DMLP, DMLP * DD):
        starts.append(starts[-1] + size // LANES)
    grad_ref[: starts[0], :] = jnp.zeros((starts[0], LANES), low_type)
    slot_rows = sent_out.shape[1]
    slots = 2 * sent_out.shape[0]
    core = core_ref[0, 0]
    copies = []

    def send_from(first_row, last_row):
        for slot in range(slots):
            if first_row <= slot * slot_rows < last_row:
                rows = grad_ref.at[pl.ds(slot * slot_rows, slot_rows), :]
                side = slot % 2
                pair = slot // 2

                def start(target, rows=rows, pair=pair, slot=slot):
                    pltpu.make_async_copy(rows, target.at[pair], copy_sems.at[slot]).start()

                pl.when(core == side)(partial(start, kept_out))
                pl.when(core != side)(partial(start, sent_out))
                copies.append(
                    pltpu.make_async_copy(rows, kept_out.at[pair], copy_sems.at[slot])
                )

    def put(left_side, right_ref_columns, pieces, base):
        depth = left_side.shape[1]
        for piece, columns in right_ref_columns:
            product = dot_tn(left_side, columns)
            for half in range(columns.shape[1] // LANES):
                work[pl.ds(base + piece + half, depth, stride=pieces), :] = product[
                    :, half * LANES : (half + 1) * LANES
                ]

    def flush(start, size):
        grad_ref[start : start + size, :] = work[:size, :].astype(low_type)
        send_from(start, start + size)

    def pairs_of(values):
        return [
            (2 * pair, values[:, 2 * pair * LANES : 2 * (pair + 1) * LANES])
            for pair in range(values.shape[1] // (2 * LANES))
        ]

    put(top, pairs_of(pred_grad), PIX // LANES, 0)
    flush(starts[4], DD * PIX // LANES)
    decoded_grad, last_terms = norm_backward(
        dot_nt(pred_grad, head_w[...]), top_hat, top_inverse, last_gain
    )
    grad_low = decoded_grad.astype(low_type)
    inner_grad = jnp.zeros((TOKENS, DD), jnp.float32)
    for part in range(4):
        columns = slice(part * quarter, (part + 1) * quarter)
        put(activated_ref[:, columns], pairs_of(grad_low), DD // LANES, part * quarter * DD // LANES)
    flush(starts[3], DMLP * DD // LANES)
    for part in range(4):
        columns = slice(part * quarter, (part + 1) * quarter)
        act_grad = dot_nt(grad_low, down_w[columns, :])
        raised_grad = (act_grad * raised_ref[:, columns]).astype(low_type)
        put(inner, pairs_of(raised_grad), DMLP // LANES, part * quarter // LANES)
        inner_grad = inner_grad + dot_nt(raised_grad, up_w[:, columns])
    flush(starts[2], DD * DMLP // LANES)
    middle_part, second_terms = norm_backward(inner_grad, second_hat, second_inverse, second_gain)
    middle_grad = decoded_grad + middle_part
    middle_low = middle_grad.astype(low_type)
    put(mixed_low, pairs_of(middle_low), DD // LANES, 0)
    flush(starts[1], DD * DD // LANES)
    mixed_ref[...] = dot_nt(middle_low, out_w[...])
    packed_grad_ref[...] = jnp.zeros(packed_grad_ref.shape, jnp.float32)

    def attend_back(head, carry):
        block = pl.multiple_of(head // per_block * LANES, LANES)
        inside = lane_head == head % per_block
        out_grad = mixed_ref[:, pl.ds(block, LANES)].astype(low_type)
        query = packed_ref[:, pl.ds(block, LANES)]
        key = packed_ref[:, pl.ds(DD + block, LANES)]
        value = packed_ref[:, pl.ds(2 * DD + block, LANES)]
        probability = prob_ref[head]
        value_grad = dot_tn(probability.astype(low_type), out_grad)
        prob_grad = dot_nt(jnp.where(inside, out_grad, 0), value)
        score_grad = (
            probability * (prob_grad - jnp.sum(probability * prob_grad, -1, keepdims=True))
        ).astype(low_type)
        query_grad = forward_dot(score_grad, key) * scaling
        key_grad = dot_tn(score_grad, query) * scaling
        for piece, values in enumerate((query_grad, key_grad, value_grad)):
            packed_grad_ref[:, pl.ds(piece * DD + block, LANES)] += jnp.where(inside, values, 0.0)
        return carry

    lax.fori_loop(0, DHEADS, attend_back, 0, unroll=8)
    normed_grad = jnp.zeros((TOKENS, DD), jnp.float32)
    for piece in range(3):
        columns = slice(piece * DD, (piece + 1) * DD)
        packed_low = packed_grad_ref[:, columns].astype(low_type)
        put(normed, pairs_of(packed_low), 3 * DD // LANES, piece * DD // LANES)
        normed_grad = normed_grad + dot_nt(packed_low, packed_w[:, columns])
    flush(starts[0], 3 * DD * DD // LANES)
    token_part, first_terms = norm_backward(normed_grad, first_hat, first_inverse, first_gain)
    token_grad = middle_grad + token_part
    latent_grad = dot_tn(select, token_grad.astype(low_type)).astype(low_type)
    latent_out[...] = latent_grad
    if latent_rows > 0:
        for part in range(slot_rows // latent_rows):
            columns = DD // (slot_rows // latent_rows)
            product = dot_tn(final_ref[...], latent_grad[:, part * columns : (part + 1) * columns])
            grad_ref[part * latent_rows : part * latent_rows + D, :] = product.astype(low_type)
    for row, terms in enumerate((first_terms, second_terms, last_terms, mask * token_grad)):
        small_out[row : row + 1, :] = jnp.sum(terms, axis=0, keepdims=True)
    send_from(0, starts[0])
    for copy in copies:
        copy.wait()


def decode(
    latent_rows, core, scale, final_low, latent, select, mask, table, small, pixels, weights, slots, slot_rows
):
    half = jax.ShapeDtypeStruct((slots // 2, slot_rows, LANES), low_type)
    return pl.pallas_call(
        partial(decoder_kernel, latent_rows),
        in_specs=[pl.BlockSpec(memory_space=pltpu.SMEM)] * 2
        + [pl.BlockSpec(memory_space=pltpu.VMEM)] * 12,
        out_specs=[pl.BlockSpec(memory_space=pltpu.HBM)] * 2
        + [pl.BlockSpec(memory_space=pltpu.VMEM)] * 3,
        out_shape=(
            half,
            half,
            jax.ShapeDtypeStruct(latent.shape, low_type),
            jax.ShapeDtypeStruct(small.shape, jnp.float32),
            jax.ShapeDtypeStruct((1, 1), jnp.float32),
        ),
        scratch_shapes=[
            pltpu.VMEM((slots * slot_rows, LANES), low_type),
            pltpu.SemaphoreType.DMA((slots,)),
            pltpu.VMEM((DD * DMLP // LANES, LANES), jnp.float32),
            pltpu.VMEM((TOKENS, 3 * DD), low_type),
            pltpu.VMEM((TOKENS, DD), jnp.float32),
            pltpu.VMEM((DHEADS, TOKENS, TOKENS), jnp.float32),
            pltpu.VMEM((TOKENS, DMLP), jnp.float32),
            pltpu.VMEM((TOKENS, DMLP), low_type),
            pltpu.VMEM((TOKENS, 3 * DD), jnp.float32),
        ],
        compiler_params=pltpu.CompilerParams(vmem_limit_bytes=36 * 2**20),
        cost_estimate=pl.CostEstimate(
            flops=6 * TOKENS * slots * slot_rows * LANES,
            bytes_accessed=4 * slots * slot_rows * LANES,
            transcendentals=TOKENS * (DMLP + DHEADS * TOKENS),
        ),
    )(core, scale, final_low, latent, select, mask, table, small, pixels, *weights)


def cut_spans(rows_of, slots, slot_rows):
    spans = []
    start = 0
    for source, rows in enumerate(rows_of):
        for slot in range(slots):
            first = max(start, slot * slot_rows)
            last = min(start + rows, (slot + 1) * slot_rows)
            if first < last:
                spans.append((source, first - start, slot, first - slot * slot_rows, last - first))
        start += rows
    return spans


def move_spans(core, spans, sources, sent, kept, sems):
    def move(number, target):
        source, first, slot, place, size = spans[number]
        return pltpu.make_async_copy(
            sources[source].at[pl.ds(first, size), :],
            target.at[slot // 2, pl.ds(place, size), :],
            sems.at[number],
        )

    for number, span in enumerate(spans):
        side = span[2] % 2
        pl.when(core == side)(lambda number=number: move(number, kept).start())
        pl.when(core != side)(lambda number=number: move(number, sent).start())
    for number in range(len(spans)):
        move(number, kept).wait()


def smem(value):
    return value.reshape(1, 1)


def run_kernel(kernel, tokens, arguments, outputs, scratch=(), flops=0, scalars=0, saved=0):
    count = len(tokens)
    held = arguments[len(arguments) - saved :]

    def body(*refs):
        refs = refs[count:]
        sources = refs[len(arguments) - saved : len(arguments)]
        given, rest = refs[: len(arguments) - saved], refs[len(arguments) :]
        results, rest = rest[: len(outputs)], rest[len(outputs) :]
        own, local = rest[: len(scratch)], rest[len(scratch) :][:saved]
        if saved:
            sems = rest[-1]
            copies = [
                pltpu.make_async_copy(source, target, sems.at[number])
                for number, (source, target) in enumerate(zip(sources, local))
            ]
            for copy in copies:
                copy.start()
            for copy in copies:
                copy.wait()
        kernel(*given, *local, *results, *own)

    return pl.pallas_call(
        body,
        in_specs=[pl.BlockSpec(memory_space=pl.ANY)] * count
        + [pl.BlockSpec(memory_space=pltpu.SMEM)] * scalars
        + [pl.BlockSpec(memory_space=pltpu.VMEM)] * (len(arguments) - scalars - saved)
        + [pl.BlockSpec(memory_space=pltpu.HBM)] * saved,
        out_specs=[pl.BlockSpec(memory_space=pltpu.VMEM)] * len(outputs),
        out_shape=[jax.ShapeDtypeStruct(shape, kind) for shape, kind in outputs],
        scratch_shapes=list(scratch)
        + [pltpu.VMEM(array.shape, array.dtype) for array in held]
        + [pltpu.SemaphoreType.DMA((saved,))] * (saved > 0),
        compiler_params=pltpu.CompilerParams(vmem_limit_bytes=16 * 2**20),
        cost_estimate=pl.CostEstimate(flops=flops, bytes_accessed=2**20, transcendentals=0),
    )(*tokens, *arguments)


def put_terms(terms, outs):
    for place, out in enumerate(outs):
        out[...] = terms[place * VIS : (place + 1) * VIS].astype(out.dtype)


def term_outputs(groups):
    return [((VIS, D), jnp.float32)] + [((VIS, D), low_type)] * (groups - 1)


def sum_terms(refs):
    total = refs[0][...]
    for ref in refs[1:]:
        total = total + ref[...].astype(jnp.float32)
    return total


def join(refs):
    return jnp.concatenate([ref[...] for ref in refs], 0)


def exchange(terms):
    return [terms[0]] + [swap(terms[step], "mp", step) for step in range(1, len(terms))]


def spread(values):
    groups = lax.axis_size("mp")
    return [values] + [swap(values, "mp", step) for step in range(1, groups)]


def head_lanes(rows, columns):
    return lax.broadcasted_iota(jnp.int32, (rows, columns), 1) // (D // HEADS)


def enter_encoder(seen, patch_w, table, gain, packed_w, out_w, valid):
    groups = lax.axis_size("mp")
    rows, columns = groups * VIS, D // groups
    heads = HEADS // groups
    scaling = (D // HEADS) ** (-0.5)

    def kernel(seen, patch_w, table, gain, packed_w, out_w, valid, *outs):
        residual_out, hat_out, inverse_out, normed_out, packed_out, prob_out, mixed_out = outs[:7]
        residual = forward_dot(seen[...], patch_w[...]) + table[...]
        norm, hat, inverse = norm_forward(residual, gain[...])
        residual_out[...] = residual[:VIS]
        hat_out[...] = hat[:VIS]
        inverse_out[...] = jnp.broadcast_to(inverse[:VIS], (VIS, LANES))
        normed = norm.astype(low_type)
        normed_out[...] = normed
        packed = forward_dot(normed, packed_w[...]).astype(low_type)
        packed_out[...] = packed
        query, key, value = [packed[:, third * columns : (third + 1) * columns] for third in range(3)]
        one = lax.broadcasted_iota(jnp.int32, (rows, rows), 0) // VIS
        other = lax.broadcasted_iota(jnp.int32, (rows, rows), 1) // VIS
        allowed = (one == other) & (valid[...] > 0.5)
        lanes = head_lanes(rows, columns)
        mixed = jnp.zeros((rows, columns), jnp.float32)
        for head in range(heads):
            inside = lanes == head
            scores = dot_nt(jnp.where(inside, query, 0), key) * scaling
            scores = jnp.where(allowed, scores, -1e30)
            exponent = jnp.exp(scores - jnp.max(scores, -1, keepdims=True))
            probability = exponent / jnp.sum(exponent, -1, keepdims=True)
            prob_out[head] = probability
            mixed = mixed + jnp.where(inside, forward_dot(probability.astype(low_type), value), 0.0)
        mixed_low = mixed.astype(low_type)
        mixed_out[...] = mixed_low
        put_terms(forward_dot(mixed_low, out_w[...]), outs[7:])

    outputs = [
        ((VIS, D), jnp.float32),
        ((VIS, D), jnp.float32),
        ((VIS, LANES), jnp.float32),
        ((rows, D), low_type),
        ((rows, 3 * columns), low_type),
        ((heads, rows, rows), jnp.float32),
        ((rows, columns), low_type),
    ] + term_outputs(groups)
    results = run_kernel(
        kernel, [], [seen, patch_w, table, gain, packed_w, out_w, valid], outputs, flops=10**9
    )
    return results[:7], results[7:]


def norm_of_sum(terms, residual, gain):
    count = len(terms)

    def kernel(*refs):
        residual, gain = refs[count : count + 2]
        sum_out, low_out, hat_out, inverse_out = refs[count + 2 :]
        total = residual[...] + sum_terms(refs[:count])
        norm, hat, inverse = norm_forward(total, gain[...])
        sum_out[...] = total
        low_out[...] = norm.astype(low_type)
        hat_out[...] = hat
        inverse_out[...] = jnp.broadcast_to(inverse, (VIS, LANES))

    outputs = [
        ((VIS, D), jnp.float32),
        ((VIS, D), low_type),
        ((VIS, D), jnp.float32),
        ((VIS, LANES), jnp.float32),
    ]
    return run_kernel(kernel, [], [*terms, residual, gain], outputs)


def raise_and_lower(inner, up_w, down_w):
    groups = len(inner)

    def kernel(*refs):
        up_w, down_w, inner_out = refs[groups : groups + 3]
        inner = join(refs[:groups])
        inner_out[...] = inner
        activated, slope = gelu_pair(forward_dot(inner, up_w[...]))
        put_terms(forward_dot(activated.astype(low_type), down_w[...]), refs[groups + 3 :])

    outputs = [((groups * VIS, D), low_type)] + term_outputs(groups)
    results = run_kernel(kernel, [], [*inner, up_w, down_w], outputs, flops=6 * 10**8)
    return results[0], results[1:]


def latent_of_sum(tokens, terms, residual, gain, latent_w):
    count = len(terms)

    def kernel(*refs):
        residual, gain, latent_w, low_out, hat_out, inverse_out, latent_out = refs[count:]
        norm, hat, inverse = norm_forward(residual[...] + sum_terms(refs[:count]), gain[...])
        final_low = norm.astype(low_type)
        low_out[...] = final_low
        hat_out[...] = hat
        inverse_out[...] = jnp.broadcast_to(inverse, (VIS, LANES))
        columns = latent_w.shape[2]
        for place in range(count):
            latent_out[:, place * columns : (place + 1) * columns] = forward_dot(
                final_low, latent_w[place]
            ).astype(low_type)

    outputs = [
        ((VIS, D), low_type),
        ((VIS, D), jnp.float32),
        ((VIS, LANES), jnp.float32),
        ((VIS, DD), low_type),
    ]
    return run_kernel(kernel, tokens, [*terms, residual, gain, latent_w], outputs)


def latent_back(tokens, member, along, latent_grad, latent_w, hat, inverse, gain):
    groups, rows, columns = latent_w.shape

    def kernel(member, latent_grad, latent_w, hat, inverse, gain, grad_out, gain_out, work, *outs):
        total = jnp.zeros((VIS, D), jnp.float32)
        for place in range(groups):
            cut = latent_grad[:, place * columns : (place + 1) * columns]
            work[place] = cut
            total = total + dot_nt(cut, latent_w[place])
        gradient, terms = norm_backward(total, hat[...], inverse[:, :1], gain[...])
        grad_out[...] = gradient
        for step, out in enumerate(outs):
            out[:, :D] = gradient.astype(low_type)
            if not along:
                out[:, D:] = work[member[0, 0] ^ step]
        gain_out[...] = jnp.sum(terms, axis=0, keepdims=True)

    outputs = [((VIS, D), jnp.float32), ((1, D), jnp.float32), ((groups, VIS, columns), low_type)]
    outputs += [((VIS, D + (0 if along else columns)), low_type)] * groups
    results = run_kernel(
        kernel,
        tokens,
        [smem(member), latent_grad, latent_w, hat, inverse, gain],
        outputs,
        scalars=1,
    )
    return results[0], results[1], results[3:]


def norm_back_of_sum(tokens, terms, upstream, hat, inverse, gain):
    count = len(terms)

    def kernel(*refs):
        upstream, hat, inverse, gain, grad_out, low_out, gain_out = refs[count:]
        part, gain_terms = norm_backward(
            sum_terms(refs[:count]), hat[...], inverse[:, :1], gain[...]
        )
        gradient = upstream[...] + part
        grad_out[...] = gradient
        low_out[...] = gradient.astype(low_type)
        gain_out[...] = jnp.sum(gain_terms, axis=0, keepdims=True)

    outputs = [((VIS, D), jnp.float32), ((VIS, D), low_type), ((1, D), jnp.float32)]
    return run_kernel(kernel, tokens, [*terms, upstream, hat, inverse, gain], outputs)


def mlp_back(tokens, core, grads, finals, inner, up_w, down_w, slots, slot_rows, first_row):
    groups = len(grads)
    embed_cols = grads[0].shape[1] - D
    count = len(tokens)
    given = groups + len(finals)
    spans = cut_spans([first_row, up_w.shape[0], down_w.shape[0]], slots, slot_rows)
    spans = [span for span in spans if span[0] > 0]

    def kernel(*refs):
        core, refs = refs[count], refs[count + 1 :]
        sources = refs[given : given + 3]
        outs = refs[given + 3 :]
        *outs, inner, up_w, down_w, load_sems = outs
        copies = [
            pltpu.make_async_copy(source, target, load_sems.at[number])
            for number, (source, target) in enumerate(zip(sources, (inner, up_w, down_w)))
        ]
        for copy in copies:
            copy.start()
        for copy in copies:
            copy.wait()
        both = join(refs[:groups])
        grad_low = both[:, :D]
        inner_low = inner[...]
        activated, slope = gelu_pair(forward_dot(inner_low, up_w[...]))
        raised_grad = (dot_nt(grad_low, down_w[...]) * slope).astype(low_type)
        put_terms(dot_nt(raised_grad, up_w[...]), outs[2 : 2 + groups])
        down_grad = dot_tn(activated.astype(low_type), grad_low).astype(low_type)
        up_grad = dot_tn(inner_low, raised_grad).astype(low_type)
        if slots > 0:
            up_work, down_work, sems = outs[2 + groups :][-3:]
            up_work[...] = up_grad
            down_work[...] = down_grad
            move_spans(core[0, 0], spans, [None, up_work, down_work], outs[0], outs[1], sems)
        else:
            outs[0][...] = up_grad
            outs[1][...] = down_grad
        if embed_cols > 0:
            final_low = join(refs[groups:given])
            outs[2 + groups][...] = dot_tn(final_low, both[:, D:]).astype(low_type)

    space = pltpu.VMEM
    shapes = [up_w.shape, down_w.shape]
    scratch = []
    if slots > 0:
        space = pltpu.HBM
        shapes = [(slots // 2, slot_rows, D)] * 2
        scratch = [
            pltpu.VMEM(up_w.shape, low_type),
            pltpu.VMEM(down_w.shape, low_type),
            pltpu.SemaphoreType.DMA((len(spans),)),
        ]
    outputs = [(shape, low_type) for shape in shapes] + term_outputs(groups)
    if embed_cols > 0:
        outputs.append(((D, embed_cols), low_type))
    results = pl.pallas_call(
        kernel,
        in_specs=[pl.BlockSpec(memory_space=pl.ANY)] * count
        + [pl.BlockSpec(memory_space=pltpu.SMEM)]
        + [pl.BlockSpec(memory_space=pltpu.VMEM)] * given
        + [pl.BlockSpec(memory_space=pltpu.HBM)] * 3,
        out_specs=[pl.BlockSpec(memory_space=space)] * 2
        + [pl.BlockSpec(memory_space=pltpu.VMEM)] * (len(outputs) - 2),
        out_shape=[jax.ShapeDtypeStruct(shape, kind) for shape, kind in outputs],
        scratch_shapes=scratch
        + [pltpu.VMEM(array.shape, low_type) for array in (inner, up_w, down_w)]
        + [pltpu.SemaphoreType.DMA((3,))],
        compiler_params=pltpu.CompilerParams(vmem_limit_bytes=16 * 2**20),
        cost_estimate=pl.CostEstimate(flops=15 * 10**8, bytes_accessed=2**20, transcendentals=0),
    )(*tokens, smem(core), *grads, *finals, inner, up_w, down_w)
    return results[:2], results[2 : 2 + groups], results[2 + groups :]


def attend_back(tokens, grad_low, normed, packed, prob, mixed, packed_w, out_w):
    groups = len(grad_low)
    rows, columns = groups * VIS, D // groups
    heads = HEADS // groups
    scaling = (D // HEADS) ** (-0.5)

    def kernel(*refs):
        normed, packed, prob, mixed, packed_w, out_w, packed_out, out_out = refs[
            groups : groups + 8
        ]
        grad_low = join(refs[:groups])
        mixed_grad = dot_nt(grad_low, out_w[...]).astype(low_type)
        query, key, value = [packed[:, third * columns : (third + 1) * columns] for third in range(3)]
        lanes = head_lanes(rows, columns)
        totals = [jnp.zeros((rows, columns), jnp.float32)] * 3
        for head in range(heads):
            inside = lanes == head
            probability = prob[head]
            value_grad = dot_tn(probability.astype(low_type), mixed_grad)
            prob_grad = dot_nt(jnp.where(inside, mixed_grad, 0), value)
            score_grad = (
                probability * (prob_grad - jnp.sum(probability * prob_grad, -1, keepdims=True))
            ).astype(low_type)
            query_grad = forward_dot(score_grad, key) * scaling
            key_grad = dot_tn(score_grad, query) * scaling
            totals = [
                total + jnp.where(inside, values, 0.0)
                for total, values in zip(totals, (query_grad, key_grad, value_grad))
            ]
        packed_grad = jnp.concatenate(totals, 1).astype(low_type)
        put_terms(dot_nt(packed_grad, packed_w[...]), refs[groups + 8 :])
        out_out[...] = dot_tn(mixed[...], grad_low).astype(low_type)
        packed_out[...] = dot_tn(normed[...], packed_grad).astype(low_type)

    outputs = [(packed_w.shape, low_type), (out_w.shape, low_type)] + term_outputs(groups)
    results = run_kernel(
        kernel,
        tokens,
        [*grad_low, normed, packed, prob, mixed, packed_w, out_w],
        outputs,
        flops=10**9,
        saved=6,
    )
    return results[:2], results[2:]


def last_norm_back(tokens, terms, upstream, hat, inverse, gain, second_gain, last_gain, dec_small):
    count = len(terms)

    def kernel(*refs):
        upstream, hat, inverse, gain, second_gain, last_gain, dec_small, low_out, work = refs[count:]
        part, gain_terms = norm_backward(
            sum_terms(refs[:count]), hat[...], inverse[:, :1], gain[...]
        )
        low_out[:VIS, :] = (upstream[...] + part).astype(low_type)
        work[...] = jnp.zeros(work.shape, jnp.float32)
        work[0:1, :] = jnp.sum(gain_terms, axis=0, keepdims=True)
        work[1:2, :] = second_gain[...]
        work[2:3, :] = last_gain[...]
        work[3:7, :DD] = dec_small[:4, :]
        values = work[...]
        high = values.astype(low_type)
        rest = (values - high.astype(jnp.float32)).astype(low_type)
        low_out[VIS:, :] = jnp.concatenate([high, rest], 0)

    return run_kernel(
        kernel,
        tokens,
        [*terms, upstream, hat, inverse, gain, second_gain, last_gain, dec_small],
        [((VIS + 16, D), low_type)],
        [pltpu.VMEM((8, D), jnp.float32)],
    )[0]


def patch_back(tokens, member, core, seen, grads, row_count):
    groups = len(grads)
    tail = PIX - groups * row_count
    early = 0 < tail <= row_count

    def kernel(member, core, seen, *refs):
        kept_out, sent_out, work = refs[groups:]
        rows_low = jnp.concatenate([ref[:VIS, :] for ref in refs[:groups]], 0)
        gains = jnp.zeros((8, D), jnp.float32)
        for ref in refs[:groups]:
            parts = ref[VIS:, :].astype(jnp.float32)
            gains = gains + (parts[:8] + parts[8:])
        if early:
            work[:PIX, :] = dot_tn(seen[...], rows_low)
            work[PIX:, :] = jnp.zeros((work.shape[0] - PIX, D), jnp.float32)
            rows = work[pl.ds(pl.multiple_of(member[0, 0] * row_count, 8), row_count), :]
            last = work[PIX - tail : PIX - tail + row_count, :]
            even = core[0, 0] == 0
            kept_out[:row_count, :] = jnp.where(even, rows, last)
            sent_out[:row_count, :] = jnp.where(even, last, rows)
        kept_out[kept_out.shape[0] - 8 :, :] = gains
        sent_out[sent_out.shape[0] - 8 :, :] = gains

    rows = row_count if early else 0
    return run_kernel(
        kernel,
        tokens,
        [smem(member), smem(core), seen, *grads],
        [((rows + 8, D), jnp.float32)] * 2,
        [pltpu.VMEM((PIX + row_count, D), jnp.float32)],
        4 * 10**8,
        2,
    )


def pack_block(tokens, core, packed_grad, out_grad, sent, kept):
    depth, columns = packed_grad.shape
    pair = depth // 2
    nine = 2 * columns // LANES
    six = D // LANES
    count = len(tokens)
    tiles = (columns + LANES - 1) // LANES
    slots, slot_rows = 2 * sent.shape[0], sent.shape[1]
    hidden_rows = 2 * D
    rows_of = [depth * columns // D, out_grad.shape[0], hidden_rows]
    rows_of.append(slots * slot_rows - sum(rows_of))
    spans = [span for span in cut_spans(rows_of, slots, slot_rows) if span[0] != 2]
    late = [span for span in spans if span[0] == 0]
    soon = [span for span in spans if span[0] != 0]

    def kernel(*refs):
        core, packed, out_grad, sent_in, kept_in, sent_out, kept_out = refs[count : count + 7]
        wide, flat, rows, zeros, out_work, late_sems, soon_sems = refs[count + 7 :]
        zeros[...] = jnp.zeros(zeros.shape, low_type)
        out_work[...] = out_grad[...]
        halves = []
        for tile in range(tiles):
            lanes = min(LANES, columns - tile * LANES)
            wide[tile * depth : (tile + 1) * depth, :lanes] = packed[
                :, tile * LANES : tile * LANES + lanes
            ].astype(jnp.float32)
        for side in range(2):
            pieces = [wide[pl.ds(tile * depth + side, pair, stride=2), :] for tile in range(tiles)]
            halves.append(jnp.concatenate(pieces, 1)[:, :columns])
        both = jnp.concatenate(halves, 1)
        for tile in range(nine):
            flat[pl.ds(tile, pair, stride=nine), :] = both[:, tile * LANES : (tile + 1) * LANES]
        for piece in range(six):
            rows[:, piece * LANES : (piece + 1) * LANES] = flat[
                pl.ds(piece, rows.shape[0], stride=six), :
            ].astype(low_type)
        sources = [rows, out_work, None, zeros]
        move_spans(core[0, 0], late + soon, sources, sent_out, kept_out, late_sems)

    return pl.pallas_call(
        kernel,
        in_specs=[pl.BlockSpec(memory_space=pl.ANY)] * count
        + [pl.BlockSpec(memory_space=pltpu.SMEM)]
        + [pl.BlockSpec(memory_space=pltpu.VMEM)] * 2
        + [pl.BlockSpec(memory_space=pltpu.HBM)] * 2,
        out_specs=[pl.BlockSpec(memory_space=pltpu.HBM)] * 2,
        out_shape=[jax.ShapeDtypeStruct(sent.shape, low_type)] * 2,
        input_output_aliases={count + 3: 0, count + 4: 1},
        scratch_shapes=[
            pltpu.VMEM((tiles * depth, LANES), jnp.float32),
            pltpu.VMEM((pair * nine, LANES), jnp.float32),
            pltpu.VMEM((rows_of[0], D), low_type),
            pltpu.VMEM((rows_of[-1], D), low_type),
            pltpu.VMEM(out_grad.shape, low_type),
            pltpu.SemaphoreType.DMA((len(spans),)),
            pltpu.SemaphoreType.DMA((len(spans),)),
        ],
        compiler_params=pltpu.CompilerParams(vmem_limit_bytes=16 * 2**20),
        cost_estimate=pl.CostEstimate(flops=0, bytes_accessed=8 * 2**20, transcendentals=0),
    )(*tokens, smem(core), packed_grad, out_grad, sent, kept)


def close_shared(tokens, place, owner, arrived, patch_rows):
    groups, lane_rows, lanes = arrived.shape
    pieces = patch_rows.shape[1] // LANES

    def kernel(place, owner, arrived, patch_rows, shared_out, latent_out, square_out, work):
        total = arrived[0].astype(jnp.float32)
        for member in range(1, groups):
            total = total + arrived[member].astype(jnp.float32)
        latent_out[...] = total[:D]
        for piece in range(pieces):
            work[pl.ds(piece, patch_rows.shape[0], stride=pieces), :] = patch_rows[
                :, piece * LANES : (piece + 1) * LANES
            ]
        patch = jnp.where(owner[0, 0] == 1, work[...], 0.0)
        total = jnp.where(place[0, 0] == 0, 0.0, total) + patch
        shared_out[...] = total
        squares = jnp.sum(total * total, axis=0, keepdims=True)
        square_out[...] = jnp.sum(squares, axis=1, keepdims=True)

    return run_kernel(
        kernel,
        tokens,
        [smem(place), smem(owner), arrived, patch_rows],
        [((lane_rows, lanes), jnp.float32), ((D, lanes), jnp.float32), ((1, 1), jnp.float32)],
        [pltpu.VMEM((lane_rows, lanes), jnp.float32)],
        scalars=2,
    )


def close_block(halves, latent):
    rows = [half.shape[0] for half in halves]
    pieces = D // LANES
    latent_rows = latent.shape[0] // pieces

    def kernel(one, two, latent, block_out, square_out):
        block_out[: rows[0], :] = one[...]
        block_out[rows[0] :, :] = two[...]
        last = slice(sum(rows) - latent_rows, sum(rows))
        for piece in range(pieces):
            block_out[last, piece * LANES : (piece + 1) * LANES] += latent[
                pl.ds(piece, latent_rows, stride=pieces), :
            ]
        total = block_out[...]
        squares = jnp.sum(total * total, axis=0, keepdims=True)
        square_out[...] = jnp.sum(squares, axis=1, keepdims=True)

    return run_kernel(
        kernel,
        [],
        [*halves, latent],
        [((sum(rows), D), jnp.float32), ((1, 1), jnp.float32)],
    )


def on_device(
    pixels,
    visible,
    block_master,
    block_first,
    block_second,
    shared_master,
    shared_first,
    shared_second,
    gains_master,
    gains_first,
    gains_second,
):
    groups = lax.axis_size("mp")
    replicas = lax.axis_size("dp")
    member = lax.axis_index("mp")
    model_cols = D // groups
    mlp_cols = MLP // groups
    embed_cols = DD // groups
    block_rows = block_master.shape[1] // D
    shared_rows = shared_master.shape[0] // 128

    own_pixels = pick(pixels, member, 0)
    own_visible = pick(visible, member, 0)
    hidden_mask = (1 - own_visible).astype(jnp.float32)
    hidden_count = jnp.sum(1 - own_visible).astype(jnp.float32)

    block_lanes = block_master.reshape(-1, 128)
    shared_lanes = shared_master.reshape(-1, 128)
    shared_low = shared_lanes.astype(low_type)
    block_rowed = low_rows(block_lanes, D)
    shared_flat = lax.all_gather(shared_low, ("dp", "mp"), axis=0).reshape(-1, 128)

    patch_size = PIX * D
    head_rows = shared_master.shape[0] // D
    tail_length = patch_size - groups * head_rows * D
    early = 0 < tail_length <= shared_master.shape[0] and groups * head_rows < PIX
    small_length = gains_master.shape[0]
    small_row = jnp.concatenate([lax.reduce_precision(gains_master, 8, 7), hidden_count[None]])
    small_row = jnp.pad(small_row, (0, -small_row.shape[0] % 128))
    near_visible = reorder(visible, member)
    near_pixels = reorder(pixels, member)
    select, slot_patch, key_valid = visible_slots(near_visible)
    chosen = (slot_patch[:, :, None] == jnp.arange(PATCHES)[None, None, :]).astype(low_type)
    seen_patches = jnp.einsum(
        "isp,ipd->isd", chosen, near_pixels, preferred_element_type=jnp.float32
    ).astype(low_type)
    small_table, block_flat = gather_early(small_row, block_rowed)
    gain_flat = small_table[:, :small_length].reshape(-1)
    count_total = jnp.sum(small_table[:, small_length])

    bounds = [0, 3 * model_cols, model_cols, mlp_cols, mlp_cols, embed_cols]
    bounds = [sum(bounds[: place + 1]) for place in range(len(bounds))]
    enc_packed, enc_out, enc_up, enc_down, enc_latent = [
        block_flat[low:high] for low, high in zip(bounds[:-1], bounds[1:])
    ]
    enc_packed = enc_packed.reshape(D, 3 * model_cols)
    enc_up = enc_up.reshape(D, mlp_cols)
    own_latent_w = enc_latent.reshape(D, embed_cols)

    (patch_w,) = unpack(shared_flat, 0, [(PIX, D)])
    dec_weights = unpack(
        shared_flat, PIX * D, [(DD, 3 * DD), (DD, DD), (DD, DMLP), (DMLP, DD), (DD, PIX)]
    )
    enc_one, enc_two, enc_last, dec_one, dec_two, dec_last, mask_token = cut_pieces(
        gain_flat, [(D,), (D,), (D,), (DD,), (DD,), (DD,), (DD,)]
    )

    latent_w = reorder(share_by_core(own_latent_w), member)
    saved, terms = enter_encoder(
        seen_patches.reshape(-1, PIX),
        patch_w,
        position_table(slot_patch, D).reshape(-1, D),
        enc_one[None],
        enc_packed,
        enc_out,
        key_valid.astype(jnp.float32).reshape(1, -1),
    )
    residual, first_hat, first_inverse, normed, packed, prob, mixed_heads = saved
    middle, inner_low, second_hat, second_inverse = norm_of_sum(
        exchange(terms), residual, enc_two[None]
    )
    inner_low = spread(inner_low)
    inner_low, terms = raise_and_lower(inner_low, enc_up, enc_down)
    final_low, final_hat, final_inverse, latent = latent_of_sum(
        [], exchange(terms), middle, enc_last[None], latent_w
    )

    pad = ((0, TOKENS - PATCHES), (0, 0))
    place = lax.axis_index("dp")
    along = early and shared_rows >= D and bounds[4] >= (replicas - 1) * block_rows
    along = along and block_rows % 16 == 0
    sent_grad, kept_grad, latent_grad, dec_small, loss_local = decode(
        shared_rows if along else 0,
        (place & 1).reshape(1, 1),
        (2.0 / (PIX * count_total)).reshape(1, 1),
        final_low,
        latent,
        jnp.pad(select[0].T.astype(low_type), pad),
        jnp.pad(hidden_mask[:, None], pad),
        jnp.pad(position_table(jnp.arange(PATCHES), DD), pad),
        jnp.pad(jnp.stack([dec_one, dec_two, dec_last, mask_token]), ((0, 4), (0, 0))),
        jnp.pad(own_pixels, pad),
        dec_weights,
        replicas,
        groups * shared_rows,
    )
    loss_local = loss_local[0, 0]
    got_grad = swap(sent_grad, "dp", 1)

    encoded_grad, enc_last_grad, encoded_low = latent_back(
        [], member, along, latent_grad, latent_w, final_hat, final_inverse, enc_last[None]
    )
    (up_grad, down_grad), terms, latent_wgrad = mlp_back(
        [],
        place & 1,
        exchange(encoded_low),
        [] if along else spread(final_low),
        inner_low,
        enc_up,
        enc_down,
        replicas if along else 0,
        block_rows,
        bounds[2],
    )
    terms = exchange(terms)
    column_totals, column_first = first_stage(kept_grad, after_all(got_grad, terms[1:]))
    middle_grad, middle_low, enc_two_grad = norm_back_of_sum(
        [], terms, encoded_grad, second_hat, second_inverse, enc_two[None]
    )
    (packed_grad, out_grad), terms = attend_back(
        column_first, spread(middle_low), normed, packed, prob, mixed_heads, enc_packed, enc_out
    )
    terms = exchange(terms)
    if along:
        sent_block, kept_block = pack_block(
            terms[1:], place & 1, packed_grad, out_grad, up_grad, down_grad
        )
        block_totals, block_sent = first_stage(kept_block, swap(sent_block, "dp", 1))
    else:
        block_grad = jnp.concatenate(
            [
                piece.reshape(-1, D)
                for piece in (packed_grad, out_grad, up_grad, down_grad, latent_wgrad[0])
            ]
        )
        block_share = reduce_dp(block_grad.reshape(replicas, block_rows, D))
        block_sent = []
    column_halves, column_last = later_stages(column_totals, terms[1:])
    column_share = jnp.concatenate(column_halves, 0)
    residual_low = last_norm_back(
        [],
        terms,
        middle_grad,
        first_hat,
        first_inverse,
        enc_one[None],
        enc_two_grad,
        enc_last_grad,
        dec_small,
    )

    residual_all = spread(residual_low)
    kept, sent = patch_back(
        block_sent,
        member,
        place & 1,
        seen_patches.reshape(-1, PIX),
        residual_all,
        head_rows,
    )
    column_share = column_share.reshape(groups, shared_rows, 128).astype(low_type)
    arrived = to_members(column_share)
    total = kept + swap(sent, "dp", 1)
    gain_rows = total[-8:]
    if early:
        total = total[:-8]
        total_low = total.astype(low_type)
        for dp in range(2, replicas, 2):
            pairs = [(dp * groups + mp, mp) for mp in range(groups)] + [((dp + 1) * groups, groups)]
            total = total + pair_permute(total_low, pairs).astype(jnp.float32)
        owner = (place == 0) | ((place == 1) & (member == 0))
        gain_rows = sum_chips(gain_rows)
        if along:
            block_halves, block_last = later_stages(block_totals)
            shared_share, latent_share, shared_square = close_shared(
                [], place, owner.astype(jnp.int32), arrived, total
            )
            latent_share = lax.ppermute(latent_share, "dp", [(0, replicas - 1)])
            block_share, block_square = close_block(block_halves, latent_share)
            squares = block_square[0, 0] + shared_square[0, 0]
        else:
            shared_share = jnp.sum(arrived.astype(jnp.float32), 0)
            shared_share = shared_share + jnp.where(owner, total.reshape(-1, 128), 0.0)
    else:
        patch_rows = outer_sum(seen_patches[0], residual_low[:VIS])
        patch_rows = patch_rows.astype(low_type).reshape(-1, 128)
        patch_rows = jnp.pad(patch_rows, ((0, shared_flat.shape[0] - patch_rows.shape[0]), (0, 0)))
        column = reduce_dp(patch_rows.reshape(replicas, groups * shared_rows, 128))
        column = column.reshape(groups, shared_rows, 128).astype(low_type)
        shared_share = jnp.sum(arrived.astype(jnp.float32), 0)
        shared_share = shared_share + jnp.sum(to_members(column).astype(jnp.float32), 0)
        gain_rows = sum_chips(gain_rows)
    pad_length = gain_flat.shape[0] - 3 * D - 4 * DD
    gain_grad = jnp.concatenate(
        [
            gain_rows[:3].reshape(-1),
            gain_rows[3:7, :DD].reshape(-1),
            jnp.zeros((pad_length,), jnp.float32),
        ]
    )
    own = lax.axis_index("dp") * groups + member
    gain_share = lax.dynamic_slice_in_dim(gain_grad, own * small_length, small_length)
    if not along:
        squares = jnp.sum(block_share * block_share) + jnp.sum(shared_share * shared_share)
    squares = squares + jnp.sum(gain_share * gain_share)
    sums = sum_small(jnp.stack([squares, loss_local]).reshape(1, 2))
    square_total, loss_total = sums[0, 0], sums[0, 1]
    grad_norm = jnp.sqrt(square_total)
    factor = jnp.minimum(1.0, clip_norm / (grad_norm + 1e-06))
    block_out, shared_out = update(
        factor,
        block_share,
        [block_first.reshape(-1, 128), block_second.reshape(-1, 128), block_lanes],
        shared_share,
        [shared_first.reshape(-1, 128), shared_second.reshape(-1, 128), shared_lanes],
    )
    block_out = tuple(piece.reshape(block_master.shape) for piece in block_out)
    shared_out = tuple(piece.reshape(-1) for piece in shared_out)
    gain_out = adamw(gain_share, gains_first, gains_second, gains_master, factor, rate_gains, 0.0)
    return (grad_norm, loss_total, count_total) + block_out + shared_out + gain_out


def solution(mesh):
    return jax.shard_map(
        on_device,
        mesh=mesh,
        in_specs=(
            P("dp", None, None),
            P("dp", None),
            P("mp", "dp"),
            P("mp", "dp"),
            P("mp", "dp"),
            P(("dp", "mp")),
            P(("dp", "mp")),
            P(("dp", "mp")),
            P(("dp", "mp")),
            P(("dp", "mp")),
            P(("dp", "mp")),
        ),
        out_specs=(
            P(),
            P(),
            P(),
            P("mp", "dp"),
            P("mp", "dp"),
            P("mp", "dp"),
            P("mp", "dp"),
            P(("dp", "mp")),
            P(("dp", "mp")),
            P(("dp", "mp")),
            P(("dp", "mp")),
            P(("dp", "mp")),
            P(("dp", "mp")),
            P(("dp", "mp")),
            P(("dp", "mp")),
        ),
        check_vma=False,
    )
```

```python
from functools import partial
import math

import jax
import jax.numpy as jnp
from jax import lax
from jax.experimental import pallas as pl
from jax.experimental.pallas import tpu as pltpu
from jax.sharding import PartitionSpec as P

D = 768
HEADS = 12
MLP = 3072
DD = 512
DHEADS = 16
DMLP = 2048
PIX = 768
PATCHES = 196
VIS = 64
STEP = 10


low_type = jnp.bfloat16
clip_norm = 0.0002
beta_one = 0.9
beta_two = 0.95
adam_eps = 1e-10
rate_matrix = 0.03
rate_gains = 0.7
weight_decay = 0.1


def forward_dot(left_side, right_side):
    return jnp.dot(left_side, right_side, preferred_element_type=jnp.float32)


def back_dot(left_side, right_side):
    return lax.dot_general(
        left_side,
        right_side,
        (((left_side.ndim - 1,), (1,)), ((), ())),
        preferred_element_type=jnp.float32,
    )


def outer_sum(left_side, right_side):
    left_rows = left_side.reshape(-1, left_side.shape[-1])
    right_rows = right_side.reshape(-1, right_side.shape[-1])
    return lax.dot_general(
        left_rows, right_rows, (((0,), (0,)), ((), ())), preferred_element_type=jnp.float32
    )


def swap(values, axis_name, distance):
    count = lax.axis_size(axis_name)
    return lax.ppermute(values, axis_name, [(place, place ^ distance) for place in range(count)])


def share(values):
    groups = lax.axis_size("mp")
    return jnp.stack([values] + [swap(values, "mp", step) for step in range(1, groups)])


def share_by_core(values):
    core = lax.axis_index("dp") & 1
    rows = values.shape[0] // 2
    near = share(lax.dynamic_slice_in_dim(values, core * rows, rows, 0))
    other = swap(near, "dp", 1)
    first = jnp.where(core == 0, near, other)
    return jnp.concatenate([first, jnp.where(core == 0, other, near)], 1)


def pick(values, index, dim):
    return lax.dynamic_index_in_dim(values, index, dim, keepdims=False)


def reorder(values, place):
    return jnp.stack([pick(values, place ^ step, 0) for step in range(values.shape[0])])


def bits_of(count):
    return count.bit_length() - 1


def after(values, token):
    first = token[(0,) * token.ndim].astype(jnp.float32)
    return values + jnp.minimum(jnp.abs(first), 0.0).astype(values.dtype)


def after_all(values, tokens):
    for token in tokens:
        values = after(values, token)
    return values


def half_cut(values, side, dim):
    return (pick(values, side, dim), pick(values, 1 - side, dim))


def bit_orders():
    higher = tuple(range(3, bits_of(lax.axis_size("dp"))))
    return ((1, 2) + higher, (2, 1) + higher)


def first_stage(kept_whole, got_whole):
    width = bits_of(lax.axis_size("dp"))
    place = lax.axis_index("dp")
    rows = kept_whole.shape[1]
    split = (2,) * (width - 1) + kept_whole.shape[1:]
    both = [piece.reshape(split) for piece in (kept_whole, got_whole)]
    totals, sents = [], []
    for (first, last), order in zip(((0, rows // 2), (rows // 2, rows)), bit_orders()):
        dim = width - 1 - order[0]
        side = (place >> order[0]) & 1

        def part_of(values, where, dim=dim, first=first, last=last):
            starts = [0] * values.ndim
            sizes = list(values.shape)
            starts[dim], sizes[dim] = where, 1
            starts[width - 1], sizes[width - 1] = first, last - first
            cut = lax.dynamic_slice(values, starts, sizes)
            return cut.reshape(sizes[:dim] + sizes[dim + 1 :]).astype(jnp.float32)

        kept, sent = [sum(part_of(piece, where) for piece in both) for where in (side, 1 - side)]
        sent = sent.astype(low_type)
        sents.append(sent)
        totals.append(kept + swap(sent, "dp", 1 << order[0]).astype(jnp.float32))
    return totals, sents


def later_stages(totals, tokens=()):
    width = bits_of(lax.axis_size("dp"))
    place = lax.axis_index("dp")
    halves, sents = [], []
    for total, order in zip(totals, bit_orders()):
        total = after_all(total, tokens)
        left = [bit for bit in range(width - 1, 0, -1) if bit != order[0]]
        for bit in order[1:]:
            kept, sent = half_cut(total, (place >> bit) & 1, left.index(bit))
            sent = sent.astype(low_type)
            total = kept + swap(sent, "dp", 1 << bit).astype(jnp.float32)
            left.remove(bit)
        sents.append(sent)
        halves.append(total)
    return halves, sents


def reduce_dp(values):
    place = lax.axis_index("dp")
    shaped = values.reshape((-1, 2) + values.shape[1:])
    kept, sent = half_cut(shaped, place & 1, 1)
    totals, sents = first_stage(kept, swap(sent, "dp", 1))
    return jnp.concatenate(later_stages(totals)[0], 0)


def to_members(values):
    return lax.all_to_all(values, "mp", 0, 0, tiled=True)


def sum_chips(row):
    width = bits_of(lax.axis_size("dp"))
    if width == 3:
        place = lax.axis_index("dp") >> 1
        rows = jnp.stack([row] + [swap(row, "dp", 2 * step) for step in range(1, 4)])
        return jnp.sum(reorder(rows, place), 0)
    for bit in range(1, width):
        row = row + swap(row, "dp", 1 << bit)
    return row


def sum_small(row):
    row = sum_chips(row + swap(row, "dp", 1))
    return jnp.sum(reorder(share(row), lax.axis_index("mp")), 0)


def pair_permute(values, pairs):
    return lax.ppermute(values, ("dp", "mp"), pairs)


def gather_early(small_row, block_rows):
    replicas = lax.axis_size("dp")
    place = lax.axis_index("dp")
    member = lax.axis_index("mp")
    width = bits_of(replicas)
    higher = tuple(range(3, width))
    orders = ((1, 2) + higher, (2, 1) + higher)
    half_rows = block_rows.shape[0] // 2
    halves = [block_rows[None, :half_rows], block_rows[None, half_rows:]]
    table = reorder(share(small_row), member)[None]
    for level in range(width - 1):
        halves = [
            jnp.concatenate([half, swap(half, "dp", 1 << order[level])], 0)
            for half, order in zip(halves, orders)
        ]
    placed = []
    for half, order in zip(halves, orders):
        shaped = half.reshape((2,) * (width - 1) + half.shape[1:])
        dims = [width - 2 - order.index(bit) for bit in range(width - 1, 0, -1)]
        placed.append(shaped.transpose(dims + [width - 1, width]).reshape(half.shape))
    near = jnp.concatenate(placed, 1)
    both = jnp.stack([near, swap(near, "dp", 1)], 1).reshape((replicas,) + block_rows.shape)
    block_flat = reorder(both, place).reshape(-1, block_rows.shape[1])
    for bit in range(width):
        table = jnp.concatenate([table, swap(table, "dp", 1 << bit)], 0)
    return reorder(table, place).reshape(-1, small_row.shape[0]), block_flat


def position_table(places, row_width):
    column = jnp.arange(row_width)
    step_rate = jnp.exp(-(column // 2 * 2).astype(jnp.float32) * (math.log(10000.0) / row_width))
    angle = places.astype(jnp.float32)[..., None] * step_rate
    return jnp.where(column % 2 == 0, jnp.sin(angle), jnp.cos(angle))


def visible_slots(visible):
    slot_rank = jnp.cumsum(visible, 1) - 1
    select = (
        (visible[:, None, :] == 1) & (slot_rank[:, None, :] == jnp.arange(VIS)[None, :, None])
    ).astype(jnp.int32)
    slot_patch = jnp.sum(select * jnp.arange(visible.shape[1])[None, None, :], 2)
    key_valid = jnp.arange(VIS)[None, :] < jnp.sum(visible, 1)[:, None]
    return (select, slot_patch, key_valid)


def cut_pieces(flat_vector, shapes):
    pieces = []
    offset = 0
    for shape in shapes:
        length = math.prod(shape)
        pieces.append(flat_vector[offset : offset + length].reshape(shape))
        offset += length
    return pieces


def norm_forward(residual, gain_vec):
    center = residual - jnp.mean(residual, -1, keepdims=True)
    inverse = lax.rsqrt(jnp.mean(center * center, -1, keepdims=True) + 1e-06)
    normal_hat = center * inverse
    return (normal_hat * gain_vec, normal_hat, inverse)


def norm_backward(gradient, normal_hat, inverse, gain_vec):
    hat_grad = gradient * gain_vec
    residual_grad = inverse * (
        hat_grad
        - jnp.mean(hat_grad, -1, keepdims=True)
        - normal_hat * jnp.mean(hat_grad * normal_hat, -1, keepdims=True)
    )
    return (residual_grad, gradient * normal_hat)


def split_heads(packed, head_count):
    batch_size, length, row_width = packed.shape
    unpacked = packed.reshape(batch_size, length, 3, head_count, row_width // (3 * head_count))
    return (unpacked[:, :, 0], unpacked[:, :, 1], unpacked[:, :, 2])


def scores_of(query_part, key_part, key_valid, scaling):
    raw_scores = (
        jnp.einsum("blhd,bmhd->bhlm", query_part, key_part, preferred_element_type=jnp.float32)
        * scaling
    )
    return jnp.where(key_valid[:, None, None, :], raw_scores, -1e30)


def attend_forward(packed, key_valid, head_count, scaling):
    query_part, key_part, value_part = split_heads(packed, head_count)
    scores = scores_of(query_part, key_part, key_valid, scaling)
    row_top = jnp.max(scores, -1, keepdims=True)
    exponent = jnp.exp(scores - row_top)
    row_total = jnp.sum(exponent, -1, keepdims=True)
    probability = (exponent / row_total).astype(low_type)
    mixed_heads = jnp.einsum(
        "bhlm,bmhd->blhd", probability, value_part, preferred_element_type=jnp.float32
    )
    batch_size, length = (key_valid.shape[0], packed.shape[1])
    return (
        mixed_heads.reshape(batch_size, length, -1).astype(low_type),
        row_top + jnp.log(row_total),
    )


def attend_backward(packed, log_total, key_valid, mixed_grad, head_count, scaling):
    query_part, key_part, value_part = split_heads(packed, head_count)
    batch_size, length, row_width = mixed_grad.shape
    out_grad = mixed_grad.reshape(batch_size, length, head_count, -1)
    probability = jnp.exp(scores_of(query_part, key_part, key_valid, scaling) - log_total)
    value_grad = jnp.einsum(
        "bhlm,blhd->bmhd",
        probability.astype(low_type),
        out_grad,
        preferred_element_type=jnp.float32,
    )
    prob_grad = jnp.einsum(
        "blhd,bmhd->bhlm", out_grad, value_part, preferred_element_type=jnp.float32
    )
    score_grad = (
        probability * (prob_grad - jnp.sum(probability * prob_grad, -1, keepdims=True))
    ).astype(low_type)
    query_grad = (
        jnp.einsum("bhlm,bmhd->blhd", score_grad, key_part, preferred_element_type=jnp.float32)
        * scaling
    )
    key_grad = (
        jnp.einsum("bhlm,blhd->bmhd", score_grad, query_part, preferred_element_type=jnp.float32)
        * scaling
    )
    stacked = jnp.stack([query_grad, key_grad, value_grad], 2)
    return stacked.reshape(batch_size, length, -1).astype(low_type)


def cut_rows(rows, shapes):
    pieces = []
    offset = 0
    for shape in shapes:
        length = math.prod(shape) // 128
        pieces.append(rows[offset : offset + length].reshape(shape))
        offset += length
    return pieces


def mlp_backward(
    gradient, grad_low, activated, raised, inner_low, up_w, down_w, total_sum, norm_saved
):
    down_grad = outer_sum(activated, grad_low)
    act_grad = back_dot(grad_low, down_w)
    unused, gelu_back = jax.vjp(partial(jax.nn.gelu, approximate=True), raised)
    raised_grad = gelu_back(act_grad)[0].astype(low_type)
    up_grad = outer_sum(inner_low, raised_grad)
    inner_grad = total_sum(back_dot(raised_grad, up_w))
    normal_hat, inverse, gain_vec = norm_saved
    middle_part, second_terms = norm_backward(inner_grad, normal_hat, inverse, gain_vec)
    return (gradient + middle_part, down_grad, up_grad, second_terms)


def adamw(gradient, first_old, second_old, master, factor, step_rate, decay_rate):
    gradient = gradient * factor
    first_new = beta_one * first_old + (1 - beta_one) * gradient
    second_new = beta_two * second_old + (1 - beta_two) * gradient * gradient
    first_hat = first_new / (1 - beta_one**STEP)
    second_hat = second_new / (1 - beta_two**STEP)
    master_new = master - step_rate * (
        first_hat / (jnp.sqrt(second_hat) + adam_eps) + decay_rate * master
    )
    return (first_new, second_new, master_new, master_new.astype(jnp.bfloat16))


def low_rows(block_lanes, row_width):
    pieces = row_width // 128

    def kernel(block_ref, block_out):
        for piece in range(pieces):
            lanes = slice(piece * 128, (piece + 1) * 128)
            spots = pl.ds(piece, block_out.shape[0], stride=pieces)
            block_out[:, lanes] = block_ref[spots, :].astype(low_type)

    return pl.pallas_call(
        kernel,
        out_shape=jax.ShapeDtypeStruct((block_lanes.shape[0] // pieces, row_width), low_type),
        compiler_params=pltpu.CompilerParams(vmem_limit_bytes=8 * 2**20),
    )(block_lanes)


def adamw_of(gradient, first_old, second_old, master, step_rate, decay_rate):
    first_new = beta_one * first_old + (1 - beta_one) * gradient
    second_new = beta_two * second_old + (1 - beta_two) * gradient * gradient
    first_hat = first_new / (1 - beta_one**STEP)
    second_hat = second_new / (1 - beta_two**STEP)
    master_new = master - step_rate * (
        first_hat / (jnp.sqrt(second_hat) + adam_eps) + decay_rate * master
    )
    return (first_new, second_new, master_new, master_new.astype(low_type))


def update(factor, block_rows, block_state, shared_lanes, shared_state):
    pieces = block_rows.shape[1] // 128

    def kernel(factor_ref, *refs):
        block_grad, shared_grad = refs[0], refs[4]
        scale = factor_ref[0, 0]
        rows = block_grad.shape[0]
        block_in, block_to = refs[1:4], refs[8:12]
        shared_in, shared_to = refs[5:8], refs[12:16]
        for piece in range(pieces):
            spots = pl.ds(piece, rows, stride=pieces)
            gradient = block_grad[:, piece * 128 : (piece + 1) * 128] * scale
            results = adamw_of(
                gradient, *[ref[spots, :] for ref in block_in], rate_matrix, weight_decay
            )
            for ref, result in zip(block_to[:3], results[:3]):
                ref[spots, :] = result
        block_to[3][...] = block_to[2][...].astype(low_type).reshape(block_to[3].shape)
        results = adamw_of(
            shared_grad[...] * scale, *[ref[...] for ref in shared_in], rate_matrix, weight_decay
        )
        for ref, result in zip(shared_to, results):
            ref[...] = result

    kinds = (jnp.float32, jnp.float32, jnp.float32, low_type)
    shapes = [block_state[0].shape] * 4 + [shared_state[0].shape] * 4
    shapes[3] = (1, math.prod(shapes[3]))
    results = pl.pallas_call(
        kernel,
        in_specs=[pl.BlockSpec(memory_space=pltpu.SMEM)]
        + [pl.BlockSpec(memory_space=pltpu.VMEM)] * 8,
        out_shape=[jax.ShapeDtypeStruct(shape, kind) for shape, kind in zip(shapes, kinds * 2)],
        compiler_params=pltpu.CompilerParams(vmem_limit_bytes=20 * 2**20),
    )(factor.reshape(1, 1), block_rows, *block_state, shared_lanes, *shared_state)
    return (tuple(results[:4]), tuple(results[4:]))


TOKENS = 208
LANES = 128


def dot_tn(left_side, right_side):
    return lax.dot_general(
        left_side, right_side, (((0,), (0,)), ((), ())), preferred_element_type=jnp.float32
    )


def dot_nt(left_side, right_side):
    return lax.dot_general(
        left_side, right_side, (((1,), (1,)), ((), ())), preferred_element_type=jnp.float32
    )


def gelu_pair(raised):
    rate = math.sqrt(2.0 / math.pi)
    square = raised * raised
    curve = jnp.tanh(rate * (raised + 0.044715 * raised * square))
    half = 0.5 * (1.0 + curve)
    slope = half + 0.5 * raised * (1.0 - curve * curve) * rate * (1.0 + 0.134145 * square)
    return raised * half, slope


def unpack(lanes, first_entry, shapes):
    step = 64

    def kernel(lanes_ref, *refs):
        work = refs[-1]
        start = first_entry // LANES
        for out in refs[:-1]:
            depth, pieces = out.shape[0], out.shape[1] // LANES
            span = step * pieces

            def chunk(index, carry, out=out, start=start, pieces=pieces, span=span):
                source = pl.ds(pl.multiple_of(start + index * span, 64), span)
                work[:span, :] = lanes_ref[source, :].astype(jnp.float32)
                rows = pl.ds(pl.multiple_of(index * step, step), step)
                for piece in range(pieces):
                    out[rows, piece * LANES : (piece + 1) * LANES] = work[
                        pl.ds(piece, step, stride=pieces), :
                    ].astype(low_type)
                return carry

            lax.fori_loop(0, depth // step, chunk, 0, unroll=2)
            start += depth * pieces

    entries = sum(math.prod(shape) for shape in shapes)
    widest = max(shape[1] for shape in shapes)
    block = first_entry // LANES + entries // LANES
    return pl.pallas_call(
        kernel,
        grid=(1,),
        in_specs=[pl.BlockSpec((block, LANES), lambda index: (0, 0))],
        out_specs=[pl.BlockSpec(shape, lambda index: (0, 0)) for shape in shapes],
        out_shape=[jax.ShapeDtypeStruct(shape, low_type) for shape in shapes],
        scratch_shapes=[pltpu.VMEM((step * widest // LANES, LANES), jnp.float32)],
        compiler_params=pltpu.CompilerParams(vmem_limit_bytes=36 * 2**20),
        cost_estimate=pl.CostEstimate(flops=0, bytes_accessed=4 * entries, transcendentals=0),
    )(lanes)


def decoder_kernel(
    latent_rows,
    core_ref,
    scale_ref,
    final_ref,
    latent_ref,
    select_ref,
    mask_ref,
    table_ref,
    small_ref,
    pixels_ref,
    packed_w,
    out_w,
    up_w,
    down_w,
    head_w,
    sent_out,
    kept_out,
    latent_out,
    small_out,
    loss_out,
    grad_ref,
    copy_sems,
    work,
    packed_ref,
    mixed_ref,
    prob_ref,
    raised_ref,
    activated_ref,
    packed_grad_ref,
):
    scaling = (DD // DHEADS) ** (-0.5)
    width = DD // DHEADS
    per_block = LANES // width
    first_gain, second_gain, last_gain, mask_token = [
        small_ref[row : row + 1, :] for row in range(4)
    ]
    mask = mask_ref[...]
    select = select_ref[...]
    key_valid = lax.broadcasted_iota(jnp.int32, (TOKENS, TOKENS), 1) < PATCHES
    lane_head = lax.broadcasted_iota(jnp.int32, (TOKENS, LANES), 1) // width
    quarter = DMLP // 4

    tokens = forward_dot(select, latent_ref[...]) + mask * mask_token + table_ref[...]
    first_norm, first_hat, first_inverse = norm_forward(tokens, first_gain)
    normed = first_norm.astype(low_type)
    for piece in range(3):
        columns = slice(piece * DD, (piece + 1) * DD)
        packed_ref[:, columns] = forward_dot(normed, packed_w[:, columns]).astype(low_type)
    mixed_ref[...] = jnp.zeros(mixed_ref.shape, jnp.float32)

    def attend(head, carry):
        block = pl.multiple_of(head // per_block * LANES, LANES)
        inside = lane_head == head % per_block
        query = jnp.where(inside, packed_ref[:, pl.ds(block, LANES)], 0)
        key = packed_ref[:, pl.ds(DD + block, LANES)]
        value = packed_ref[:, pl.ds(2 * DD + block, LANES)]
        scores = jnp.where(key_valid, dot_nt(query, key) * scaling, -1e30)
        exponent = jnp.exp(scores - jnp.max(scores, -1, keepdims=True))
        probability = exponent / jnp.sum(exponent, -1, keepdims=True)
        prob_ref[head] = probability
        mixed = forward_dot(probability.astype(low_type), value)
        mixed_ref[:, pl.ds(block, LANES)] += jnp.where(inside, mixed, 0.0)
        return carry

    lax.fori_loop(0, DHEADS, attend, 0, unroll=16)
    mixed_low = mixed_ref[...].astype(low_type)
    middle = tokens + forward_dot(mixed_low, out_w[...])
    second_norm, second_hat, second_inverse = norm_forward(middle, second_gain)
    inner = second_norm.astype(low_type)
    decoded = middle
    for part in range(4):
        columns = slice(part * quarter, (part + 1) * quarter)
        raised = forward_dot(inner, up_w[:, columns])
        activated, slope = gelu_pair(raised)
        raised_ref[:, columns] = slope
        activated = activated.astype(low_type)
        activated_ref[:, columns] = activated
        decoded = decoded + forward_dot(activated, down_w[columns, :])
    top_norm, top_hat, top_inverse = norm_forward(decoded, last_gain)
    top = top_norm.astype(low_type)
    predicted = forward_dot(top, head_w[...])
    target = pixels_ref[...].astype(jnp.float32)
    center = target - jnp.mean(target, -1, keepdims=True)
    target = center * lax.rsqrt(jnp.mean(center * center, -1, keepdims=True) + 1e-06)
    errors = predicted - target
    loss_out[...] = jnp.sum(
        mask * jnp.mean(errors * errors, -1, keepdims=True), axis=0, keepdims=True
    )
    pred_grad = (errors * (mask * scale_ref[0, 0])).astype(low_type)

    starts = [PIX * D // LANES]
    for size in (3 * DD * DD, DD * DD, DD * DMLP, DMLP * DD):
        starts.append(starts[-1] + size // LANES)
    grad_ref[: starts[0], :] = jnp.zeros((starts[0], LANES), low_type)
    slot_rows = sent_out.shape[1]
    slots = 2 * sent_out.shape[0]
    core = core_ref[0, 0]
    copies = []

    def send_from(first_row, last_row):
        for slot in range(slots):
            if first_row <= slot * slot_rows < last_row:
                rows = grad_ref.at[pl.ds(slot * slot_rows, slot_rows), :]
                side = slot % 2
                pair = slot // 2

                def start(target, rows=rows, pair=pair, slot=slot):
                    pltpu.make_async_copy(rows, target.at[pair], copy_sems.at[slot]).start()

                pl.when(core == side)(partial(start, kept_out))
                pl.when(core != side)(partial(start, sent_out))
                copies.append(
                    pltpu.make_async_copy(rows, kept_out.at[pair], copy_sems.at[slot])
                )

    def put(left_side, right_ref_columns, pieces, base):
        depth = left_side.shape[1]
        for piece, columns in right_ref_columns:
            product = dot_tn(left_side, columns)
            for half in range(columns.shape[1] // LANES):
                work[pl.ds(base + piece + half, depth, stride=pieces), :] = product[
                    :, half * LANES : (half + 1) * LANES
                ]

    def flush(start, size):
        grad_ref[start : start + size, :] = work[:size, :].astype(low_type)
        send_from(start, start + size)

    def pairs_of(values):
        return [
            (2 * pair, values[:, 2 * pair * LANES : 2 * (pair + 1) * LANES])
            for pair in range(values.shape[1] // (2 * LANES))
        ]

    put(top, pairs_of(pred_grad), PIX // LANES, 0)
    flush(starts[4], DD * PIX // LANES)
    decoded_grad, last_terms = norm_backward(
        dot_nt(pred_grad, head_w[...]), top_hat, top_inverse, last_gain
    )
    grad_low = decoded_grad.astype(low_type)
    inner_grad = jnp.zeros((TOKENS, DD), jnp.float32)
    for part in range(4):
        columns = slice(part * quarter, (part + 1) * quarter)
        put(activated_ref[:, columns], pairs_of(grad_low), DD // LANES, part * quarter * DD // LANES)
    flush(starts[3], DMLP * DD // LANES)
    for part in range(4):
        columns = slice(part * quarter, (part + 1) * quarter)
        act_grad = dot_nt(grad_low, down_w[columns, :])
        raised_grad = (act_grad * raised_ref[:, columns]).astype(low_type)
        put(inner, pairs_of(raised_grad), DMLP // LANES, part * quarter // LANES)
        inner_grad = inner_grad + dot_nt(raised_grad, up_w[:, columns])
    flush(starts[2], DD * DMLP // LANES)
    middle_part, second_terms = norm_backward(inner_grad, second_hat, second_inverse, second_gain)
    middle_grad = decoded_grad + middle_part
    middle_low = middle_grad.astype(low_type)
    put(mixed_low, pairs_of(middle_low), DD // LANES, 0)
    flush(starts[1], DD * DD // LANES)
    mixed_ref[...] = dot_nt(middle_low, out_w[...])
    packed_grad_ref[...] = jnp.zeros(packed_grad_ref.shape, jnp.float32)

    def attend_back(head, carry):
        block = pl.multiple_of(head // per_block * LANES, LANES)
        inside = lane_head == head % per_block
        out_grad = mixed_ref[:, pl.ds(block, LANES)].astype(low_type)
        query = packed_ref[:, pl.ds(block, LANES)]
        key = packed_ref[:, pl.ds(DD + block, LANES)]
        value = packed_ref[:, pl.ds(2 * DD + block, LANES)]
        probability = prob_ref[head]
        value_grad = dot_tn(probability.astype(low_type), out_grad)
        prob_grad = dot_nt(jnp.where(inside, out_grad, 0), value)
        score_grad = (
            probability * (prob_grad - jnp.sum(probability * prob_grad, -1, keepdims=True))
        ).astype(low_type)
        query_grad = forward_dot(score_grad, key) * scaling
        key_grad = dot_tn(score_grad, query) * scaling
        for piece, values in enumerate((query_grad, key_grad, value_grad)):
            packed_grad_ref[:, pl.ds(piece * DD + block, LANES)] += jnp.where(inside, values, 0.0)
        return carry

    lax.fori_loop(0, DHEADS, attend_back, 0, unroll=16)
    normed_grad = jnp.zeros((TOKENS, DD), jnp.float32)
    for piece in range(3):
        columns = slice(piece * DD, (piece + 1) * DD)
        packed_low = packed_grad_ref[:, columns].astype(low_type)
        put(normed, pairs_of(packed_low), 3 * DD // LANES, piece * DD // LANES)
        normed_grad = normed_grad + dot_nt(packed_low, packed_w[:, columns])
    flush(starts[0], 3 * DD * DD // LANES)
    token_part, first_terms = norm_backward(normed_grad, first_hat, first_inverse, first_gain)
    token_grad = middle_grad + token_part
    latent_grad = dot_tn(select, token_grad.astype(low_type)).astype(low_type)
    latent_out[...] = latent_grad
    if latent_rows > 0:
        for part in range(slot_rows // latent_rows):
            columns = DD // (slot_rows // latent_rows)
            product = dot_tn(final_ref[...], latent_grad[:, part * columns : (part + 1) * columns])
            grad_ref[part * latent_rows : part * latent_rows + D, :] = product.astype(low_type)
    for row, terms in enumerate((first_terms, second_terms, last_terms, mask * token_grad)):
        small_out[row : row + 1, :] = jnp.sum(terms, axis=0, keepdims=True)
    send_from(0, starts[0])
    for copy in copies:
        copy.wait()


def decode(
    latent_rows, core, scale, final_low, latent, select, mask, table, small, pixels, weights, slots, slot_rows
):
    half = jax.ShapeDtypeStruct((slots // 2, slot_rows, LANES), low_type)
    return pl.pallas_call(
        partial(decoder_kernel, latent_rows),
        in_specs=[pl.BlockSpec(memory_space=pltpu.SMEM)] * 2
        + [pl.BlockSpec(memory_space=pltpu.VMEM)] * 12,
        out_specs=[pl.BlockSpec(memory_space=pltpu.HBM)] * 2
        + [pl.BlockSpec(memory_space=pltpu.VMEM)] * 3,
        out_shape=(
            half,
            half,
            jax.ShapeDtypeStruct(latent.shape, low_type),
            jax.ShapeDtypeStruct(small.shape, jnp.float32),
            jax.ShapeDtypeStruct((1, 1), jnp.float32),
        ),
        scratch_shapes=[
            pltpu.VMEM((slots * slot_rows, LANES), low_type),
            pltpu.SemaphoreType.DMA((slots,)),
            pltpu.VMEM((DD * DMLP // LANES, LANES), jnp.float32),
            pltpu.VMEM((TOKENS, 3 * DD), low_type),
            pltpu.VMEM((TOKENS, DD), jnp.float32),
            pltpu.VMEM((DHEADS, TOKENS, TOKENS), jnp.float32),
            pltpu.VMEM((TOKENS, DMLP), jnp.float32),
            pltpu.VMEM((TOKENS, DMLP), low_type),
            pltpu.VMEM((TOKENS, 3 * DD), jnp.float32),
        ],
        compiler_params=pltpu.CompilerParams(vmem_limit_bytes=36 * 2**20),
        cost_estimate=pl.CostEstimate(
            flops=6 * TOKENS * slots * slot_rows * LANES,
            bytes_accessed=4 * slots * slot_rows * LANES,
            transcendentals=TOKENS * (DMLP + DHEADS * TOKENS),
        ),
    )(core, scale, final_low, latent, select, mask, table, small, pixels, *weights)


def cut_spans(rows_of, slots, slot_rows):
    spans = []
    start = 0
    for source, rows in enumerate(rows_of):
        for slot in range(slots):
            first = max(start, slot * slot_rows)
            last = min(start + rows, (slot + 1) * slot_rows)
            if first < last:
                spans.append((source, first - start, slot, first - slot * slot_rows, last - first))
        start += rows
    return spans


def move_spans(core, spans, sources, sent, kept, sems):
    def move(number, target):
        source, first, slot, place, size = spans[number]
        return pltpu.make_async_copy(
            sources[source].at[pl.ds(first, size), :],
            target.at[slot // 2, pl.ds(place, size), :],
            sems.at[number],
        )

    for number, span in enumerate(spans):
        side = span[2] % 2
        pl.when(core == side)(lambda number=number: move(number, kept).start())
        pl.when(core != side)(lambda number=number: move(number, sent).start())
    for number in range(len(spans)):
        move(number, kept).wait()


def smem(value):
    return value.reshape(1, 1)


def run_kernel(kernel, tokens, arguments, outputs, scratch=(), flops=0, scalars=0, saved=0):
    count = len(tokens)
    held = arguments[len(arguments) - saved :]

    def body(*refs):
        refs = refs[count:]
        sources = refs[len(arguments) - saved : len(arguments)]
        given, rest = refs[: len(arguments) - saved], refs[len(arguments) :]
        results, rest = rest[: len(outputs)], rest[len(outputs) :]
        own, local = rest[: len(scratch)], rest[len(scratch) :][:saved]
        if saved:
            sems = rest[-1]
            copies = [
                pltpu.make_async_copy(source, target, sems.at[number])
                for number, (source, target) in enumerate(zip(sources, local))
            ]
            for copy in copies:
                copy.start()
            for copy in copies:
                copy.wait()
        kernel(*given, *local, *results, *own)

    return pl.pallas_call(
        body,
        in_specs=[pl.BlockSpec(memory_space=pl.ANY)] * count
        + [pl.BlockSpec(memory_space=pltpu.SMEM)] * scalars
        + [pl.BlockSpec(memory_space=pltpu.VMEM)] * (len(arguments) - scalars - saved)
        + [pl.BlockSpec(memory_space=pltpu.HBM)] * saved,
        out_specs=[pl.BlockSpec(memory_space=pltpu.VMEM)] * len(outputs),
        out_shape=[jax.ShapeDtypeStruct(shape, kind) for shape, kind in outputs],
        scratch_shapes=list(scratch)
        + [pltpu.VMEM(array.shape, array.dtype) for array in held]
        + [pltpu.SemaphoreType.DMA((saved,))] * (saved > 0),
        compiler_params=pltpu.CompilerParams(vmem_limit_bytes=16 * 2**20),
        cost_estimate=pl.CostEstimate(flops=flops, bytes_accessed=2**20, transcendentals=0),
    )(*tokens, *arguments)


def put_terms(terms, outs):
    for place, out in enumerate(outs):
        out[...] = terms[place * VIS : (place + 1) * VIS].astype(out.dtype)


def term_outputs(groups):
    return [((VIS, D), jnp.float32)] + [((VIS, D), low_type)] * (groups - 1)


def sum_terms(refs):
    total = refs[0][...]
    for ref in refs[1:]:
        total = total + ref[...].astype(jnp.float32)
    return total


def join(refs):
    return jnp.concatenate([ref[...] for ref in refs], 0)


def exchange(terms):
    return [terms[0]] + [swap(terms[step], "mp", step) for step in range(1, len(terms))]


def spread(values):
    groups = lax.axis_size("mp")
    return [values] + [swap(values, "mp", step) for step in range(1, groups)]


def head_lanes(rows, columns):
    return lax.broadcasted_iota(jnp.int32, (rows, columns), 1) // (D // HEADS)


def enter_encoder(seen, patch_w, table, gain, packed_w, out_w, valid):
    groups = lax.axis_size("mp")
    rows, columns = groups * VIS, D // groups
    heads = HEADS // groups
    scaling = (D // HEADS) ** (-0.5)

    def kernel(seen, patch_w, table, gain, packed_w, out_w, valid, *outs):
        residual_out, hat_out, inverse_out, normed_out, packed_out, prob_out, mixed_out = outs[:7]
        residual = forward_dot(seen[...], patch_w[...]) + table[...]
        norm, hat, inverse = norm_forward(residual, gain[...])
        residual_out[...] = residual[:VIS]
        hat_out[...] = hat[:VIS]
        inverse_out[...] = jnp.broadcast_to(inverse[:VIS], (VIS, LANES))
        normed = norm.astype(low_type)
        normed_out[...] = normed
        packed = forward_dot(normed, packed_w[...]).astype(low_type)
        packed_out[...] = packed
        query, key, value = [packed[:, third * columns : (third + 1) * columns] for third in range(3)]
        one = lax.broadcasted_iota(jnp.int32, (rows, rows), 0) // VIS
        other = lax.broadcasted_iota(jnp.int32, (rows, rows), 1) // VIS
        allowed = (one == other) & (valid[...] > 0.5)
        lanes = head_lanes(rows, columns)
        mixed = jnp.zeros((rows, columns), jnp.float32)
        for head in range(heads):
            inside = lanes == head
            scores = dot_nt(jnp.where(inside, query, 0), key) * scaling
            scores = jnp.where(allowed, scores, -1e30)
            exponent = jnp.exp(scores - jnp.max(scores, -1, keepdims=True))
            probability = exponent / jnp.sum(exponent, -1, keepdims=True)
            prob_out[head] = probability
            mixed = mixed + jnp.where(inside, forward_dot(probability.astype(low_type), value), 0.0)
        mixed_low = mixed.astype(low_type)
        mixed_out[...] = mixed_low
        put_terms(forward_dot(mixed_low, out_w[...]), outs[7:])

    outputs = [
        ((VIS, D), jnp.float32),
        ((VIS, D), jnp.float32),
        ((VIS, LANES), jnp.float32),
        ((rows, D), low_type),
        ((rows, 3 * columns), low_type),
        ((heads, rows, rows), jnp.float32),
        ((rows, columns), low_type),
    ] + term_outputs(groups)
    results = run_kernel(
        kernel, [], [seen, patch_w, table, gain, packed_w, out_w, valid], outputs, flops=10**9
    )
    return results[:7], results[7:]


def norm_of_sum(terms, residual, gain):
    count = len(terms)

    def kernel(*refs):
        residual, gain = refs[count : count + 2]
        sum_out, low_out, hat_out, inverse_out = refs[count + 2 :]
        total = residual[...] + sum_terms(refs[:count])
        norm, hat, inverse = norm_forward(total, gain[...])
        sum_out[...] = total
        low_out[...] = norm.astype(low_type)
        hat_out[...] = hat
        inverse_out[...] = jnp.broadcast_to(inverse, (VIS, LANES))

    outputs = [
        ((VIS, D), jnp.float32),
        ((VIS, D), low_type),
        ((VIS, D), jnp.float32),
        ((VIS, LANES), jnp.float32),
    ]
    return run_kernel(kernel, [], [*terms, residual, gain], outputs)


def raise_and_lower(inner, up_w, down_w):
    groups = len(inner)

    def kernel(*refs):
        up_w, down_w, inner_out = refs[groups : groups + 3]
        inner = join(refs[:groups])
        inner_out[...] = inner
        activated, slope = gelu_pair(forward_dot(inner, up_w[...]))
        put_terms(forward_dot(activated.astype(low_type), down_w[...]), refs[groups + 3 :])

    outputs = [((groups * VIS, D), low_type)] + term_outputs(groups)
    results = run_kernel(kernel, [], [*inner, up_w, down_w], outputs, flops=6 * 10**8)
    return results[0], results[1:]


def latent_of_sum(tokens, terms, residual, gain, latent_w):
    count = len(terms)

    def kernel(*refs):
        residual, gain, latent_w, low_out, hat_out, inverse_out, latent_out = refs[count:]
        norm, hat, inverse = norm_forward(residual[...] + sum_terms(refs[:count]), gain[...])
        final_low = norm.astype(low_type)
        low_out[...] = final_low
        hat_out[...] = hat
        inverse_out[...] = jnp.broadcast_to(inverse, (VIS, LANES))
        columns = latent_w.shape[2]
        for place in range(count):
            latent_out[:, place * columns : (place + 1) * columns] = forward_dot(
                final_low, latent_w[place]
            ).astype(low_type)

    outputs = [
        ((VIS, D), low_type),
        ((VIS, D), jnp.float32),
        ((VIS, LANES), jnp.float32),
        ((VIS, DD), low_type),
    ]
    return run_kernel(kernel, tokens, [*terms, residual, gain, latent_w], outputs)


def latent_back(tokens, member, along, latent_grad, latent_w, hat, inverse, gain):
    groups, rows, columns = latent_w.shape

    def kernel(member, latent_grad, latent_w, hat, inverse, gain, grad_out, gain_out, work, *outs):
        total = jnp.zeros((VIS, D), jnp.float32)
        for place in range(groups):
            cut = latent_grad[:, place * columns : (place + 1) * columns]
            work[place] = cut
            total = total + dot_nt(cut, latent_w[place])
        gradient, terms = norm_backward(total, hat[...], inverse[:, :1], gain[...])
        grad_out[...] = gradient
        for step, out in enumerate(outs):
            out[:, :D] = gradient.astype(low_type)
            if not along:
                out[:, D:] = work[member[0, 0] ^ step]
        gain_out[...] = jnp.sum(terms, axis=0, keepdims=True)

    outputs = [((VIS, D), jnp.float32), ((1, D), jnp.float32), ((groups, VIS, columns), low_type)]
    outputs += [((VIS, D + (0 if along else columns)), low_type)] * groups
    results = run_kernel(
        kernel,
        tokens,
        [smem(member), latent_grad, latent_w, hat, inverse, gain],
        outputs,
        scalars=1,
    )
    return results[0], results[1], results[3:]


def norm_back_of_sum(tokens, terms, upstream, hat, inverse, gain):
    count = len(terms)

    def kernel(*refs):
        upstream, hat, inverse, gain, grad_out, low_out, gain_out = refs[count:]
        part, gain_terms = norm_backward(
            sum_terms(refs[:count]), hat[...], inverse[:, :1], gain[...]
        )
        gradient = upstream[...] + part
        grad_out[...] = gradient
        low_out[...] = gradient.astype(low_type)
        gain_out[...] = jnp.sum(gain_terms, axis=0, keepdims=True)

    outputs = [((VIS, D), jnp.float32), ((VIS, D), low_type), ((1, D), jnp.float32)]
    return run_kernel(kernel, tokens, [*terms, upstream, hat, inverse, gain], outputs)


def mlp_back(tokens, core, grads, finals, inner, up_w, down_w, slots, slot_rows, first_row):
    groups = len(grads)
    embed_cols = grads[0].shape[1] - D
    count = len(tokens)
    given = groups + len(finals)
    spans = cut_spans([first_row, up_w.shape[0], down_w.shape[0]], slots, slot_rows)
    spans = [span for span in spans if span[0] > 0]

    def kernel(*refs):
        core, refs = refs[count], refs[count + 1 :]
        sources = refs[given : given + 3]
        outs = refs[given + 3 :]
        *outs, inner, up_w, down_w, load_sems = outs
        copies = [
            pltpu.make_async_copy(source, target, load_sems.at[number])
            for number, (source, target) in enumerate(zip(sources, (inner, up_w, down_w)))
        ]
        for copy in copies:
            copy.start()
        for copy in copies:
            copy.wait()
        both = join(refs[:groups])
        grad_low = both[:, :D]
        inner_low = inner[...]
        activated, slope = gelu_pair(forward_dot(inner_low, up_w[...]))
        raised_grad = (dot_nt(grad_low, down_w[...]) * slope).astype(low_type)
        put_terms(dot_nt(raised_grad, up_w[...]), outs[2 : 2 + groups])
        down_grad = dot_tn(activated.astype(low_type), grad_low).astype(low_type)
        up_grad = dot_tn(inner_low, raised_grad).astype(low_type)
        if slots > 0:
            up_work, down_work, sems = outs[2 + groups :][-3:]
            up_work[...] = up_grad
            down_work[...] = down_grad
            move_spans(core[0, 0], spans, [None, up_work, down_work], outs[0], outs[1], sems)
        else:
            outs[0][...] = up_grad
            outs[1][...] = down_grad
        if embed_cols > 0:
            final_low = join(refs[groups:given])
            outs[2 + groups][...] = dot_tn(final_low, both[:, D:]).astype(low_type)

    space = pltpu.VMEM
    shapes = [up_w.shape, down_w.shape]
    scratch = []
    if slots > 0:
        space = pltpu.HBM
        shapes = [(slots // 2, slot_rows, D)] * 2
        scratch = [
            pltpu.VMEM(up_w.shape, low_type),
            pltpu.VMEM(down_w.shape, low_type),
            pltpu.SemaphoreType.DMA((len(spans),)),
        ]
    outputs = [(shape, low_type) for shape in shapes] + term_outputs(groups)
    if embed_cols > 0:
        outputs.append(((D, embed_cols), low_type))
    results = pl.pallas_call(
        kernel,
        in_specs=[pl.BlockSpec(memory_space=pl.ANY)] * count
        + [pl.BlockSpec(memory_space=pltpu.SMEM)]
        + [pl.BlockSpec(memory_space=pltpu.VMEM)] * given
        + [pl.BlockSpec(memory_space=pltpu.HBM)] * 3,
        out_specs=[pl.BlockSpec(memory_space=space)] * 2
        + [pl.BlockSpec(memory_space=pltpu.VMEM)] * (len(outputs) - 2),
        out_shape=[jax.ShapeDtypeStruct(shape, kind) for shape, kind in outputs],
        scratch_shapes=scratch
        + [pltpu.VMEM(array.shape, low_type) for array in (inner, up_w, down_w)]
        + [pltpu.SemaphoreType.DMA((3,))],
        compiler_params=pltpu.CompilerParams(vmem_limit_bytes=16 * 2**20),
        cost_estimate=pl.CostEstimate(flops=15 * 10**8, bytes_accessed=2**20, transcendentals=0),
    )(*tokens, smem(core), *grads, *finals, inner, up_w, down_w)
    return results[:2], results[2 : 2 + groups], results[2 + groups :]


def attend_back(tokens, grad_low, normed, packed, prob, mixed, packed_w, out_w):
    groups = len(grad_low)
    rows, columns = groups * VIS, D // groups
    heads = HEADS // groups
    scaling = (D // HEADS) ** (-0.5)

    def kernel(*refs):
        normed, packed, prob, mixed, packed_w, out_w, packed_out, out_out = refs[
            groups : groups + 8
        ]
        grad_low = join(refs[:groups])
        mixed_grad = dot_nt(grad_low, out_w[...]).astype(low_type)
        query, key, value = [packed[:, third * columns : (third + 1) * columns] for third in range(3)]
        lanes = head_lanes(rows, columns)
        totals = [jnp.zeros((rows, columns), jnp.float32)] * 3
        for head in range(heads):
            inside = lanes == head
            probability = prob[head]
            value_grad = dot_tn(probability.astype(low_type), mixed_grad)
            prob_grad = dot_nt(jnp.where(inside, mixed_grad, 0), value)
            score_grad = (
                probability * (prob_grad - jnp.sum(probability * prob_grad, -1, keepdims=True))
            ).astype(low_type)
            query_grad = forward_dot(score_grad, key) * scaling
            key_grad = dot_tn(score_grad, query) * scaling
            totals = [
                total + jnp.where(inside, values, 0.0)
                for total, values in zip(totals, (query_grad, key_grad, value_grad))
            ]
        packed_grad = jnp.concatenate(totals, 1).astype(low_type)
        put_terms(dot_nt(packed_grad, packed_w[...]), refs[groups + 8 :])
        out_out[...] = dot_tn(mixed[...], grad_low).astype(low_type)
        packed_out[...] = dot_tn(normed[...], packed_grad).astype(low_type)

    outputs = [(packed_w.shape, low_type), (out_w.shape, low_type)] + term_outputs(groups)
    results = run_kernel(
        kernel,
        tokens,
        [*grad_low, normed, packed, prob, mixed, packed_w, out_w],
        outputs,
        flops=10**9,
        saved=6,
    )
    return results[:2], results[2:]


def last_norm_back(tokens, terms, upstream, hat, inverse, gain, second_gain, last_gain, dec_small):
    count = len(terms)

    def kernel(*refs):
        upstream, hat, inverse, gain, second_gain, last_gain, dec_small, low_out, work = refs[count:]
        part, gain_terms = norm_backward(
            sum_terms(refs[:count]), hat[...], inverse[:, :1], gain[...]
        )
        low_out[:VIS, :] = (upstream[...] + part).astype(low_type)
        work[...] = jnp.zeros(work.shape, jnp.float32)
        work[0:1, :] = jnp.sum(gain_terms, axis=0, keepdims=True)
        work[1:2, :] = second_gain[...]
        work[2:3, :] = last_gain[...]
        work[3:7, :DD] = dec_small[:4, :]
        values = work[...]
        high = values.astype(low_type)
        rest = (values - high.astype(jnp.float32)).astype(low_type)
        low_out[VIS:, :] = jnp.concatenate([high, rest], 0)

    return run_kernel(
        kernel,
        tokens,
        [*terms, upstream, hat, inverse, gain, second_gain, last_gain, dec_small],
        [((VIS + 16, D), low_type)],
        [pltpu.VMEM((8, D), jnp.float32)],
    )[0]


def patch_back(tokens, member, core, seen, grads, row_count):
    groups = len(grads)
    tail = PIX - groups * row_count
    early = 0 < tail <= row_count

    def kernel(member, core, seen, *refs):
        kept_out, sent_out, work = refs[groups:]
        rows_low = jnp.concatenate([ref[:VIS, :] for ref in refs[:groups]], 0)
        gains = jnp.zeros((8, D), jnp.float32)
        for ref in refs[:groups]:
            parts = ref[VIS:, :].astype(jnp.float32)
            gains = gains + (parts[:8] + parts[8:])
        if early:
            work[:PIX, :] = dot_tn(seen[...], rows_low)
            work[PIX:, :] = jnp.zeros((work.shape[0] - PIX, D), jnp.float32)
            rows = work[pl.ds(pl.multiple_of(member[0, 0] * row_count, 8), row_count), :]
            last = work[PIX - tail : PIX - tail + row_count, :]
            even = core[0, 0] == 0
            kept_out[:row_count, :] = jnp.where(even, rows, last)
            sent_out[:row_count, :] = jnp.where(even, last, rows)
        kept_out[kept_out.shape[0] - 8 :, :] = gains
        sent_out[sent_out.shape[0] - 8 :, :] = gains

    rows = row_count if early else 0
    return run_kernel(
        kernel,
        tokens,
        [smem(member), smem(core), seen, *grads],
        [((rows + 8, D), jnp.float32)] * 2,
        [pltpu.VMEM((PIX + row_count, D), jnp.float32)],
        4 * 10**8,
        2,
    )


def pack_block(tokens, core, packed_grad, out_grad, sent, kept):
    depth, columns = packed_grad.shape
    pair = depth // 2
    nine = 2 * columns // LANES
    six = D // LANES
    count = len(tokens)
    tiles = (columns + LANES - 1) // LANES
    slots, slot_rows = 2 * sent.shape[0], sent.shape[1]
    hidden_rows = 2 * D
    rows_of = [depth * columns // D, out_grad.shape[0], hidden_rows]
    rows_of.append(slots * slot_rows - sum(rows_of))
    spans = [span for span in cut_spans(rows_of, slots, slot_rows) if span[0] != 2]
    late = [span for span in spans if span[0] == 0]
    soon = [span for span in spans if span[0] != 0]

    def kernel(*refs):
        core, packed, out_grad, sent_in, kept_in, sent_out, kept_out = refs[count : count + 7]
        wide, flat, rows, zeros, out_work, late_sems, soon_sems = refs[count + 7 :]
        zeros[...] = jnp.zeros(zeros.shape, low_type)
        out_work[...] = out_grad[...]
        halves = []
        for tile in range(tiles):
            lanes = min(LANES, columns - tile * LANES)
            wide[tile * depth : (tile + 1) * depth, :lanes] = packed[
                :, tile * LANES : tile * LANES + lanes
            ].astype(jnp.float32)
        for side in range(2):
            pieces = [wide[pl.ds(tile * depth + side, pair, stride=2), :] for tile in range(tiles)]
            halves.append(jnp.concatenate(pieces, 1)[:, :columns])
        both = jnp.concatenate(halves, 1)
        for tile in range(nine):
            flat[pl.ds(tile, pair, stride=nine), :] = both[:, tile * LANES : (tile + 1) * LANES]
        for piece in range(six):
            rows[:, piece * LANES : (piece + 1) * LANES] = flat[
                pl.ds(piece, rows.shape[0], stride=six), :
            ].astype(low_type)
        sources = [rows, out_work, None, zeros]
        move_spans(core[0, 0], late + soon, sources, sent_out, kept_out, late_sems)

    return pl.pallas_call(
        kernel,
        in_specs=[pl.BlockSpec(memory_space=pl.ANY)] * count
        + [pl.BlockSpec(memory_space=pltpu.SMEM)]
        + [pl.BlockSpec(memory_space=pltpu.VMEM)] * 2
        + [pl.BlockSpec(memory_space=pltpu.HBM)] * 2,
        out_specs=[pl.BlockSpec(memory_space=pltpu.HBM)] * 2,
        out_shape=[jax.ShapeDtypeStruct(sent.shape, low_type)] * 2,
        input_output_aliases={count + 3: 0, count + 4: 1},
        scratch_shapes=[
            pltpu.VMEM((tiles * depth, LANES), jnp.float32),
            pltpu.VMEM((pair * nine, LANES), jnp.float32),
            pltpu.VMEM((rows_of[0], D), low_type),
            pltpu.VMEM((rows_of[-1], D), low_type),
            pltpu.VMEM(out_grad.shape, low_type),
            pltpu.SemaphoreType.DMA((len(spans),)),
            pltpu.SemaphoreType.DMA((len(spans),)),
        ],
        compiler_params=pltpu.CompilerParams(vmem_limit_bytes=16 * 2**20),
        cost_estimate=pl.CostEstimate(flops=0, bytes_accessed=8 * 2**20, transcendentals=0),
    )(*tokens, smem(core), packed_grad, out_grad, sent, kept)


def close_shared(tokens, place, owner, arrived, patch_rows):
    groups, lane_rows, lanes = arrived.shape
    pieces = patch_rows.shape[1] // LANES

    def kernel(place, owner, arrived, patch_rows, shared_out, latent_out, square_out, work):
        total = arrived[0].astype(jnp.float32)
        for member in range(1, groups):
            total = total + arrived[member].astype(jnp.float32)
        latent_out[...] = total[:D]
        for piece in range(pieces):
            work[pl.ds(piece, patch_rows.shape[0], stride=pieces), :] = patch_rows[
                :, piece * LANES : (piece + 1) * LANES
            ]
        patch = jnp.where(owner[0, 0] == 1, work[...], 0.0)
        total = jnp.where(place[0, 0] == 0, 0.0, total) + patch
        shared_out[...] = total
        squares = jnp.sum(total * total, axis=0, keepdims=True)
        square_out[...] = jnp.sum(squares, axis=1, keepdims=True)

    return run_kernel(
        kernel,
        tokens,
        [smem(place), smem(owner), arrived, patch_rows],
        [((lane_rows, lanes), jnp.float32), ((D, lanes), jnp.float32), ((1, 1), jnp.float32)],
        [pltpu.VMEM((lane_rows, lanes), jnp.float32)],
        scalars=2,
    )


def close_block(halves, latent):
    rows = [half.shape[0] for half in halves]
    pieces = D // LANES
    latent_rows = latent.shape[0] // pieces

    def kernel(one, two, latent, block_out, square_out):
        block_out[: rows[0], :] = one[...]
        block_out[rows[0] :, :] = two[...]
        last = slice(sum(rows) - latent_rows, sum(rows))
        for piece in range(pieces):
            block_out[last, piece * LANES : (piece + 1) * LANES] += latent[
                pl.ds(piece, latent_rows, stride=pieces), :
            ]
        total = block_out[...]
        squares = jnp.sum(total * total, axis=0, keepdims=True)
        square_out[...] = jnp.sum(squares, axis=1, keepdims=True)

    return run_kernel(
        kernel,
        [],
        [*halves, latent],
        [((sum(rows), D), jnp.float32), ((1, 1), jnp.float32)],
    )


def on_device(
    pixels,
    visible,
    block_master,
    block_first,
    block_second,
    shared_master,
    shared_first,
    shared_second,
    gains_master,
    gains_first,
    gains_second,
):
    groups = lax.axis_size("mp")
    replicas = lax.axis_size("dp")
    member = lax.axis_index("mp")
    model_cols = D // groups
    mlp_cols = MLP // groups
    embed_cols = DD // groups
    block_rows = block_master.shape[1] // D
    shared_rows = shared_master.shape[0] // 128

    own_pixels = pick(pixels, member, 0)
    own_visible = pick(visible, member, 0)
    hidden_mask = (1 - own_visible).astype(jnp.float32)
    hidden_count = jnp.sum(1 - own_visible).astype(jnp.float32)

    block_lanes = block_master.reshape(-1, 128)
    shared_lanes = shared_master.reshape(-1, 128)
    shared_low = shared_lanes.astype(low_type)
    block_rowed = low_rows(block_lanes, D)
    shared_flat = lax.all_gather(shared_low, ("dp", "mp"), axis=0).reshape(-1, 128)

    patch_size = PIX * D
    head_rows = shared_master.shape[0] // D
    tail_length = patch_size - groups * head_rows * D
    early = 0 < tail_length <= shared_master.shape[0] and groups * head_rows < PIX
    small_length = gains_master.shape[0]
    small_row = jnp.concatenate([lax.reduce_precision(gains_master, 8, 7), hidden_count[None]])
    small_row = jnp.pad(small_row, (0, -small_row.shape[0] % 128))
    near_visible = reorder(visible, member)
    near_pixels = reorder(pixels, member)
    select, slot_patch, key_valid = visible_slots(near_visible)
    chosen = (slot_patch[:, :, None] == jnp.arange(PATCHES)[None, None, :]).astype(low_type)
    seen_patches = jnp.einsum(
        "isp,ipd->isd", chosen, near_pixels, preferred_element_type=jnp.float32
    ).astype(low_type)
    small_table, block_flat = gather_early(small_row, block_rowed)
    gain_flat = small_table[:, :small_length].reshape(-1)
    count_total = jnp.sum(small_table[:, small_length])

    bounds = [0, 3 * model_cols, model_cols, mlp_cols, mlp_cols, embed_cols]
    bounds = [sum(bounds[: place + 1]) for place in range(len(bounds))]
    enc_packed, enc_out, enc_up, enc_down, enc_latent = [
        block_flat[low:high] for low, high in zip(bounds[:-1], bounds[1:])
    ]
    enc_packed = enc_packed.reshape(D, 3 * model_cols)
    enc_up = enc_up.reshape(D, mlp_cols)
    own_latent_w = enc_latent.reshape(D, embed_cols)

    (patch_w,) = unpack(shared_flat, 0, [(PIX, D)])
    dec_weights = unpack(
        shared_flat, PIX * D, [(DD, 3 * DD), (DD, DD), (DD, DMLP), (DMLP, DD), (DD, PIX)]
    )
    enc_one, enc_two, enc_last, dec_one, dec_two, dec_last, mask_token = cut_pieces(
        gain_flat, [(D,), (D,), (D,), (DD,), (DD,), (DD,), (DD,)]
    )

    latent_w = reorder(share_by_core(own_latent_w), member)
    saved, terms = enter_encoder(
        seen_patches.reshape(-1, PIX),
        patch_w,
        position_table(slot_patch, D).reshape(-1, D),
        enc_one[None],
        enc_packed,
        enc_out,
        key_valid.astype(jnp.float32).reshape(1, -1),
    )
    residual, first_hat, first_inverse, normed, packed, prob, mixed_heads = saved
    middle, inner_low, second_hat, second_inverse = norm_of_sum(
        exchange(terms), residual, enc_two[None]
    )
    inner_low = spread(inner_low)
    inner_low, terms = raise_and_lower(inner_low, enc_up, enc_down)
    final_low, final_hat, final_inverse, latent = latent_of_sum(
        [], exchange(terms), middle, enc_last[None], latent_w
    )

    pad = ((0, TOKENS - PATCHES), (0, 0))
    place = lax.axis_index("dp")
    along = early and shared_rows >= D and bounds[4] >= (replicas - 1) * block_rows
    along = along and block_rows % 16 == 0
    sent_grad, kept_grad, latent_grad, dec_small, loss_local = decode(
        shared_rows if along else 0,
        (place & 1).reshape(1, 1),
        (2.0 / (PIX * count_total)).reshape(1, 1),
        final_low,
        latent,
        jnp.pad(select[0].T.astype(low_type), pad),
        jnp.pad(hidden_mask[:, None], pad),
        jnp.pad(position_table(jnp.arange(PATCHES), DD), pad),
        jnp.pad(jnp.stack([dec_one, dec_two, dec_last, mask_token]), ((0, 4), (0, 0))),
        jnp.pad(own_pixels, pad),
        dec_weights,
        replicas,
        groups * shared_rows,
    )
    loss_local = loss_local[0, 0]
    got_grad = swap(sent_grad, "dp", 1)

    encoded_grad, enc_last_grad, encoded_low = latent_back(
        [], member, along, latent_grad, latent_w, final_hat, final_inverse, enc_last[None]
    )
    (up_grad, down_grad), terms, latent_wgrad = mlp_back(
        [],
        place & 1,
        exchange(encoded_low),
        [] if along else spread(final_low),
        inner_low,
        enc_up,
        enc_down,
        replicas if along else 0,
        block_rows,
        bounds[2],
    )
    terms = exchange(terms)
    column_totals, column_first = first_stage(kept_grad, after_all(got_grad, terms[1:]))
    middle_grad, middle_low, enc_two_grad = norm_back_of_sum(
        [], terms, encoded_grad, second_hat, second_inverse, enc_two[None]
    )
    (packed_grad, out_grad), terms = attend_back(
        column_first, spread(middle_low), normed, packed, prob, mixed_heads, enc_packed, enc_out
    )
    terms = exchange(terms)
    if along:
        sent_block, kept_block = pack_block(
            terms[1:], place & 1, packed_grad, out_grad, up_grad, down_grad
        )
        block_totals, block_sent = first_stage(kept_block, swap(sent_block, "dp", 1))
    else:
        block_grad = jnp.concatenate(
            [
                piece.reshape(-1, D)
                for piece in (packed_grad, out_grad, up_grad, down_grad, latent_wgrad[0])
            ]
        )
        block_share = reduce_dp(block_grad.reshape(replicas, block_rows, D))
        block_sent = []
    column_halves, column_last = later_stages(column_totals, terms[1:])
    column_share = jnp.concatenate(column_halves, 0)
    residual_low = last_norm_back(
        [],
        terms,
        middle_grad,
        first_hat,
        first_inverse,
        enc_one[None],
        enc_two_grad,
        enc_last_grad,
        dec_small,
    )

    residual_all = spread(residual_low)
    kept, sent = patch_back(
        block_sent,
        member,
        place & 1,
        seen_patches.reshape(-1, PIX),
        residual_all,
        head_rows,
    )
    column_share = column_share.reshape(groups, shared_rows, 128).astype(low_type)
    arrived = to_members(column_share)
    total = kept + swap(sent, "dp", 1)
    gain_rows = total[-8:]
    if early:
        total = total[:-8]
        total_low = total.astype(low_type)
        for dp in range(2, replicas, 2):
            pairs = [(dp * groups + mp, mp) for mp in range(groups)] + [((dp + 1) * groups, groups)]
            total = total + pair_permute(total_low, pairs).astype(jnp.float32)
        owner = (place == 0) | ((place == 1) & (member == 0))
        gain_rows = sum_chips(gain_rows)
        if along:
            block_halves, block_last = later_stages(block_totals)
            shared_share, latent_share, shared_square = close_shared(
                [], place, owner.astype(jnp.int32), arrived, total
            )
            latent_share = lax.ppermute(latent_share, "dp", [(0, replicas - 1)])
            block_share, block_square = close_block(block_halves, latent_share)
            squares = block_square[0, 0] + shared_square[0, 0]
        else:
            shared_share = jnp.sum(arrived.astype(jnp.float32), 0)
            shared_share = shared_share + jnp.where(owner, total.reshape(-1, 128), 0.0)
    else:
        patch_rows = outer_sum(seen_patches[0], residual_low[:VIS])
        patch_rows = patch_rows.astype(low_type).reshape(-1, 128)
        patch_rows = jnp.pad(patch_rows, ((0, shared_flat.shape[0] - patch_rows.shape[0]), (0, 0)))
        column = reduce_dp(patch_rows.reshape(replicas, groups * shared_rows, 128))
        column = column.reshape(groups, shared_rows, 128).astype(low_type)
        shared_share = jnp.sum(arrived.astype(jnp.float32), 0)
        shared_share = shared_share + jnp.sum(to_members(column).astype(jnp.float32), 0)
        gain_rows = sum_chips(gain_rows)
    pad_length = gain_flat.shape[0] - 3 * D - 4 * DD
    gain_grad = jnp.concatenate(
        [
            gain_rows[:3].reshape(-1),
            gain_rows[3:7, :DD].reshape(-1),
            jnp.zeros((pad_length,), jnp.float32),
        ]
    )
    own = lax.axis_index("dp") * groups + member
    gain_share = lax.dynamic_slice_in_dim(gain_grad, own * small_length, small_length)
    if not along:
        squares = jnp.sum(block_share * block_share) + jnp.sum(shared_share * shared_share)
    squares = squares + jnp.sum(gain_share * gain_share)
    sums = sum_small(jnp.stack([squares, loss_local]).reshape(1, 2))
    square_total, loss_total = sums[0, 0], sums[0, 1]
    grad_norm = jnp.sqrt(square_total)
    factor = jnp.minimum(1.0, clip_norm / (grad_norm + 1e-06))
    block_out, shared_out = update(
        factor,
        block_share,
        [block_first.reshape(-1, 128), block_second.reshape(-1, 128), block_lanes],
        shared_share,
        [shared_first.reshape(-1, 128), shared_second.reshape(-1, 128), shared_lanes],
    )
    block_out = tuple(piece.reshape(block_master.shape) for piece in block_out)
    shared_out = tuple(piece.reshape(-1) for piece in shared_out)
    gain_out = adamw(gain_share, gains_first, gains_second, gains_master, factor, rate_gains, 0.0)
    return (grad_norm, loss_total, count_total) + block_out + shared_out + gain_out


def solution(mesh):
    return jax.shard_map(
        on_device,
        mesh=mesh,
        in_specs=(
            P("dp", None, None),
            P("dp", None),
            P("mp", "dp"),
            P("mp", "dp"),
            P("mp", "dp"),
            P(("dp", "mp")),
            P(("dp", "mp")),
            P(("dp", "mp")),
            P(("dp", "mp")),
            P(("dp", "mp")),
            P(("dp", "mp")),
        ),
        out_specs=(
            P(),
            P(),
            P(),
            P("mp", "dp"),
            P("mp", "dp"),
            P("mp", "dp"),
            P("mp", "dp"),
            P(("dp", "mp")),
            P(("dp", "mp")),
            P(("dp", "mp")),
            P(("dp", "mp")),
            P(("dp", "mp")),
            P(("dp", "mp")),
            P(("dp", "mp")),
            P(("dp", "mp")),
        ),
        check_vma=False,
    )
```
